128 devices in a mesh: section: 2 (over core), fsdp: 4 (over x), ctx: 16 (over z, y).
Axes of the slice: x: 4, y: 4, z: 4, core: 2. Of those that a mesh axis runs over, the one named last changes fastest.
Arguments:
- inputs: bfloat16 [8, 1024, 1536], P('fsdp', 'ctx'), may hold values from -6 to 6
- positions: int32 [8, 1024], P('fsdp', 'ctx'), may hold values from 0 to 1023, as said below
- out_grad: bfloat16 [8, 1024, 1536], P('fsdp', 'ctx'), may hold values from -6 to 6
- norm_attn: bfloat16 [2, 1536], P('section', 'fsdp'), may hold values from 0.099609375 to 1.8984375
- w_query: bfloat16 [2, 1536, 1536], P('section', 'fsdp'), may hold values from -0.15625 to 0.15625
- key_weight: bfloat16 [2, 1536, 768], P('section', 'fsdp'), may hold values from -0.15625 to 0.15625
- value_weight: bfloat16 [2, 1536, 768], P('section', 'fsdp'), may hold values from -0.15625 to 0.15625
- output_weight: bfloat16 [2, 1536, 1536], P('section', 'fsdp'), may hold values from -1.25 to 1.25
- norm_mlp: bfloat16 [2, 1536], P('section', 'fsdp'), may hold values from 0.099609375 to 1.8984375
- w_gate: bfloat16 [2, 1536, 4096], P('section', 'fsdp'), may hold values from -0.15625 to 0.15625
- w_up: bfloat16 [2, 1536, 4096], P('section', 'fsdp'), may hold values from -0.15625 to 0.15625
- w_down: bfloat16 [2, 4096, 1536], P('section', 'fsdp'), may hold values from -0.09375 to 0.09375
Outputs:
- section_out: bfloat16 [2, 8, 1024, 1536], P('section', 'fsdp', 'ctx')
- section_grad: bfloat16 [2, 8, 1024, 1536], P('section', 'fsdp', 'ctx')
- grad_norm_attn: float32 [2, 1536], P('section', 'fsdp')
- grad_query: float32 [2, 1536, 1536], P('section', 'fsdp')
- grad_key: float32 [2, 1536, 768], P('section', 'fsdp')
- grad_value: float32 [2, 1536, 768], P('section', 'fsdp')
- grad_out: float32 [2, 1536, 1536], P('section', 'fsdp')
- grad_norm_mlp: float32 [2, 1536], P('section', 'fsdp')
- grad_gate: float32 [2, 1536, 4096], P('section', 'fsdp')
- grad_up: float32 [2, 1536, 4096], P('section', 'fsdp')
- grad_down: float32 [2, 4096, 1536], P('section', 'fsdp')
The draws below stay inside these ranges and needn't reach their ends.
Inputs may be any that keep to these rules, and one draw needn't show every extreme that they name: In every sequence each position appears once. The rows of a sequence fall into blocks of 32 rows of consecutive rising positions starting at a multiple of 32; the first half of each ctx device's rows holds block p and its second half block 2 N - 1 - p, with N the devices of ctx and p a different number for each device.
All inputs are finite; a program needn't handle non-finite values.
Results may differ from the reference program's by a relative error of at most 0.029.
Values may be sent and summed in bfloat16 or wider, within the bound.
A program may use at most 384 MiB of HBM per device.

```python
from functools import partial
import jax
import jax.numpy as jnp
from jax import lax

MODEL_WIDTH = 1536
QUERY_HEADS = 16
KEY_VALUE_HEADS = 8
HEAD_SIZE = 96
FF = 4096
BLOCK_ROWS = 32
SEQ_LEN = 1024
SEQS = 8
N_SECTION = 2
N_CTX = 16


def draw_positions(key, part):
    key = jax.random.fold_in(key, 7)
    seq_keys = jax.random.split(key, SEQS)
    orders = jax.vmap(lambda one_key: jax.random.permutation(one_key, N_CTX))(seq_keys).astype(jnp.int32)
    offsets = jnp.arange(BLOCK_ROWS, dtype=jnp.int32)
    lower = orders[:, :, None] * BLOCK_ROWS + offsets[None, None, :]
    upper = (2 * N_CTX - 1 - orders)[:, :, None] * BLOCK_ROWS + offsets[None, None, :]
    return jnp.concatenate([lower, upper], axis=2).reshape(SEQS, SEQ_LEN).astype(jnp.int32)


def block_levels(stream_key, shape, shards, least, top_value):
    def one(axis_at, shards_of):
        heights = jax.random.uniform(jax.random.fold_in(jax.random.fold_in(stream_key, 6), axis_at), (shards_of,), jnp.float32, least / len(shards), top_value / len(shards))
        return jnp.repeat(jnp.exp(heights), shape[axis_at] // shards_of).reshape((-1,) + (1,) * (len(shape) - axis_at - 1))

    factor_of = one(*shards[0])
    for cut in shards[1:]:
        factor_of = factor_of * one(*cut)
    return factor_of


def normal_values(rng, shape, width, reach, cuts=(), kind=jnp.bfloat16):
    entries = width * jax.random.normal(rng, shape, jnp.float32)
    if cuts:
        entries = entries * block_levels(rng, shape, cuts, -0.22, 0.18)
    return jnp.clip(entries, -reach, reach).astype(kind)


def setup_inputs(seed: int = 0) -> dict:
    arg_keys = jax.random.split(jax.random.key(seed), 13)
    inputs = normal_values(arg_keys[0], (SEQS, SEQ_LEN, MODEL_WIDTH), 1.0, 6.0, ((0, 4), (1, 16)))
    positions = draw_positions(jax.random.fold_in(arg_keys[12], 71), 0)
    out_grad = normal_values(arg_keys[2], (SEQS, SEQ_LEN, MODEL_WIDTH), 1.0, 6.0, ((0, 4), (1, 16)))
    norm_attn = jnp.clip(1.0 + 0.18 * jax.random.normal(arg_keys[3], (N_SECTION, MODEL_WIDTH), jnp.float32), 0.099609375, 1.8984375).astype(jnp.bfloat16)
    w_query = normal_values(arg_keys[4], (N_SECTION, MODEL_WIDTH, QUERY_HEADS * HEAD_SIZE), MODEL_WIDTH ** -0.5, 0.15625, ((0, 2), (1, 4)))
    key_weight = normal_values(arg_keys[5], (N_SECTION, MODEL_WIDTH, KEY_VALUE_HEADS * HEAD_SIZE), MODEL_WIDTH ** -0.5, 0.15625, ((0, 2), (1, 4)))
    value_weight = normal_values(arg_keys[6], (N_SECTION, MODEL_WIDTH, KEY_VALUE_HEADS * HEAD_SIZE), MODEL_WIDTH ** -0.5, 0.15625, ((0, 2), (1, 4)))
    output_weight = normal_values(arg_keys[7], (N_SECTION, QUERY_HEADS * HEAD_SIZE, MODEL_WIDTH), (QUERY_HEADS * HEAD_SIZE // 64) ** -0.5, 1.25, ((0, 2), (1, 4)))
    norm_mlp = jnp.clip(1.0 + 0.18 * jax.random.normal(arg_keys[8], (N_SECTION, MODEL_WIDTH), jnp.float32), 0.099609375, 1.8984375).astype(jnp.bfloat16)
    w_gate = normal_values(arg_keys[9], (N_SECTION, MODEL_WIDTH, FF), MODEL_WIDTH ** -0.5, 0.15625, ((0, 2), (1, 4)))
    w_up = normal_values(arg_keys[10], (N_SECTION, MODEL_WIDTH, FF), MODEL_WIDTH ** -0.5, 0.15625, ((0, 2), (1, 4)))
    w_down = normal_values(arg_keys[11], (N_SECTION, FF, MODEL_WIDTH), FF ** -0.5, 0.09375, ((0, 2), (1, 4)))
    return dict(inputs=inputs, positions=positions, out_grad=out_grad, norm_attn=norm_attn, w_query=w_query, key_weight=key_weight, value_weight=value_weight, output_weight=output_weight, norm_mlp=norm_mlp, w_gate=w_gate, w_up=w_up, w_down=w_down)


THETA = 100000.0
EPSILON = 1e-05
HIGHEST_PRECISION = lax.Precision.HIGHEST

@jax.custom_vjp
def lowered_copy(v):
    return lax.optimization_barrier(v.astype(jnp.bfloat16)).astype(jnp.float32)

@jax.custom_vjp
def low_back(v):
    return v

def low_keep(v):
    return (lowered_copy(v), None)

def low_pass(kept, grad):
    return (grad,)

def back_keep(v):
    return (v, None)

def back_low(kept, grad):
    return (lowered_copy(grad),)
lowered_copy.defvjp(low_keep, low_pass)
low_back.defvjp(back_keep, back_low)

def rms_scale(values, gain_vec):
    return values * lax.rsqrt(lax.optimization_barrier(jnp.mean(values * values, axis=-1, keepdims=True)) + EPSILON) * gain_vec

def rotary_turn(values, token_locations):
    half_width = values.shape[-1] // 2
    frequency = THETA ** (-(jnp.arange(half_width, dtype=jnp.float32) * 2.0 / values.shape[-1]))
    angles = token_locations.astype(jnp.float32)[:, None] * frequency[None, :]
    cosine = jnp.cos(angles)[:, None, :]
    sine_part = jnp.sin(angles)[:, None, :]
    first_half = values[..., :half_width]
    second_half = values[..., half_width:]
    return jnp.concatenate([first_half * cosine - second_half * sine_part, second_half * cosine + first_half * sine_part], axis=-1)

def matrix_product(left_side, right_side):
    return jnp.dot(left_side, right_side, precision=HIGHEST_PRECISION, preferred_element_type=jnp.float32)

def attend_group(operands, visible):
    query_group, key_head, value_head = operands
    scores = low_back(jnp.einsum('qgd,kd->gqk', query_group, key_head, precision=HIGHEST_PRECISION) * HEAD_SIZE ** (-0.5))
    scores = jnp.where(visible[None], scores, -1e+30)
    row_max = lax.optimization_barrier(jnp.max(scores, axis=-1, keepdims=True))
    exponent = jnp.exp(scores - row_max)
    probabilities = lowered_copy(exponent / lax.optimization_barrier(jnp.sum(exponent, axis=-1, keepdims=True)))
    return jnp.einsum('gqk,kd->qgd', probabilities, value_head, precision=HIGHEST_PRECISION)

def run_layer(stream, token_locations, params):
    gain_attn, w_query, key_weight, value_weight, output_weight, gain_mlp, w_gate, w_up, w_down = params
    count_of_rows = stream.shape[0]
    stream = low_back(stream)
    normalized = lowered_copy(rms_scale(stream, gain_attn))
    query_proj = low_back(matrix_product(normalized, w_query))
    key_projected = low_back(matrix_product(normalized, key_weight))
    value_projected = low_back(matrix_product(normalized, value_weight))
    query_rows = lowered_copy(rotary_turn(query_proj.reshape(count_of_rows, QUERY_HEADS, HEAD_SIZE), token_locations))
    rows_of_keys = lowered_copy(rotary_turn(key_projected.reshape(count_of_rows, KEY_VALUE_HEADS, HEAD_SIZE), token_locations))
    rows_of_values = lowered_copy(value_projected).reshape(count_of_rows, KEY_VALUE_HEADS, HEAD_SIZE)
    visible = token_locations[:, None] >= token_locations[None, :]
    grouped_heads = query_rows.reshape(count_of_rows, KEY_VALUE_HEADS, QUERY_HEADS // KEY_VALUE_HEADS, HEAD_SIZE).transpose(1, 0, 2, 3)
    head_fn = jax.checkpoint(partial(attend_group, visible=visible))
    attention = lax.map(head_fn, (grouped_heads, rows_of_keys.transpose(1, 0, 2), rows_of_values.transpose(1, 0, 2)))
    attention = attention.transpose(1, 0, 2, 3).reshape(count_of_rows, QUERY_HEADS * HEAD_SIZE)
    attended = lowered_copy(low_back(attention))
    stream_mid = stream + low_back(matrix_product(attended, output_weight))
    normed_mlp = lowered_copy(rms_scale(stream_mid, gain_mlp))
    gate_proj = low_back(matrix_product(normed_mlp, w_gate))
    up_proj = low_back(matrix_product(normed_mlp, w_up))
    hidden = lowered_copy(jax.nn.silu(gate_proj) * up_proj)
    return lowered_copy(stream_mid + low_back(matrix_product(hidden, w_down)))

def reference(inputs, positions, out_grad, norm_attn, w_query, key_weight, value_weight, output_weight, norm_mlp, w_gate, w_up, w_down):
    params = tuple((member.astype(jnp.float32) for member in (norm_attn, w_query, key_weight, value_weight, output_weight, norm_mlp, w_gate, w_up, w_down)))
    starts = inputs.astype(jnp.float32)
    tap_zero = jnp.zeros_like(starts)

    def forward(starts, tap_zero, params):

        def per_sequence(running, operands):
            start_rows, tap_rows, token_locations = operands
            first_out = run_layer(start_rows, token_locations, tuple((member[0] for member in params)))
            second_out = run_layer(first_out + tap_rows, token_locations, tuple((member[1] for member in params)))
            return (running, (first_out, second_out))
        _, results = lax.scan(per_sequence, jnp.zeros((), jnp.float32), (starts, tap_zero, positions))
        return results
    (first_outs, second_outs), pullback = jax.vjp(forward, starts, tap_zero, params)
    start_grad, tap_grad, param_grads = pullback((jnp.zeros_like(first_outs), out_grad.astype(jnp.float32)))
    section_out = jnp.stack([first_outs, second_outs]).astype(jnp.bfloat16)
    section_grad = jnp.stack([start_grad, tap_grad]).astype(jnp.bfloat16)
    return (section_out, section_grad, param_grads[0], param_grads[1], param_grads[2], param_grads[3], param_grads[4], param_grads[5], param_grads[6], param_grads[7], param_grads[8])
```

```python
import jax
import jax.numpy as jnp
from jax import lax
from jax.experimental import pallas as pl
from jax.experimental.pallas import tpu as pltpu
from jax.sharding import PartitionSpec as P

QUERY_HEADS = 16
KEY_VALUE_HEADS = 8
HEAD_SIZE = 96
WIDTH = 1536
FF = 4096
THETA = 100000.0
EPSILON = 1e-05
MESH = pl.DeviceIdType.MESH
N_X = 4
N_C = 16
BF = jnp.bfloat16
F32 = jnp.float32


def mm(a, b):
    return jnp.dot(a, b, preferred_element_type=F32)


def mm_tn(a, b):
    return lax.dot_general(a, b, (((0,), (0,)), ((), ())), preferred_element_type=F32)


def mm_nt(a, b):
    return lax.dot_general(a, b, (((1,), (1,)), ((), ())), preferred_element_type=F32)


def exchange(arrays, outs, axis, n, stage, cid):
    count = len(arrays)

    def kernel(*refs):
        srcs, dsts = refs[:count], refs[count : 2 * count]
        send, recv, local_sem = refs[2 * count :]
        me = lax.axis_index(axis)

        def run():
            barrier = pltpu.get_barrier_semaphore()
            for k in range(1, n):
                pl.semaphore_signal(
                    barrier,
                    inc=1,
                    device_id={axis: lax.rem(me + k, n)},
                    device_id_type=MESH,
                )
            pl.semaphore_wait(barrier, n - 1)
            copies = []
            for k in range(1, n):
                peer = lax.rem(me + k, n)
                for i in range(count):
                    copy = pltpu.make_async_remote_copy(
                        src_ref=outs[i][1](srcs[i], peer),
                        dst_ref=outs[i][2](dsts[i], me),
                        send_sem=send.at[i, k - 1],
                        recv_sem=recv.at[i, k - 1],
                        device_id={axis: peer},
                        device_id_type=MESH,
                    )
                    copy.start()
                    copies.append(copy)
            for i in range(count):
                copy = pltpu.make_async_copy(
                    outs[i][1](srcs[i], me), outs[i][2](dsts[i], me), local_sem.at[i]
                )
                copy.start()
                copies.append(copy)
            for copy in copies:
                copy.wait()

        if stage is None:
            run()
        else:
            pl.when(lax.axis_index("section") == stage)(run)

    return pl.pallas_call(
        kernel,
        out_shape=[jax.ShapeDtypeStruct(o[0], a.dtype) for a, o in zip(arrays, outs)],
        in_specs=[pl.BlockSpec(memory_space=pl.ANY)] * count,
        out_specs=[pl.BlockSpec(memory_space=pl.ANY)] * count,
        scratch_shapes=[
            pltpu.SemaphoreType.DMA((count, n - 1)),
            pltpu.SemaphoreType.DMA((count, n - 1)),
            pltpu.SemaphoreType.DMA((count,)),
        ],
        compiler_params=pltpu.CompilerParams(collective_id=cid, has_side_effects=True),
    )(*arrays)


def slot(ref, index):
    return ref.at[index]


def gather_x(v, stage, cid):
    r = exchange([v], [((N_X,) + v.shape, lambda ref, p: ref, slot)], "fsdp", N_X, stage, cid)[0]
    return r.reshape((N_X * v.shape[0],) + v.shape[1:])


def reduce_x(partial, stage, cid):
    v = partial.astype(BF).reshape(N_X, -1, partial.shape[-1])
    r = exchange([v], [(v.shape, slot, slot)], "fsdp", N_X, stage, cid)[0]
    return jnp.sum(r.astype(F32), axis=0)


def swap_c(v, stage, cid):
    return exchange([v], [(v.shape, slot, slot)], "ctx", N_C, stage, cid)[0]


def hop(v, source, cid):
    def kernel(src, dst, send, recv):
        me = lax.axis_index("section")
        barrier = pltpu.get_barrier_semaphore()
        pl.semaphore_signal(barrier, inc=1, device_id={"section": 1 - me}, device_id_type=MESH)
        pl.semaphore_wait(barrier, 1)
        copy = pltpu.make_async_remote_copy(
            src_ref=src,
            dst_ref=dst,
            send_sem=send,
            recv_sem=recv,
            device_id={"section": 1 - me},
            device_id_type=MESH,
        )

        @pl.when(me == source)
        def _():
            copy.start()
            copy.wait_send()

        @pl.when(me != source)
        def _():
            copy.wait_recv()

    return pl.pallas_call(
        kernel,
        out_shape=jax.ShapeDtypeStruct(v.shape, v.dtype),
        in_specs=[pl.BlockSpec(memory_space=pl.ANY)],
        out_specs=pl.BlockSpec(memory_space=pl.ANY),
        scratch_shapes=[pltpu.SemaphoreType.DMA, pltpu.SemaphoreType.DMA],
        compiler_params=pltpu.CompilerParams(collective_id=cid, has_side_effects=True),
    )(v)


def rms(v, gain):
    return v * lax.rsqrt(jnp.mean(v * v, axis=-1, keepdims=True) + EPSILON) * gain


def rotate(u, table, sign):
    cosine, sine = (t[:, None, None, :] for t in table)
    sine = sine * sign
    rows, groups, _ = u.shape
    heads = u.reshape(rows, groups, 4, 96)
    a, b = heads[:, :, :3, :48], heads[:, :, :3, 48:]
    turned = jnp.concatenate([a * cosine - b * sine, b * cosine + a * sine], axis=-1)
    return jnp.concatenate([turned, heads[:, :, 3:]], axis=2).reshape(rows, groups, 384)


def local(
    inputs,
    positions,
    out_grad,
    norm_attn,
    w_query,
    key_weight,
    value_weight,
    output_weight,
    norm_mlp,
    w_gate,
    w_up,
    w_down,
):
    section = lax.axis_index("section")
    x_idx = lax.axis_index("fsdp")
    c_idx = lax.axis_index("ctx")
    is_first = section == 0

    pos8 = lax.all_gather(positions, "fsdp", axis=0, tiled=True)
    pos_all = lax.all_gather(pos8, "ctx", axis=1, tiled=True)
    pos_seq = lax.dynamic_index_in_dim(pos_all, c_idx // 2, 0, keepdims=False)
    freq = THETA ** (-(jnp.arange(48, dtype=F32) * 2.0 / 96))

    def table_of(p):
        ang = p.reshape(-1).astype(F32)[:, None] * freq[None, :]
        return jnp.cos(ang), jnp.sin(ang)

    table_c = table_of(pos8)
    table_s = table_of(pos_seq)
    gains = lax.all_gather(jnp.concatenate([norm_attn, norm_mlp], 0), "fsdp", axis=1, tiled=True)
    gain_attn, gain_mlp = gains[0].astype(F32), gains[1].astype(F32)

    wqkv_shard = jnp.concatenate(
        [
            w_query[0].reshape(384, 8, 192),
            key_weight[0].reshape(384, 8, 96),
            value_weight[0].reshape(384, 8, 96),
        ],
        axis=2,
    ).reshape(384, 4, 768)
    wqkv_shard = wqkv_shard.transpose(1, 0, 2)

    def cols(ref, p):
        return ref.at[:, pl.ds(pl.multiple_of(p * 1024, 1024), 1024)]

    def rows(ref, p):
        return ref.at[pl.ds(pl.multiple_of(p * 384, 384), 384)]

    wqkv, wg, wu = exchange(
        [wqkv_shard, w_gate[0], w_up[0]],
        [((1536, 768), slot, rows), ((1536, 1024), cols, rows), ((1536, 1024), cols, rows)],
        "fsdp",
        N_X,
        None,
        0,
    )
    wo = output_weight[0]
    wd = w_down[0]

    visible = pos_seq[:, None] >= pos_seq[None, :]
    scale = HEAD_SIZE ** (-0.5)

    def forward(stage, xin, base):
        x32 = xin.astype(F32)
        nf = gather_x(rms(x32, gain_attn).astype(BF), stage, base)
        u = mm(nf, wqkv).reshape(512, 2, 384)
        r = rotate(u, table_c, 1.0).astype(BF)
        send = r.reshape(8, 64, 2, 384).transpose(0, 2, 1, 3).reshape(16, 64, 384)
        qkv = swap_c(send, stage, base + 1).reshape(1024, 384)
        q = qkv[:, :192].reshape(1024, 2, 96)
        k = qkv[:, 192:288]
        v = qkv[:, 288:]
        scores = jnp.einsum("qgd,kd->gqk", q, k, preferred_element_type=F32) * scale
        scores = jnp.where(visible[None], scores, -1e30)
        top = jnp.max(scores, axis=-1, keepdims=True)
        e = jnp.exp(scores - top)
        total = jnp.sum(e, axis=-1, keepdims=True)
        probs = (e / total).astype(BF)
        lse = top + jnp.log(total)
        att = jnp.einsum("gqk,kd->qgd", probs, v, preferred_element_type=F32).astype(BF)
        att = swap_c(att.reshape(16, 64, 192), stage, base + 2)
        att = att.reshape(8, 2, 64, 192).transpose(0, 2, 1, 3).reshape(512, 384)
        mid = x32 + reduce_x(mm(att, wo), stage, base + 3)
        n2 = gather_x(rms(mid, gain_mlp).astype(BF), stage, base + 4)
        gate = mm(n2, wg)
        up = mm(n2, wu)
        hidden = (jax.nn.silu(gate) * up).astype(BF)
        out = (mid + reduce_x(mm(hidden, wd), stage, base + 5)).astype(BF)
        return out, (x32, nf, q, k, v, lse, att, mid, n2, gate, up, hidden)

    def backward(stage, dy, kept, base):
        x32, nf, q, k, v, lse, att, mid, n2, gate, up, hidden = kept
        dyf = gather_x(dy, stage, base)
        dhidden = mm_nt(dyf, wd)
        sig = jax.nn.sigmoid(gate)
        dgate = (dhidden * up * (sig * (1.0 + gate * (1.0 - sig)))).astype(BF)
        dup = (dhidden * (gate * sig)).astype(BF)
        dn2 = reduce_x(mm_nt(dgate, wg) + mm_nt(dup, wu), stage, base + 1)
        _, back_mlp = jax.vjp(rms, mid, gain_mlp)
        dmid, g_mlp = back_mlp(dn2)
        dmid = dmid + dy.astype(F32)
        dbr = gather_x(dmid.astype(BF), stage, base + 2)
        datt = mm_nt(dbr, wo).astype(BF)
        send = datt.reshape(8, 64, 2, 192).transpose(0, 2, 1, 3).reshape(16, 64, 192)
        da = swap_c(send, stage, base + 3).reshape(1024, 2, 96)
        scores = jnp.einsum("qgd,kd->gqk", q, k, preferred_element_type=F32) * scale
        probs = jnp.exp(jnp.where(visible[None], scores, -1e30) - lse)
        dprobs = jnp.einsum("qgd,kd->gqk", da, v, preferred_element_type=F32)
        dv = jnp.einsum("gqk,qgd->kd", probs.astype(BF), da, preferred_element_type=F32)
        dot = jnp.sum(probs * dprobs, axis=-1, keepdims=True)
        ds = (probs * (dprobs - dot)).astype(BF)
        dq = jnp.einsum("gqk,kd->qgd", ds, k, preferred_element_type=F32) * scale
        dk = jnp.einsum("gqk,qgd->kd", ds, q, preferred_element_type=F32) * scale
        dqkv = jnp.concatenate([dq.reshape(1024, 192), dk, dv], axis=1)
        dqkv = rotate(dqkv[:, None], table_s, -1.0).astype(BF).reshape(16, 64, 384)
        dqkv = swap_c(dqkv, stage, base + 4)
        dqkv = dqkv.reshape(8, 2, 64, 384).transpose(0, 2, 1, 3).reshape(512, 768)
        dn = reduce_x(mm_nt(dqkv, wqkv), stage, base + 5)
        _, back_attn = jax.vjp(rms, x32, gain_attn)
        dx, g_attn = back_attn(dn)
        dx = (dx + dmid).astype(BF)
        return dx, (g_attn, g_mlp, nf, dqkv, att, dbr, n2, dgate, dup, hidden, dyf)

    def choose(a, b):
        return jax.tree.map(lambda p, q: jnp.where(is_first, p, q), a, b)

    x_own = inputs.reshape(128, WIDTH)
    out0, kept0 = forward(0, x_own, 1)
    out1, kept1 = forward(1, hop(out0, 0, 7), 8)
    dx1, parts1 = backward(1, out_grad.reshape(128, WIDTH), kept1, 14)
    dx0, parts0 = backward(0, hop(dx1, 1, 20), kept0, 21)
    section_out = choose(out0, out1).reshape(1, 2, 64, WIDTH)
    section_grad = choose(dx0, dx1).reshape(1, 2, 64, WIDTH)
    g_attn, g_mlp, nf, dqkv, att, dbr, n2, dgate, dup, hidden, dyf = choose(parts0, parts1)

    wide = jnp.concatenate([mm_tn(n2, dgate), mm_tn(n2, dup), mm_tn(nf, dqkv)], axis=1).astype(BF)
    down = mm_tn(hidden, dyf).astype(BF)
    gout = mm_tn(att, dbr).astype(BF)
    wide = lax.psum_scatter(wide, "ctx", scatter_dimension=0, tiled=True)
    down = lax.psum_scatter(down, "ctx", scatter_dimension=0, tiled=True)
    gout = lax.psum_scatter(gout, "ctx", scatter_dimension=0, tiled=True)
    perm = [
        (x * 16 + c, (c // 4) * 16 + 4 * x + c % 4) for x in range(N_X) for c in range(N_C)
    ]
    wide = lax.ppermute(wide, ("fsdp", "ctx"), perm)
    wide = lax.all_gather(wide, "ctx", axis=0, tiled=True)
    down = lax.all_gather(down, "ctx", axis=0, tiled=True)
    gout = lax.all_gather(gout, "ctx", axis=0, tiled=True)
    wide = wide.reshape(4, 384, 2816).transpose(1, 0, 2).astype(F32)
    g_gate = wide[:, :, :1024].reshape(1, 384, FF)
    g_up = wide[:, :, 1024:2048].reshape(1, 384, FF)
    heads = wide[:, :, 2048:].reshape(384, 8, 384)
    g_query = heads[:, :, :192].reshape(1, 384, 1536)
    g_key = heads[:, :, 192:288].reshape(1, 384, 768)
    g_value = heads[:, :, 288:].reshape(1, 384, 768)
    g_gain = lax.psum(jnp.stack([g_attn, g_mlp]), ("fsdp", "ctx"))
    g_gain = lax.dynamic_slice_in_dim(g_gain, x_idx * 384, 384, 1)
    return (
        section_out,
        section_grad,
        g_gain[0:1],
        g_query,
        g_key,
        g_value,
        gout.astype(F32)[None],
        g_gain[1:2],
        g_gate,
        g_up,
        down.astype(F32)[None],
    )


def solution(mesh):
    rows = P("section", "fsdp", None)
    return jax.shard_map(
        local,
        mesh=mesh,
        in_specs=(
            P("fsdp", "ctx", None),
            P("fsdp", "ctx"),
            P("fsdp", "ctx", None),
            P("section", "fsdp"),
            rows,
            rows,
            rows,
            rows,
            P("section", "fsdp"),
            rows,
            rows,
            rows,
        ),
        out_specs=(
            P("section", "fsdp", "ctx", None),
            P("section", "fsdp", "ctx", None),
            P("section", "fsdp"),
            rows,
            rows,
            rows,
            rows,
            P("section", "fsdp"),
            rows,
            rows,
            rows,
        ),
        check_vma=False,
    )
```

```python
import jax
import jax.numpy as jnp
from jax import lax
from jax.experimental import pallas as pl
from jax.experimental.pallas import tpu as pltpu
from jax.sharding import PartitionSpec as P

QUERY_HEADS = 16
KEY_VALUE_HEADS = 8
HEAD_SIZE = 96
WIDTH = 1536
FF = 4096
THETA = 100000.0
EPSILON = 1e-05
MESH = pl.DeviceIdType.MESH
N_X = 4
N_C = 16
BF = jnp.bfloat16
F32 = jnp.float32


def mm(a, b):
    return jnp.dot(a, b, preferred_element_type=F32)


def mm_tn(a, b):
    return lax.dot_general(a, b, (((0,), (0,)), ((), ())), preferred_element_type=F32)


def mm_nt(a, b):
    return lax.dot_general(a, b, (((1,), (1,)), ((), ())), preferred_element_type=F32)


def exchange(arrays, outs, axis, n, stage, cid):
    count = len(arrays)

    def kernel(*refs):
        srcs, dsts = refs[:count], refs[count : 2 * count]
        send, recv, local_sem = refs[2 * count :]
        me = lax.axis_index(axis)

        def run():
            barrier = pltpu.get_barrier_semaphore()
            for k in range(1, n):
                pl.semaphore_signal(
                    barrier,
                    inc=1,
                    device_id={axis: lax.rem(me + k, n)},
                    device_id_type=MESH,
                )
            pl.semaphore_wait(barrier, n - 1)
            copies = []
            for k in range(1, n):
                peer = lax.rem(me + k, n)
                for i in range(count):
                    copy = pltpu.make_async_remote_copy(
                        src_ref=outs[i][1](srcs[i], peer),
                        dst_ref=outs[i][2](dsts[i], me),
                        send_sem=send.at[i, k - 1],
                        recv_sem=recv.at[i, k - 1],
                        device_id={axis: peer},
                        device_id_type=MESH,
                    )
                    copy.start()
                    copies.append(copy)
            for i in range(count):
                copy = pltpu.make_async_copy(
                    outs[i][1](srcs[i], me), outs[i][2](dsts[i], me), local_sem.at[i]
                )
                copy.start()
                copies.append(copy)
            for copy in copies:
                copy.wait()

        if stage is None:
            run()
        else:
            pl.when(lax.axis_index("section") == stage)(run)

    return pl.pallas_call(
        kernel,
        out_shape=[jax.ShapeDtypeStruct(o[0], a.dtype) for a, o in zip(arrays, outs)],
        in_specs=[pl.BlockSpec(memory_space=pl.ANY)] * count,
        out_specs=[pl.BlockSpec(memory_space=pl.ANY)] * count,
        scratch_shapes=[
            pltpu.SemaphoreType.DMA((count, n - 1)),
            pltpu.SemaphoreType.DMA((count, n - 1)),
            pltpu.SemaphoreType.DMA((count,)),
        ],
        compiler_params=pltpu.CompilerParams(collective_id=cid, has_side_effects=True),
    )(*arrays)


def slot(ref, index):
    return ref.at[index]


def gather_x(v, stage, cid):
    r = exchange([v], [((N_X,) + v.shape, lambda ref, p: ref, slot)], "fsdp", N_X, stage, cid)[0]
    return r.reshape((N_X * v.shape[0],) + v.shape[1:])


def reduce_x(partial, stage, cid):
    v = partial.astype(BF).reshape(N_X, -1, partial.shape[-1])
    r = exchange([v], [(v.shape, slot, slot)], "fsdp", N_X, stage, cid)[0]
    return jnp.sum(r.astype(F32), axis=0)


def swap_c(v, stage, cid):
    return exchange([v], [(v.shape, slot, slot)], "ctx", N_C, stage, cid)[0]


def hop(v, source, cid):
    def kernel(src, dst, send, recv):
        me = lax.axis_index("section")
        barrier = pltpu.get_barrier_semaphore()
        pl.semaphore_signal(barrier, inc=1, device_id={"section": 1 - me}, device_id_type=MESH)
        pl.semaphore_wait(barrier, 1)
        copy = pltpu.make_async_remote_copy(
            src_ref=src,
            dst_ref=dst,
            send_sem=send,
            recv_sem=recv,
            device_id={"section": 1 - me},
            device_id_type=MESH,
        )

        @pl.when(me == source)
        def _():
            copy.start()
            copy.wait_send()

        @pl.when(me != source)
        def _():
            copy.wait_recv()

    return pl.pallas_call(
        kernel,
        out_shape=jax.ShapeDtypeStruct(v.shape, v.dtype),
        in_specs=[pl.BlockSpec(memory_space=pl.ANY)],
        out_specs=pl.BlockSpec(memory_space=pl.ANY),
        scratch_shapes=[pltpu.SemaphoreType.DMA, pltpu.SemaphoreType.DMA],
        compiler_params=pltpu.CompilerParams(collective_id=cid, has_side_effects=True),
    )(v)


def rms(v, gain):
    return v * lax.rsqrt(jnp.mean(v * v, axis=-1, keepdims=True) + EPSILON) * gain


def rotate(u, table, sign):
    cosine, sine = (t[:, None, None, :] for t in table)
    sine = sine * sign
    rows, groups, _ = u.shape
    heads = u.reshape(rows, groups, 4, 96)
    a, b = heads[:, :, :3, :48], heads[:, :, :3, 48:]
    turned = jnp.concatenate([a * cosine - b * sine, b * cosine + a * sine], axis=-1)
    return jnp.concatenate([turned, heads[:, :, 3:]], axis=2).reshape(rows, groups, 384)


def remote(src, dst, send, recv, device):
    return pltpu.make_async_remote_copy(
        src_ref=src, dst_ref=dst, send_sem=send, recv_sem=recv, device_id=device, device_id_type=MESH
    )


def part(start, size):
    return pl.ds(pl.multiple_of(start, size), size)


GRADS = {"gate": (96, 1024), "up": (96, 1024), "down": (64, 1536), "qkv": (96, 768), "out": (96, 384)}
RINGS = {"gate": ("y", 1), "up": ("y", -1), "down": ("z", 1), "qkv": ("z", -1), "out": ("z", -1)}


def grad_kernel(n2, nf, dgu, dqkv, att, dbr, hidden, dyf, gains, *refs):
    names = list(GRADS)
    held = dict(zip(names, refs[:5]))
    o_gain = refs[5]
    own = dict(zip(names, refs[6:11]))
    first = dict(zip(names, refs[11:16]))
    second = dict(zip(names, refs[16:21]))
    gain_in, send, recv, local_sem, send_g, recv_g = refs[21:]
    x = lax.axis_index("fsdp")
    c = lax.axis_index("ctx")
    y, z = lax.rem(c, 4), c // 4
    where = {"x": x, "y": y, "z": z}

    def near(axis, step):
        if axis == "x":
            return {"fsdp": lax.rem(x + step + 4, 4)}
        if axis == "y":
            return {"ctx": 4 * z + lax.rem(y + step + 4, 4)}
        return {"ctx": 4 * lax.rem(z + step + 4, 4) + y}

    mirror = {"y": {"fsdp": y, "ctx": 4 * z + x}, "z": {"fsdp": z, "ctx": 4 * x + y}}

    barrier = pltpu.get_barrier_semaphore()
    for axis in "xyz":
        for step in (1, 2, 3):
            pl.semaphore_signal(barrier, inc=1, device_id=near(axis, step), device_id_type=MESH)
    for axis in "yz":
        pl.semaphore_signal(barrier, inc=1, device_id=mirror[axis], device_id_type=MESH)
    pl.semaphore_wait(barrier, 11)

    def ring(name):
        axis, d = RINGS[name]
        other = "z" if axis == "y" else "y"
        return names.index(name), axis, other, d, where[axis], where[other]

    def at(i, d, s):
        return lax.rem(i - d * s + 8, 4)

    def copy_first(name, s, q):
        f, axis, other, d, i, j = ring(name)
        p = at(j, d, 1 + q)
        return remote(
            own[name].at[at(i, d, 1 + s), p],
            first[name].at[s, p],
            send.at[f, 4 * s + q],
            recv.at[f, 4 * s + q],
            near(axis, d),
        )

    def copy_second(name, s):
        f, axis, other, d, i, j = ring(name)
        return remote(
            own[name].at[i, at(j, d, 1 + s)],
            second[name].at[s],
            send.at[f, 12 + s],
            recv.at[f, 12 + s],
            near(other, d),
        )

    def copy_mirror(name):
        f, axis, other, d, i, j = ring(name)
        return remote(
            own[name].at[i, j], held[name].at[x, j], send.at[f, 15], recv.at[f, 15], mirror[axis]
        )

    def copy_own(name):
        f, axis, other, d, i, j = ring(name)
        group = x if name in ("gate", "up", "qkv") else i
        return pltpu.make_async_copy(own[name].at[i, j], held[name].at[group, j], local_sem.at[f])

    def copy_small(name, s):
        f, axis, other, d, i, j = ring(name)
        place = held[name].at[i, at(j, d, s)]
        return remote(place, place, send.at[f, 16 + s], recv.at[f, 16 + s], near(other, d))

    def copy_big(name, s, q):
        f, axis, other, d, i, j = ring(name)
        place = held[name].at[at(i, d, s), at(j, d, q)]
        n = 20 + 4 * s + q
        return remote(place, place, send.at[f, n], recv.at[f, n], near(axis, d))

    def gain_copy(n, k):
        axis = "xyz"[n]
        if n == 0:
            src = gains.at[:, part(lax.rem(x + k, 4) * 384, 384)]
        else:
            src = gain_in.at[n, 0]
        return remote(src, gain_in.at[n, k], send_g.at[n, k], recv_g.at[n, k], near(axis, k))

    def gain_start(n):
        for k in (1, 2, 3):
            gain_copy(n, k).start()

    def gain_sum(n):
        mine = gains[:, part(x * 384, 384)] if n == 0 else gain_in[n, 0]
        for k in (1, 2, 3):
            gain_copy(n, k).wait()
        return mine + gain_in[n, 1] + gain_in[n, 2] + gain_in[n, 3]

    gain_start(0)

    total = mm_tn(att[...], dbr[...]).astype(BF)
    for g in range(4):
        for p in range(4):
            own["out"][g, p] = total[96 * g : 96 * g + 96, 384 * p : 384 * p + 384]

    def compute(s, carry):
        def group(name):
            f, axis, other, d, i, j = ring(name)
            return at(i, d, 1 + s)

        g = group("gate")
        own["gate"][g] = mm_tn(n2[:, part(g * 384, 384)], dgu[:, :1024]).astype(BF).reshape(4, 96, 1024)
        g = group("up")
        own["up"][g] = mm_tn(n2[:, part(g * 384, 384)], dgu[:, 1024:]).astype(BF).reshape(4, 96, 1024)
        g = group("down")
        own["down"][g] = mm_tn(hidden[:, part(g * 256, 256)], dyf[...]).astype(BF).reshape(4, 64, 1536)
        g = group("qkv")
        own["qkv"][g] = mm_tn(nf[:, part(g * 384, 384)], dqkv[...]).astype(BF).reshape(4, 96, 768)

        @pl.when(s == 0)
        def _():
            for q in range(4):
                for name in names:
                    copy_first(name, 0, q).start()

        return carry

    lax.fori_loop(0, 4, compute, 0)
    gain_in[1, 0] = gain_sum(0)
    gain_start(1)

    def add_first(t, carry):
        s, q = t // 4, lax.rem(t, 4)
        for name in names:
            f, axis, other, d, i, j = ring(name)
            copy_first(name, s, q).wait_recv()
            g, p = at(i, d, 2 + s), at(j, d, 1 + q)
            own[name][g, p] = own[name][g, p] + first[name][s, p]

            @pl.when(s < 2)
            def _(name=name):
                copy_first(name, s + 1, q).start()

            @pl.when(t == 8)
            def _(name=name):
                copy_second(name, 0).start()

        return carry

    lax.fori_loop(0, 12, add_first, 0)
    gain_in[2, 0] = gain_sum(1)
    gain_start(2)

    def add_second(s, carry):
        for name in names:
            f, axis, other, d, i, j = ring(name)
            copy_second(name, s).wait_recv()
            p = at(j, d, 2 + s)
            own[name][i, p] = own[name][i, p] + second[name][s]

            @pl.when(s < 2)
            def _(name=name):
                copy_second(name, s + 1).start()

        return carry

    lax.fori_loop(0, 3, add_second, 0)

    for name in ("gate", "up", "qkv"):
        axis = RINGS[name][0]

        @pl.when(where[axis] != x)
        def _(name=name):
            copy_mirror(name).start()

        @pl.when(where[axis] == x)
        def _(name=name):
            copy_own(name).start()

    for name in ("down", "out"):
        copy_own(name).start()
    for name in ("down", "out"):
        copy_own(name).wait()
    for name in ("gate", "up", "qkv"):
        axis = RINGS[name][0]

        @pl.when(where[axis] != x)
        def _(name=name):
            copy_mirror(name).wait()

        @pl.when(where[axis] == x)
        def _(name=name):
            copy_own(name).wait()

    def hand_small(q, carry):
        for name in names:

            @pl.when(q > 0)
            def _(name=name):
                copy_small(name, q - 1).wait_recv()

            @pl.when(q < 3)
            def _(name=name):
                copy_small(name, q).start()

            copy_big(name, 0, q).start()
        return carry

    lax.fori_loop(0, 4, hand_small, 0)

    def hand_big(t, carry):
        s, q = t // 4, lax.rem(t, 4)
        for name in names:
            copy_big(name, s, q).wait_recv()

            @pl.when(s < 2)
            def _(name=name):
                copy_big(name, s + 1, q).start()

        return carry

    lax.fori_loop(0, 12, hand_big, 0)
    o_gain[...] = gain_sum(2)

    def sent(t, carry):
        s, q = t // 4, lax.rem(t, 4)
        for name in names:
            copy_first(name, s, q).wait_send()
            copy_big(name, s, q).wait_send()
        return carry

    lax.fori_loop(0, 12, sent, 0)

    def sent_small(s, carry):
        for name in names:
            copy_second(name, s).wait_send()
            copy_small(name, s).wait_send()
        return carry

    lax.fori_loop(0, 3, sent_small, 0)


def reduce_grads(n2, nf, dgu, dqkv, att, dbr, hidden, dyf, gains, cid):
    vm = pl.BlockSpec(memory_space=pltpu.VMEM)
    hbm = pl.BlockSpec(memory_space=pl.ANY)
    dma = pltpu.SemaphoreType.DMA
    sizes = list(GRADS.values())
    return pl.pallas_call(
        grad_kernel,
        out_shape=[jax.ShapeDtypeStruct((4, 4) + s, BF) for s in sizes]
        + [jax.ShapeDtypeStruct((8, 384), F32)],
        in_specs=[vm] * 9,
        out_specs=[hbm] * 5 + [vm],
        scratch_shapes=[pltpu.VMEM((4, 4) + s, BF) for s in sizes]
        + [pltpu.VMEM((3, 4) + s, BF) for s in sizes]
        + [pltpu.VMEM((3,) + s, BF) for s in sizes]
        + [
            pltpu.VMEM((3, 4, 8, 384), F32),
            dma((5, 32)),
            dma((5, 32)),
            dma((5,)),
            dma((3, 4)),
            dma((3, 4)),
        ],
        name="reduce_grads",
        compiler_params=pltpu.CompilerParams(
            collective_id=cid, has_side_effects=True, vmem_limit_bytes=60 << 20
        ),
    )(n2, nf, dgu, dqkv, att, dbr, hidden, dyf, gains)


def widen_kernel(w_gate, w_up, w_down, w_qkv, w_out, gate, up, query, key, value, g_out, g_down):
    g_down[...] = w_down[...].astype(F32)
    keys, values = [], []
    for x in range(N_X):
        gate[:, 1024 * x : 1024 * x + 1024] = w_gate[x, 0].astype(F32)
        up[:, 1024 * x : 1024 * x + 1024] = w_up[x, 0].astype(F32)
        g_out[:, 384 * x : 384 * x + 384] = w_out[0, x].astype(F32)
        heads = w_qkv[x, 0].astype(F32)
        query[:, 384 * x : 384 * x + 384] = jnp.concatenate(
            [heads[:, :192], heads[:, 384:576]], axis=1
        )
        keys += [heads[:, 192:288], heads[:, 576:672]]
        values += [heads[:, 288:384], heads[:, 672:768]]
    key[...] = jnp.concatenate(keys, axis=1)
    value[...] = jnp.concatenate(values, axis=1)


def widen(gate, up, down, qkv, out):
    steps = 8

    def spec(r, cols):
        return pl.BlockSpec((r, cols), lambda i: (i, 0))

    def shape(r, cols):
        return jax.ShapeDtypeStruct((r, cols), F32)

    def blocks(cols):
        return pl.BlockSpec((4, 1, 48, cols), lambda i: (0, i // 2, i % 2, 0))

    return pl.pallas_call(
        widen_kernel,
        grid=(steps,),
        out_shape=[
            shape(384, FF),
            shape(384, FF),
            shape(384, 1536),
            shape(384, 768),
            shape(384, 768),
            shape(384, 1536),
            shape(1024, 1536),
        ],
        in_specs=[
            blocks(1024),
            blocks(1024),
            spec(128, 1536),
            blocks(768),
            pl.BlockSpec((1, 4, 48, 384), lambda i: (i // 2, 0, i % 2, 0)),
        ],
        out_specs=[
            spec(48, FF),
            spec(48, FF),
            spec(48, 1536),
            spec(48, 768),
            spec(48, 768),
            spec(48, 1536),
            spec(128, 1536),
        ],
        name="widen",
        compiler_params=pltpu.CompilerParams(vmem_limit_bytes=60 << 20),
    )(gate, up, down.reshape(1024, 1536), qkv, out)


def local(
    inputs,
    positions,
    out_grad,
    norm_attn,
    w_query,
    key_weight,
    value_weight,
    output_weight,
    norm_mlp,
    w_gate,
    w_up,
    w_down,
):
    section = lax.axis_index("section")
    x_idx = lax.axis_index("fsdp")
    c_idx = lax.axis_index("ctx")
    is_first = section == 0

    pos8 = lax.all_gather(positions, "fsdp", axis=0, tiled=True)
    pos_all = lax.all_gather(pos8, "ctx", axis=1, tiled=True)
    pos_seq = lax.dynamic_index_in_dim(pos_all, c_idx // 2, 0, keepdims=False)
    freq = THETA ** (-(jnp.arange(48, dtype=F32) * 2.0 / 96))

    def table_of(p):
        ang = p.reshape(-1).astype(F32)[:, None] * freq[None, :]
        return jnp.cos(ang), jnp.sin(ang)

    table_c = table_of(pos8)
    table_s = table_of(pos_seq)
    gains = lax.all_gather(jnp.concatenate([norm_attn, norm_mlp], 0), "fsdp", axis=1, tiled=True)
    gain_attn, gain_mlp = gains[0].astype(F32), gains[1].astype(F32)

    wqkv_shard = jnp.concatenate(
        [
            w_query[0].reshape(384, 8, 192),
            key_weight[0].reshape(384, 8, 96),
            value_weight[0].reshape(384, 8, 96),
        ],
        axis=2,
    ).reshape(384, 4, 768)
    wqkv_shard = wqkv_shard.transpose(1, 0, 2)

    def cols(ref, p):
        return ref.at[:, pl.ds(pl.multiple_of(p * 1024, 1024), 1024)]

    def rows(ref, p):
        return ref.at[pl.ds(pl.multiple_of(p * 384, 384), 384)]

    wqkv, wg, wu = exchange(
        [wqkv_shard, w_gate[0], w_up[0]],
        [((1536, 768), slot, rows), ((1536, 1024), cols, rows), ((1536, 1024), cols, rows)],
        "fsdp",
        N_X,
        None,
        0,
    )
    wo = output_weight[0]
    wd = w_down[0]

    visible = pos_seq[:, None] >= pos_seq[None, :]
    scale = HEAD_SIZE ** (-0.5)

    def forward(stage, xin, base):
        x32 = xin.astype(F32)
        nf = gather_x(rms(x32, gain_attn).astype(BF), stage, base)
        u = mm(nf, wqkv).reshape(512, 2, 384)
        r = rotate(u, table_c, 1.0).astype(BF)
        send = r.reshape(8, 64, 2, 384).transpose(0, 2, 1, 3).reshape(16, 64, 384)
        qkv = swap_c(send, stage, base + 1).reshape(1024, 384)
        q = qkv[:, :192].reshape(1024, 2, 96)
        k = qkv[:, 192:288]
        v = qkv[:, 288:]
        scores = jnp.einsum("qgd,kd->gqk", q, k, preferred_element_type=F32) * scale
        scores = jnp.where(visible[None], scores, -1e30)
        top = jnp.max(scores, axis=-1, keepdims=True)
        e = jnp.exp(scores - top)
        total = jnp.sum(e, axis=-1, keepdims=True)
        probs = (e / total).astype(BF)
        lse = top + jnp.log(total)
        att = jnp.einsum("gqk,kd->qgd", probs, v, preferred_element_type=F32).astype(BF)
        att = swap_c(att.reshape(16, 64, 192), stage, base + 2)
        att = att.reshape(8, 2, 64, 192).transpose(0, 2, 1, 3).reshape(512, 384)
        mid = x32 + reduce_x(mm(att, wo), stage, base + 3)
        n2 = gather_x(rms(mid, gain_mlp).astype(BF), stage, base + 4)
        gate = mm(n2, wg)
        up = mm(n2, wu)
        hidden = (jax.nn.silu(gate) * up).astype(BF)
        out = (mid + reduce_x(mm(hidden, wd), stage, base + 5)).astype(BF)
        return out, (x32, nf, q, k, v, lse, att, mid, n2, gate, up, hidden)

    def backward(stage, dy, kept, base):
        x32, nf, q, k, v, lse, att, mid, n2, gate, up, hidden = kept
        dyf = gather_x(dy, stage, base)
        dhidden = mm_nt(dyf, wd)
        sig = jax.nn.sigmoid(gate)
        dgate = (dhidden * up * (sig * (1.0 + gate * (1.0 - sig)))).astype(BF)
        dup = (dhidden * (gate * sig)).astype(BF)
        dn2 = reduce_x(mm_nt(dgate, wg) + mm_nt(dup, wu), stage, base + 1)
        _, back_mlp = jax.vjp(rms, mid, gain_mlp)
        dmid, g_mlp = back_mlp(dn2)
        dmid = dmid + dy.astype(F32)
        dbr = gather_x(dmid.astype(BF), stage, base + 2)
        datt = mm_nt(dbr, wo).astype(BF)
        send = datt.reshape(8, 64, 2, 192).transpose(0, 2, 1, 3).reshape(16, 64, 192)
        da = swap_c(send, stage, base + 3).reshape(1024, 2, 96)
        scores = jnp.einsum("qgd,kd->gqk", q, k, preferred_element_type=F32) * scale
        probs = jnp.exp(jnp.where(visible[None], scores, -1e30) - lse)
        dprobs = jnp.einsum("qgd,kd->gqk", da, v, preferred_element_type=F32)
        dv = jnp.einsum("gqk,qgd->kd", probs.astype(BF), da, preferred_element_type=F32)
        dot = jnp.sum(probs * dprobs, axis=-1, keepdims=True)
        ds = (probs * (dprobs - dot)).astype(BF)
        dq = jnp.einsum("gqk,kd->qgd", ds, k, preferred_element_type=F32) * scale
        dk = jnp.einsum("gqk,qgd->kd", ds, q, preferred_element_type=F32) * scale
        dqkv = jnp.concatenate([dq.reshape(1024, 192), dk, dv], axis=1)
        dqkv = rotate(dqkv[:, None], table_s, -1.0).astype(BF).reshape(16, 64, 384)
        dqkv = swap_c(dqkv, stage, base + 4)
        dqkv = dqkv.reshape(8, 2, 64, 384).transpose(0, 2, 1, 3).reshape(512, 768)
        dn = reduce_x(mm_nt(dqkv, wqkv), stage, base + 5)
        _, back_attn = jax.vjp(rms, x32, gain_attn)
        dx, g_attn = back_attn(dn)
        dx = (dx + dmid).astype(BF)
        return dx, (g_attn, g_mlp, nf, dqkv, att, dbr, n2, dgate, dup, hidden, dyf)

    def choose(a, b):
        return jax.tree.map(lambda p, q: jnp.where(is_first, p, q), a, b)

    x_own = inputs.reshape(128, WIDTH)
    out0, kept0 = forward(0, x_own, 1)
    out1, kept1 = forward(1, hop(out0, 0, 7), 8)
    dx1, parts1 = backward(1, out_grad.reshape(128, WIDTH), kept1, 14)
    dx0, parts0 = backward(0, hop(dx1, 1, 20), kept0, 21)
    section_out = choose(out0, out1).reshape(1, 2, 64, WIDTH)
    section_grad = choose(dx0, dx1).reshape(1, 2, 64, WIDTH)
    g_attn, g_mlp, nf, dqkv, att, dbr, n2, dgate, dup, hidden, dyf = choose(parts0, parts1)

    gains = jnp.concatenate([g_attn[None], g_mlp[None], jnp.zeros((6, WIDTH), F32)], axis=0)
    *summed, g_gain = reduce_grads(
        n2, nf, jnp.concatenate([dgate, dup], axis=1), dqkv, att, dbr, hidden, dyf, gains, 27
    )
    g_gate, g_up, g_query, g_key, g_value, g_out, g_down = widen(*summed)
    return (
        section_out,
        section_grad,
        g_gain[0:1],
        g_query[None],
        g_key[None],
        g_value[None],
        g_out[None],
        g_gain[1:2],
        g_gate[None],
        g_up[None],
        g_down[None],
    )


def solution(mesh):
    rows = P("section", "fsdp", None)
    return jax.shard_map(
        local,
        mesh=mesh,
        in_specs=(
            P("fsdp", "ctx", None),
            P("fsdp", "ctx"),
            P("fsdp", "ctx", None),
            P("section", "fsdp"),
            rows,
            rows,
            rows,
            rows,
            P("section", "fsdp"),
            rows,
            rows,
            rows,
        ),
        out_specs=(
            P("section", "fsdp", "ctx", None),
            P("section", "fsdp", "ctx", None),
            P("section", "fsdp"),
            rows,
            rows,
            rows,
            rows,
            P("section", "fsdp"),
            rows,
            rows,
            rows,
        ),
        check_vma=False,
    )
```

```python
import jax
import jax.numpy as jnp
from jax import lax
from jax.experimental import pallas as pl
from jax.experimental.pallas import tpu as pltpu
from jax.sharding import PartitionSpec as P

QUERY_HEADS = 16
KEY_VALUE_HEADS = 8
HEAD_SIZE = 96
WIDTH = 1536
FF = 4096
THETA = 100000.0
EPSILON = 1e-05
MESH = pl.DeviceIdType.MESH
N_X = 4
N_C = 16
BF = jnp.bfloat16
F32 = jnp.float32


def mm(a, b):
    return jnp.dot(a, b, preferred_element_type=F32)


def mm_tn(a, b):
    return lax.dot_general(a, b, (((0,), (0,)), ((), ())), preferred_element_type=F32)


def mm_nt(a, b):
    return lax.dot_general(a, b, (((1,), (1,)), ((), ())), preferred_element_type=F32)


def remote(src, dst, send, recv, device):
    return pltpu.make_async_remote_copy(
        src_ref=src, dst_ref=dst, send_sem=send, recv_sem=recv, device_id=device, device_id_type=MESH
    )


def part(start, size):
    return pl.ds(pl.multiple_of(start, size), size)


GRADS = {"gate": (96, 1024), "up": (96, 1024), "down": (64, 1536), "qkv": (96, 768), "out": (96, 384)}
RINGS = {"gate": ("y", 1), "up": ("y", -1), "down": ("z", 1), "qkv": ("z", -1), "out": ("z", -1)}


def grad_kernel(n2, nf, dgu, dqkv, att, dbr, hidden, dyf, gains, *refs):
    names = list(GRADS)
    held = dict(zip(names, refs[:5]))
    o_gain = refs[5]
    own = dict(zip(names, refs[6:11]))
    first = dict(zip(names, refs[11:16]))
    second = dict(zip(names, refs[16:21]))
    gain_in, send, recv, local_sem, send_g, recv_g = refs[21:]
    x = lax.axis_index("fsdp")
    c = lax.axis_index("ctx")
    y, z = lax.rem(c, 4), c // 4
    where = {"x": x, "y": y, "z": z}

    def near(axis, step):
        if axis == "x":
            return {"fsdp": lax.rem(x + step + 4, 4)}
        if axis == "y":
            return {"ctx": 4 * z + lax.rem(y + step + 4, 4)}
        return {"ctx": 4 * lax.rem(z + step + 4, 4) + y}

    mirror = {"y": {"fsdp": y, "ctx": 4 * z + x}, "z": {"fsdp": z, "ctx": 4 * x + y}}

    barrier = pltpu.get_barrier_semaphore()
    for axis in "xyz":
        for step in (1, 2, 3):
            pl.semaphore_signal(barrier, inc=1, device_id=near(axis, step), device_id_type=MESH)
    for axis in "yz":
        pl.semaphore_signal(barrier, inc=1, device_id=mirror[axis], device_id_type=MESH)
    pl.semaphore_wait(barrier, 11)

    def ring(name):
        axis, d = RINGS[name]
        other = "z" if axis == "y" else "y"
        return names.index(name), axis, other, d, where[axis], where[other]

    def at(i, d, s):
        return lax.rem(i - d * s + 8, 4)

    def copy_first(name, s, q):
        f, axis, other, d, i, j = ring(name)
        p = at(j, d, 1 + q)
        return remote(
            own[name].at[at(i, d, 1 + s), p],
            first[name].at[s, p],
            send.at[f, 4 * s + q],
            recv.at[f, 4 * s + q],
            near(axis, d),
        )

    def copy_second(name, s):
        f, axis, other, d, i, j = ring(name)
        return remote(
            own[name].at[i, at(j, d, 1 + s)],
            second[name].at[s],
            send.at[f, 12 + s],
            recv.at[f, 12 + s],
            near(other, d),
        )

    def copy_mirror(name):
        f, axis, other, d, i, j = ring(name)
        return remote(
            own[name].at[i, j], held[name].at[x, j], send.at[f, 15], recv.at[f, 15], mirror[axis]
        )

    def copy_own(name):
        f, axis, other, d, i, j = ring(name)
        group = x if name in ("gate", "up", "qkv") else i
        return pltpu.make_async_copy(own[name].at[i, j], held[name].at[group, j], local_sem.at[f])

    def copy_small(name, s):
        f, axis, other, d, i, j = ring(name)
        place = held[name].at[i, at(j, d, s)]
        return remote(place, place, send.at[f, 16 + s], recv.at[f, 16 + s], near(other, d))

    def copy_big(name, s, q):
        f, axis, other, d, i, j = ring(name)
        place = held[name].at[at(i, d, s), at(j, d, q)]
        n = 20 + 4 * s + q
        return remote(place, place, send.at[f, n], recv.at[f, n], near(axis, d))

    def gain_copy(n, k):
        axis = "xyz"[n]
        if n == 0:
            src = gains.at[:, part(lax.rem(x + k, 4) * 384, 384)]
        else:
            src = gain_in.at[n, 0]
        return remote(src, gain_in.at[n, k], send_g.at[n, k], recv_g.at[n, k], near(axis, k))

    def gain_start(n):
        for k in (1, 2, 3):
            gain_copy(n, k).start()

    def gain_sum(n):
        mine = gains[:, part(x * 384, 384)] if n == 0 else gain_in[n, 0]
        for k in (1, 2, 3):
            gain_copy(n, k).wait()
        return mine + gain_in[n, 1] + gain_in[n, 2] + gain_in[n, 3]

    gain_start(0)

    total = mm_tn(att[...], dbr[...]).astype(BF)
    for g in range(4):
        for p in range(4):
            own["out"][g, p] = total[96 * g : 96 * g + 96, 384 * p : 384 * p + 384]

    def compute(s, carry):
        def group(name):
            f, axis, other, d, i, j = ring(name)
            return at(i, d, 1 + s)

        g = group("gate")
        own["gate"][g] = mm_tn(n2[:, part(g * 384, 384)], dgu[:, :1024]).astype(BF).reshape(4, 96, 1024)
        g = group("up")
        own["up"][g] = mm_tn(n2[:, part(g * 384, 384)], dgu[:, 1024:]).astype(BF).reshape(4, 96, 1024)
        g = group("down")
        own["down"][g] = mm_tn(hidden[:, part(g * 256, 256)], dyf[...]).astype(BF).reshape(4, 64, 1536)
        g = group("qkv")
        own["qkv"][g] = mm_tn(nf[:, part(g * 384, 384)], dqkv[...]).astype(BF).reshape(4, 96, 768)

        @pl.when(s == 0)
        def _():
            for q in range(4):
                for name in names:
                    copy_first(name, 0, q).start()

        return carry

    lax.fori_loop(0, 4, compute, 0)
    gain_in[1, 0] = gain_sum(0)
    gain_start(1)

    def add_first(t, carry):
        s, q = t // 4, lax.rem(t, 4)
        for name in names:
            f, axis, other, d, i, j = ring(name)
            copy_first(name, s, q).wait_recv()
            g, p = at(i, d, 2 + s), at(j, d, 1 + q)
            own[name][g, p] = own[name][g, p] + first[name][s, p]

            @pl.when(s < 2)
            def _(name=name):
                copy_first(name, s + 1, q).start()

            @pl.when(t == 8)
            def _(name=name):
                copy_second(name, 0).start()

        return carry

    lax.fori_loop(0, 12, add_first, 0)
    gain_in[2, 0] = gain_sum(1)
    gain_start(2)

    def add_second(s, carry):
        for name in names:
            f, axis, other, d, i, j = ring(name)
            copy_second(name, s).wait_recv()
            p = at(j, d, 2 + s)
            own[name][i, p] = own[name][i, p] + second[name][s]

            @pl.when(s < 2)
            def _(name=name):
                copy_second(name, s + 1).start()

        return carry

    lax.fori_loop(0, 3, add_second, 0)

    for name in ("gate", "up", "qkv"):
        axis = RINGS[name][0]

        @pl.when(where[axis] != x)
        def _(name=name):
            copy_mirror(name).start()

        @pl.when(where[axis] == x)
        def _(name=name):
            copy_own(name).start()

    for name in ("down", "out"):
        copy_own(name).start()
    for name in ("down", "out"):
        copy_own(name).wait()
    for name in ("gate", "up", "qkv"):
        axis = RINGS[name][0]

        @pl.when(where[axis] != x)
        def _(name=name):
            copy_mirror(name).wait()

        @pl.when(where[axis] == x)
        def _(name=name):
            copy_own(name).wait()

    def hand_small(q, carry):
        for name in names:

            @pl.when(q > 0)
            def _(name=name):
                copy_small(name, q - 1).wait_recv()

            @pl.when(q < 3)
            def _(name=name):
                copy_small(name, q).start()

            copy_big(name, 0, q).start()
        return carry

    lax.fori_loop(0, 4, hand_small, 0)

    def hand_big(t, carry):
        s, q = t // 4, lax.rem(t, 4)
        for name in names:
            copy_big(name, s, q).wait_recv()

            @pl.when(s < 2)
            def _(name=name):
                copy_big(name, s + 1, q).start()

        return carry

    lax.fori_loop(0, 12, hand_big, 0)
    o_gain[...] = gain_sum(2)

    def sent(t, carry):
        s, q = t // 4, lax.rem(t, 4)
        for name in names:
            copy_first(name, s, q).wait_send()
            copy_big(name, s, q).wait_send()
        return carry

    lax.fori_loop(0, 12, sent, 0)

    def sent_small(s, carry):
        for name in names:
            copy_second(name, s).wait_send()
            copy_small(name, s).wait_send()
        return carry

    lax.fori_loop(0, 3, sent_small, 0)


def reduce_grads(n2, nf, dgu, dqkv, att, dbr, hidden, dyf, gains, cid):
    vm = pl.BlockSpec(memory_space=pltpu.VMEM)
    hbm = pl.BlockSpec(memory_space=pl.ANY)
    dma = pltpu.SemaphoreType.DMA
    sizes = list(GRADS.values())
    return pl.pallas_call(
        grad_kernel,
        out_shape=[jax.ShapeDtypeStruct((4, 4) + s, BF) for s in sizes]
        + [jax.ShapeDtypeStruct((8, 384), F32)],
        in_specs=[vm] * 9,
        out_specs=[hbm] * 5 + [vm],
        scratch_shapes=[pltpu.VMEM((4, 4) + s, BF) for s in sizes]
        + [pltpu.VMEM((3, 4) + s, BF) for s in sizes]
        + [pltpu.VMEM((3,) + s, BF) for s in sizes]
        + [
            pltpu.VMEM((3, 4, 8, 384), F32),
            dma((5, 32)),
            dma((5, 32)),
            dma((5,)),
            dma((3, 4)),
            dma((3, 4)),
        ],
        name="reduce_grads",
        compiler_params=pltpu.CompilerParams(
            collective_id=cid, has_side_effects=True, vmem_limit_bytes=60 << 20
        ),
    )(n2, nf, dgu, dqkv, att, dbr, hidden, dyf, gains)


def widen_kernel(w_gate, w_up, w_down, w_qkv, w_out, gate, up, query, key, value, g_out, g_down):
    g_down[...] = w_down[...].astype(F32)
    keys, values = [], []
    for x in range(N_X):
        gate[:, 1024 * x : 1024 * x + 1024] = w_gate[x, 0].astype(F32)
        up[:, 1024 * x : 1024 * x + 1024] = w_up[x, 0].astype(F32)
        g_out[:, 384 * x : 384 * x + 384] = w_out[0, x].astype(F32)
        heads = w_qkv[x, 0].astype(F32)
        query[:, 384 * x : 384 * x + 384] = jnp.concatenate(
            [heads[:, :192], heads[:, 384:576]], axis=1
        )
        keys += [heads[:, 192:288], heads[:, 576:672]]
        values += [heads[:, 288:384], heads[:, 672:768]]
    key[...] = jnp.concatenate(keys, axis=1)
    value[...] = jnp.concatenate(values, axis=1)


def widen(gate, up, down, qkv, out):
    steps = 8

    def spec(r, cols):
        return pl.BlockSpec((r, cols), lambda i: (i, 0))

    def shape(r, cols):
        return jax.ShapeDtypeStruct((r, cols), F32)

    def blocks(cols):
        return pl.BlockSpec((4, 1, 48, cols), lambda i: (0, i // 2, i % 2, 0))

    return pl.pallas_call(
        widen_kernel,
        grid=(steps,),
        out_shape=[
            shape(384, FF),
            shape(384, FF),
            shape(384, 1536),
            shape(384, 768),
            shape(384, 768),
            shape(384, 1536),
            shape(1024, 1536),
        ],
        in_specs=[
            blocks(1024),
            blocks(1024),
            spec(128, 1536),
            blocks(768),
            pl.BlockSpec((1, 4, 48, 384), lambda i: (i // 2, 0, i % 2, 0)),
        ],
        out_specs=[
            spec(48, FF),
            spec(48, FF),
            spec(48, 1536),
            spec(48, 768),
            spec(48, 768),
            spec(48, 1536),
            spec(128, 1536),
        ],
        name="widen",
        compiler_params=pltpu.CompilerParams(vmem_limit_bytes=60 << 20),
    )(gate, up, down.reshape(1024, 1536), qkv, out)


X_GAIN, X_POS, X_IN, X_DY, X_QKV, X_GATE, X_UP, X_SUM1, X_N2, X_SUM2, X_SUM3, X_DBR, X_SUM4 = range(13)
C_POS, C_QKV, C_ATT, C_DATT, C_DQKV = range(5)
H_OUT, H_DX = range(2)
SCALE = HEAD_SIZE ** (-0.5)


def spread(w, heads):
    blank = jnp.zeros((w.shape[0], 16), w.dtype)
    pieces = []
    for h in heads:
        pieces += [w[:, 96 * h : 96 * h + 48], blank, w[:, 96 * h + 48 : 96 * h + 96], blank]
    return pieces


def as_column(row):
    eye = lax.broadcasted_iota(jnp.int32, (128, 128), 0) == lax.broadcasted_iota(
        jnp.int32, (128, 128), 1
    )
    return jnp.sum(jnp.where(eye, jnp.broadcast_to(row, (128, 128)), 0.0), axis=1, keepdims=True)


def turn(u, cosine, sine):
    return u * cosine + pltpu.roll(u, 64, 1) * sine


def layer_kernel(
    xin,
    dyin,
    pos,
    freq,
    gains,
    wq,
    wk,
    wv,
    wo,
    wd,
    wg,
    wu,
    out,
    dx,
    nf,
    n2,
    dgu,
    dqkv,
    att,
    dbr,
    hidden,
    dyf,
    ggain,
    wsend,
    wqkv,
    wgf,
    wuf,
    wop,
    xall,
    gain,
    posx,
    posv,
    posc,
    posr,
    posk,
    cos_c,
    sin_c,
    cos_s,
    sin_s,
    qsend,
    qs,
    vt,
    kt,
    lse,
    osend,
    attp,
    mid,
    gate,
    up,
    own,
    psend,
    prec,
    dsend,
    das,
    dk,
    dv,
    dqs,
    dqp,
    xs,
    xr,
    cs,
    cr,
    hs,
    hr,
):
    section = lax.axis_index("section")
    x = lax.axis_index("fsdp")
    c = lax.axis_index("ctx")
    first, second = section == 0, section == 1
    my_rows = part(128 * x, 128)

    barrier = pltpu.get_barrier_semaphore()
    for k in range(1, 4):
        pl.semaphore_signal(
            barrier, inc=1, device_id={"fsdp": lax.rem(x + k, 4)}, device_id_type=MESH
        )
    for k in range(4):
        pl.semaphore_signal(
            barrier,
            inc=1,
            device_id={"section": 1 - section, "fsdp": lax.rem(x + k, 4)},
            device_id_type=MESH,
        )

    def greet(k, carry):
        pl.semaphore_signal(
            barrier, inc=1, device_id={"ctx": lax.rem(c + k, 16)}, device_id_type=MESH
        )
        return carry

    lax.fori_loop(1, 16, greet, 0)
    pl.semaphore_wait(barrier, 22)

    def ahead(k):
        return lax.rem(x + k, 4)

    def behind(k):
        return lax.rem(x - k + 4, 4)

    def over_x(e, k, src, dst):
        return remote(src, dst, xs.at[e, k], xr.at[e, k], {"fsdp": ahead(k)})

    def over_c(e, to, src, dst):
        k = lax.rem(to - c + 16, 16)
        return remote(src, dst, cs.at[e, k], cr.at[e, k], {"ctx": to})

    def across(e, k, src, dst):
        return remote(
            src, dst, hs.at[e, k], hr.at[e, k], {"section": 1 - section, "fsdp": ahead(k)}
        )

    def rows_to_all(e, ref, k):
        return over_x(e, k, ref.at[my_rows], ref.at[my_rows])

    def sum_copy(e, k):
        n = (X_SUM1, X_SUM2, X_SUM3, X_SUM4).index(e)
        return over_x(e, k, psend.at[n % 2, ahead(k)], prec.at[n % 2, k])

    def gain_copy(k):
        place = gain.at[:, part(384 * x, 384)]
        return over_x(X_GAIN, k, gains, place)

    def pos_copy(k):
        return over_x(X_POS, k, pos, posx.at[x])

    def in_copy(k):
        return over_x(X_IN, k, xin, xall.at[my_rows])

    def dy_copy(k):
        return over_x(X_DY, k, dyin, dyf.at[my_rows])

    def qkv_copy(k):
        return over_x(X_QKV, k, wsend.at[ahead(k)], wqkv.at[part(384 * x, 384)])

    def wide_copy(e, k):
        src, dst = (wg, wgf) if e == X_GATE else (wu, wuf)
        return over_x(e, k, src.at[:, part(1024 * ahead(k), 1024)], dst.at[part(384 * x, 384)])

    for k in (2, 1, 3):
        pos_copy(k).start()
        gain_copy(k).start()
    gain[:, part(384 * x, 384)] = gains[...]
    posx[x] = pos[...]

    for b in range(4):
        pieces = []
        for j in range(2):
            pieces += spread(wq[:, 384 * b + 192 * j : 384 * b + 192 * j + 192], (0, 1))
            pieces += spread(wk[:, 96 * (2 * b + j) : 96 * (2 * b + j) + 96], (0,))
            pieces += [
                wv[:, 96 * (2 * b + j) : 96 * (2 * b + j) + 96],
                jnp.zeros((384, 32), BF),
            ]
        wsend[b] = jnp.concatenate(pieces, axis=1)
    for k in (2, 1, 3):
        qkv_copy(k).start()
    wqkv[part(384 * x, 384), :] = wsend[x]

    @pl.when(first)
    def _():
        for k in (2, 1, 3):
            in_copy(k).start()
        xall[my_rows, :] = xin[...]

    @pl.when(second)
    def _():
        for k in (2, 1, 3):
            dy_copy(k).start()
        dyf[my_rows, :] = dyin[...]

    own_wide = [
        pltpu.make_async_copy(
            src.at[:, part(1024 * x, 1024)], dst.at[part(384 * x, 384)], xs.at[e, 0]
        )
        for e, src, dst in ((X_GATE, wg, wgf), (X_UP, wu, wuf))
    ]
    for copy in own_wide:
        copy.start()

    wop[...] = jnp.zeros_like(wop)
    for h in range(4):
        wop[128 * h : 128 * h + 96, :] = wo[96 * h : 96 * h + 96, :]

    lane = lax.broadcasted_iota(jnp.int32, (1, 128), 1)
    sign = jnp.where(lane < 64, -1.0, 1.0)
    for k in (1, 3, 2):
        pos_copy(k).wait()
    for b in range(4):
        block = posx[b]
        posv[b, 0] = block
        posv[b, 1] = pltpu.roll(block, 64, 1)

    def pos_to(to):
        return over_c(C_POS, to, posv.at[to // 4, lax.rem(to, 4) // 2], posc.at[c])

    def send_pos(k, carry):
        pos_to(lax.rem(c + k, 16)).start()
        return carry

    lax.fori_loop(1, 16, send_pos, 0)
    posc[c] = posv[c // 4, lax.rem(c, 4) // 2]
    for b in range(4):
        angle = as_column(posx[b][0:1, :]) * freq[0:1, :]
        cos_c[128 * b : 128 * b + 128, :] = jnp.cos(angle)
        sin_c[128 * b : 128 * b + 128, :] = jnp.sin(angle) * sign

    def await_pos(k, carry):
        pos_to(lax.rem(c + k, 16)).wait()
        return carry

    lax.fori_loop(1, 16, await_pos, 0)

    def tables(i, carry):
        row = jnp.where(lane < 64, posc[2 * i][0:1, :], pltpu.roll(posc[2 * i + 1], 64, 1)[0:1, :])
        block = part(128 * i, 128)
        posr[0:1, block] = row
        column = as_column(row)
        posk[block, :] = jnp.broadcast_to(column, (128, 128))
        angle = column * freq[0:1, :]
        cos_s[block, :] = jnp.cos(angle)
        sin_s[block, :] = jnp.sin(angle) * sign
        return carry

    lax.fori_loop(0, 8, tables, 0)
    for k in (1, 3, 2):
        gain_copy(k).wait()
    for k in (1, 3, 2):
        qkv_copy(k).wait()
    for k in (2, 1, 3):
        wide_copy(X_GATE, k).start()
        wide_copy(X_UP, k).start()
    gain_attn, gain_mlp = gain[0:1, :], gain[1:2, :]

    def out_copy(k):
        return across(H_OUT, k, out, xall.at[my_rows])

    def to_pair(ref, e, b, i, width, dst):
        src = ref.at[part(128 * b + 64 * (i // 2), 64), pl.ds(width * (i % 2), width)]
        return over_c(e, 4 * b + i, src, dst.at[part(64 * c, 64)])

    def from_pairs(e, width, b):
        for i in range(4):
            to = 4 * b + i

            @pl.when(to != c)
            def _(to=to):
                k = lax.rem(c - to + 16, 16)
                place = (qs if width == 512 else das).at[part(64 * to, 64)]
                pltpu.make_async_copy(place, place, cr.at[e, k]).wait()

    def project(k, carry):
        b = behind(k)
        rows = part(128 * b, 128)

        @pl.when(jnp.logical_and(first, k > 0))
        def _():
            in_copy(k).wait_recv()

        @pl.when(second)
        def _():
            out_copy(k).wait_recv()

        value = xall[rows, :].astype(F32)
        normed = (
            value
            * lax.rsqrt(jnp.mean(value * value, axis=-1, keepdims=True) + EPSILON)
            * gain_attn
        ).astype(BF)
        nf[rows, :] = normed
        u = mm(normed, wqkv[...])
        cosine, sine = cos_c[rows, :], sin_c[rows, :]
        for h in range(8):
            head = u[:, 128 * h : 128 * h + 128]
            if h % 4 != 3:
                head = turn(head, cosine, sine)
            qsend[rows, 128 * h : 128 * h + 128] = head.astype(BF)
        for i in range(4):

            @pl.when(4 * b + i != c)
            def _(i=i):
                to_pair(qsend, C_QKV, b, i, 512, qs).start()

            @pl.when(4 * b + i == c)
            def _(i=i):
                qs[part(64 * c, 64), :] = qsend[
                    part(128 * b + 64 * (i // 2), 64), 512 * (i % 2) : 512 * (i % 2) + 512
                ]

        return carry

    lax.fori_loop(0, 4, project, 0)

    def await_qkv(k, carry):
        place = qs.at[part(64 * lax.rem(c - k + 16, 16), 64)]
        over_c(C_QKV, lax.rem(c + k, 16), place, place).wait_recv()
        return carry

    lax.fori_loop(1, 16, await_qkv, 0)

    vt[...] = qs[:, 384:512].T
    kt[...] = qs[:, 256:384].T

    def masked(q, cols):
        st = mm_nt(qs[:, 256:384], q) * SCALE
        return jnp.where(posk[:, 0:1] <= posr[0:1, cols], st, -1e30)

    def att_place():
        return attp.at[part(64 * (c // 2), 64), part(256 * lax.rem(c, 2), 256)]

    def att_to(to):
        return over_c(C_ATT, to, osend.at[part(64 * to, 64)], att_place())

    def attend(n, carry):
        rows = part(256 * n, 256)
        for g in range(2):
            st = masked(qs[rows, 128 * g : 128 * g + 128], rows)
            top = jnp.max(st, axis=0, keepdims=True)
            e = jnp.exp(st - top)
            total = jnp.sum(e, axis=0, keepdims=True)
            lse[g : g + 1, rows] = top + jnp.log(total)
            pt = (e * (1.0 / total)).astype(BF)
            osend[rows, 128 * g : 128 * g + 128] = mm(vt[...], pt).T.astype(BF)
        for i in range(4):
            to = 4 * n + i

            @pl.when(to != c)
            def _(to=to):
                att_to(to).start()

            @pl.when(to == c)
            def _(to=to):
                attp[part(64 * (c // 2), 64), part(256 * lax.rem(c, 2), 256)] = osend[
                    part(64 * to, 64), :
                ]

        return carry

    lax.fori_loop(0, 4, attend, 0)

    def await_att(b):
        for i in range(4):
            to = 4 * b + i

            @pl.when(to != c)
            def _(to=to, i=i):
                k = lax.rem(c - to + 16, 16)
                place = attp.at[part(64 * (2 * b + i // 2), 64), pl.ds(256 * (i % 2), 256)]
                remote(place, place, cs.at[C_ATT, k], cr.at[C_ATT, k], {"ctx": lax.rem(c + k, 16)}).wait_recv()

    def give(n, e, k, b, value):
        @pl.when(k < 4)
        def _():
            psend[n % 2, b] = value.astype(BF)
            sum_copy(e, k).start()

        @pl.when(k == 4)
        def _():
            own[...] = value

    def take(n, e):
        total = own[...]
        for k in (1, 3, 2):
            sum_copy(e, k).wait_recv()
            total = total + prec[n % 2, k].astype(F32)
        return total

    def combine(k, carry):
        b = lax.rem(x + k, 4)
        await_att(b)
        give(0, X_SUM1, k, b, mm(attp[part(128 * b, 128), :], wop[...]))
        return carry

    lax.fori_loop(1, 5, combine, 0)
    middle = xall[my_rows, :].astype(F32) + take(0, X_SUM1)
    mid[...] = middle
    n2[my_rows, :] = (
        middle * lax.rsqrt(jnp.mean(middle * middle, axis=-1, keepdims=True) + EPSILON) * gain_mlp
    ).astype(BF)
    for k in (2, 1, 3):
        rows_to_all(X_N2, n2, k).start()

    for copy in own_wide:
        copy.wait()
    for k in (1, 3, 2):
        wide_copy(X_GATE, k).wait()
        wide_copy(X_UP, k).wait()

    def pair(blocks, ref):
        return jnp.concatenate([ref[part(128 * b, 128), :] for b in blocks], axis=0)

    def feed(ks, final):
        blocks = [behind(k) for k in ks]
        a = pair(blocks, n2)
        ga, u = mm(a, wgf[...]), mm(a, wuf[...])
        h = (ga * (1.0 / (1.0 + jnp.exp(-ga))) * u).astype(BF)
        result = mm(h, wd[...])
        for n, (k, b) in enumerate(zip(ks, blocks)):
            rows, piece = part(128 * b, 128), slice(128 * n, 128 * n + 128)
            gate[rows, :] = ga[piece]
            up[rows, :] = u[piece]
            hidden[rows, :] = h[piece]
            if k == 0:
                own[...] = result[piece]
            else:
                psend[1, b] = result[piece].astype(BF)
                sum_copy(X_SUM2, 4 - k).start()

    rows_to_all(X_N2, n2, 1).wait_recv()
    feed((1, 0), False)
    rows_to_all(X_N2, n2, 3).wait_recv()
    rows_to_all(X_N2, n2, 2).wait_recv()
    feed((2, 3), True)
    out[...] = (mid[...] + take(1, X_SUM2)).astype(BF)

    @pl.when(first)
    def _():
        for k in range(4):
            out_copy(k).start()

    def dx_copy(k):
        return across(H_DX, k, dx, dyf.at[my_rows])

    @pl.when(first)
    def _():
        for k in range(4):
            dx_copy(k).wait_recv()

    @pl.when(second)
    def _():
        for k in (1, 3, 2):
            dy_copy(k).wait_recv()

    def feed_back(ks):
        blocks = [ahead(k) for k in ks]
        dh = mm_nt(pair(blocks, dyf), wd[...])
        ga, u = pair(blocks, gate), pair(blocks, up)
        s = 1.0 / (1.0 + jnp.exp(-ga))
        dga = (dh * u * (s * (1.0 + ga * (1.0 - s)))).astype(BF)
        du = (dh * (ga * s)).astype(BF)
        result = mm_nt(dga, wgf[...]) + mm_nt(du, wuf[...])
        for n, (k, b) in enumerate(zip(ks, blocks)):
            rows, piece = part(128 * b, 128), slice(128 * n, 128 * n + 128)
            dgu[rows, 0:1024] = dga[piece]
            dgu[rows, 1024:2048] = du[piece]
            if k == 0:
                own[...] = result[piece]
            else:
                psend[0, b] = result[piece].astype(BF)
                sum_copy(X_SUM3, k).start()

    for k in (1, 2, 3):
        sum_copy(X_SUM1, k).wait_send()
    feed_back((2, 1))
    feed_back((3, 0))

    def norm_back(value, grad, gain_row):
        r = lax.rsqrt(jnp.mean(value * value, axis=-1, keepdims=True) + EPSILON)
        unit = value * r
        t = grad * gain_row
        back = r * (t - unit * jnp.mean(t * unit, axis=-1, keepdims=True))
        return back, jnp.sum(grad * unit, axis=0, keepdims=True)

    back, g_mlp = norm_back(mid[...], take(2, X_SUM3), gain_mlp)
    dmid = dyf[my_rows, :].astype(F32) + back
    mid[...] = dmid
    ggain[...] = jnp.zeros_like(ggain)
    ggain[1:2, :] = g_mlp
    dbr[my_rows, :] = dmid.astype(BF)
    for k in (2, 1, 3):
        rows_to_all(X_DBR, dbr, k).start()

    def branch(k, carry):
        b = behind(k)
        rows = part(128 * b, 128)

        @pl.when(k > 0)
        def _():
            rows_to_all(X_DBR, dbr, k).wait_recv()

        dsend[rows, :] = mm_nt(dbr[rows, :], wop[...]).astype(BF)
        for i in range(4):

            @pl.when(4 * b + i != c)
            def _(i=i):
                to_pair(dsend, C_DATT, b, i, 256, das).start()

            @pl.when(4 * b + i == c)
            def _(i=i):
                das[part(64 * c, 64), :] = dsend[
                    part(128 * b + 64 * (i // 2), 64), 256 * (i % 2) : 256 * (i % 2) + 256
                ]

        return carry

    lax.fori_loop(0, 4, branch, 0)

    def await_das(k, carry):
        place = das.at[part(64 * lax.rem(c - k + 16, 16), 64)]
        over_c(C_DATT, lax.rem(c + k, 16), place, place).wait_recv()
        return carry

    lax.fori_loop(1, 16, await_das, 0)
    dk[...] = jnp.zeros_like(dk)
    dv[...] = jnp.zeros_like(dv)

    def attend_back(n, carry):
        rows = part(256 * n, 256)
        for g in range(2):
            cols = slice(128 * g, 128 * g + 128)
            q, da = qs[rows, cols], das[rows, cols]
            p = jnp.exp(masked(q, rows) - lse[g : g + 1, rows])
            dp = mm_nt(qs[:, 384:512], da)
            dv[...] += mm(p.astype(BF), da)
            ds = (p * (dp - jnp.sum(p * dp, axis=0, keepdims=True))).astype(BF)
            dk[...] += mm(ds, q)
            dq = mm(kt[...], ds).T * SCALE
            dqs[rows, cols] = turn(dq, cos_s[rows, :], -sin_s[rows, :]).astype(BF)
        return carry

    lax.fori_loop(0, 4, attend_back, 0)
    dqs[:, 256:384] = turn(dk[...] * SCALE, cos_s[...], -sin_s[...]).astype(BF)
    dqs[:, 384:512] = dv[...].astype(BF)

    def dqkv_to(to):
        place = dqp.at[part(64 * (c // 2), 64), part(512 * lax.rem(c, 2), 512)]
        return over_c(C_DQKV, to, dqs.at[part(64 * to, 64)], place)

    def send_dqkv(k, carry):
        dqkv_to(lax.rem(c + k, 16)).start()
        return carry

    lax.fori_loop(1, 16, send_dqkv, 0)
    dqp[part(64 * (c // 2), 64), part(512 * lax.rem(c, 2), 512)] = dqs[part(64 * c, 64), :]

    def await_dqkv(b):
        for i in range(4):
            to = 4 * b + i

            @pl.when(to != c)
            def _(to=to, i=i):
                k = lax.rem(c - to + 16, 16)
                place = dqp.at[part(64 * (2 * b + i // 2), 64), pl.ds(512 * (i % 2), 512)]
                remote(place, place, cs.at[C_DQKV, k], cr.at[C_DQKV, k], {"ctx": lax.rem(c + k, 16)}).wait_recv()

    for k in (1, 2, 3):
        sum_copy(X_SUM2, k).wait_send()

    def input_grad(k, carry):
        b = lax.rem(x + k, 4)
        await_dqkv(b)
        give(3, X_SUM4, k, b, mm_nt(dqp[part(128 * b, 128), :], wqkv[...]))
        return carry

    lax.fori_loop(1, 5, input_grad, 0)
    back, g_attn = norm_back(xall[my_rows, :].astype(F32), take(3, X_SUM4), gain_attn)
    dx[...] = (mid[...] + back).astype(BF)
    ggain[0:1, :] = g_attn

    @pl.when(second)
    def _():
        for k in range(4):
            dx_copy(k).start()

    for n in range(2):
        rows = slice(256 * n, 256 * n + 256)
        att[rows, :] = jnp.concatenate(
            [attp[rows, 128 * h : 128 * h + 96] for h in range(4)], axis=1
        )
        pieces = []
        for h in range(8):
            if h % 4 == 3:
                pieces.append(dqp[rows, 128 * h : 128 * h + 96])
            else:
                pieces.append(dqp[rows, 128 * h : 128 * h + 48])
                pieces.append(dqp[rows, 128 * h + 64 : 128 * h + 112])
        dqkv[rows, :] = jnp.concatenate(pieces, axis=1)

    def sent_c(k, carry):
        to = lax.rem(c + k, 16)
        place = qs.at[part(64 * to, 64)]
        over_c(C_QKV, to, place, place).wait_send()
        att_to(to).wait_send()
        place = das.at[part(64 * to, 64)]
        over_c(C_DATT, to, place, place).wait_send()
        dqkv_to(to).wait_send()
        return carry

    lax.fori_loop(1, 16, sent_c, 0)
    for k in (1, 2, 3):
        for e in (X_SUM3, X_SUM4):
            sum_copy(e, k).wait_send()
        rows_to_all(X_N2, n2, k).wait_send()
        rows_to_all(X_DBR, dbr, k).wait_send()

    @pl.when(first)
    def _():
        for k in (1, 2, 3):
            in_copy(k).wait_send()
        for k in range(4):
            out_copy(k).wait_send()

    @pl.when(second)
    def _():
        for k in (1, 2, 3):
            dy_copy(k).wait_send()
        for k in range(4):
            dx_copy(k).wait_send()


def run_layer(xin, dyin, pos, freq, gains, wq, wk, wv, wo, wd, wg, wu, cid):
    vm = pl.BlockSpec(memory_space=pltpu.VMEM)
    hbm = pl.BlockSpec(memory_space=pl.ANY)
    dma = pltpu.SemaphoreType.DMA
    shapes = [
        ((128, WIDTH), BF),
        ((128, WIDTH), BF),
        ((512, WIDTH), BF),
        ((512, WIDTH), BF),
        ((512, 2048), BF),
        ((512, 768), BF),
        ((512, 384), BF),
        ((512, WIDTH), BF),
        ((512, 1024), BF),
        ((512, WIDTH), BF),
        ((8, WIDTH), F32),
    ]
    scratch = [
        ((4, 384, 1024), BF),
        ((WIDTH, 1024), BF),
        ((WIDTH, 1024), BF),
        ((WIDTH, 1024), BF),
        ((512, WIDTH), BF),
        ((512, WIDTH), BF),
        ((8, WIDTH), F32),
        ((4, 8, 128), F32),
        ((4, 2, 8, 128), F32),
        ((16, 8, 128), F32),
        ((8, 1024), F32),
        ((1024, 128), F32),
        ((512, 128), F32),
        ((512, 128), F32),
        ((1024, 128), F32),
        ((1024, 128), F32),
        ((512, 1024), BF),
        ((1024, 512), BF),
        ((128, 1024), BF),
        ((128, 1024), BF),
        ((8, 1024), F32),
        ((1024, 256), BF),
        ((512, 512), BF),
        ((128, WIDTH), F32),
        ((512, 1024), F32),
        ((512, 1024), F32),
        ((128, WIDTH), F32),
        ((2, 4, 128, WIDTH), BF),
        ((2, 4, 128, WIDTH), BF),
        ((512, 512), BF),
        ((1024, 256), BF),
        ((1024, 128), F32),
        ((1024, 128), F32),
        ((1024, 512), BF),
        ((512, 1024), BF),
    ]
    return pl.pallas_call(
        layer_kernel,
        out_shape=[jax.ShapeDtypeStruct(s, d) for s, d in shapes],
        in_specs=[vm] * 10 + [hbm] * 2,
        out_specs=[vm] * len(shapes),
        scratch_shapes=[pltpu.VMEM(s, d) for s, d in scratch]
        + [dma((13, 4)), dma((13, 4)), dma((5, 16)), dma((5, 16)), dma((2, 4)), dma((2, 4))],
        name="layer",
        compiler_params=pltpu.CompilerParams(
            collective_id=cid, has_side_effects=True, vmem_limit_bytes=63 << 20
        ),
    )(xin, dyin, pos, freq, gains, wq, wk, wv, wo, wd, wg, wu)


def local(
    inputs,
    positions,
    out_grad,
    norm_attn,
    w_query,
    key_weight,
    value_weight,
    output_weight,
    norm_mlp,
    w_gate,
    w_up,
    w_down,
):
    lane = jnp.arange(128)
    index = jnp.where(lane < 64, lane, lane - 64)
    freq = jnp.where(index < 48, THETA ** (-(index.astype(F32) * 2.0 / HEAD_SIZE)), 0.0)
    freq = jnp.broadcast_to(freq[None], (8, 128))
    pos = jnp.broadcast_to(positions.reshape(1, 128).astype(F32), (8, 128))
    gains = jnp.concatenate([norm_attn, norm_mlp, jnp.zeros((6, 384), BF)], axis=0).astype(F32)
    out, dx, nf, n2, dgu, dqkv, att, dbr, hidden, dyf, ggain = run_layer(
        inputs.reshape(128, WIDTH),
        out_grad.reshape(128, WIDTH),
        pos,
        freq,
        gains,
        w_query[0],
        key_weight[0],
        value_weight[0],
        output_weight[0],
        w_down[0],
        w_gate[0],
        w_up[0],
        0,
    )
    *summed, g_gain = reduce_grads(n2, nf, dgu, dqkv, att, dbr, hidden, dyf, ggain, 1)
    g_gate, g_up, g_query, g_key, g_value, g_out, g_down = widen(*summed)
    return (
        out.reshape(1, 2, 64, WIDTH),
        dx.reshape(1, 2, 64, WIDTH),
        g_gain[0:1],
        g_query[None],
        g_key[None],
        g_value[None],
        g_out[None],
        g_gain[1:2],
        g_gate[None],
        g_up[None],
        g_down[None],
    )


def solution(mesh):
    rows = P("section", "fsdp", None)
    return jax.shard_map(
        local,
        mesh=mesh,
        in_specs=(
            P("fsdp", "ctx", None),
            P("fsdp", "ctx"),
            P("fsdp", "ctx", None),
            P("section", "fsdp"),
            rows,
            rows,
            rows,
            rows,
            P("section", "fsdp"),
            rows,
            rows,
            rows,
        ),
        out_specs=(
            P("section", "fsdp", "ctx", None),
            P("section", "fsdp", "ctx", None),
            P("section", "fsdp"),
            rows,
            rows,
            rows,
            rows,
            P("section", "fsdp"),
            rows,
            rows,
            rows,
        ),
        check_vma=False,
    )
```

```python
import jax
import jax.numpy as jnp
import numpy as np
from jax import lax
from jax.experimental import pallas as pl
from jax.experimental.pallas import tpu as pltpu
from jax.sharding import PartitionSpec as P

QUERY_HEADS = 16
KEY_VALUE_HEADS = 8
HEAD_SIZE = 96
WIDTH = 1536
FF = 4096
THETA = 100000.0
EPSILON = 1e-05
MESH = pl.DeviceIdType.MESH
N_X = 4
N_C = 16
BF = jnp.bfloat16
F32 = jnp.float32


def mm(a, b):
    return jnp.dot(a, b, preferred_element_type=F32)


def mm_tn(a, b):
    return lax.dot_general(a, b, (((0,), (0,)), ((), ())), preferred_element_type=F32)


def mm_nt(a, b):
    return lax.dot_general(a, b, (((1,), (1,)), ((), ())), preferred_element_type=F32)


def remote(src, dst, send, recv, device):
    return pltpu.make_async_remote_copy(
        src_ref=src, dst_ref=dst, send_sem=send, recv_sem=recv, device_id=device, device_id_type=MESH
    )


def part(start, size):
    return pl.ds(pl.multiple_of(start, size), size)


GRADS = {"gate": (96, 1024), "up": (96, 1024), "down": (64, 1536), "qkv": (96, 768), "out": (96, 384)}
RINGS = {"gate": ("y", 1), "up": ("y", -1), "down": ("z", 1), "qkv": ("z", -1), "out": ("z", -1)}


def grad_kernel(n2, nf, dgu, dqkv, att, dbr, hidden, dyf, gains, *refs):
    names = list(GRADS)
    held = dict(zip(names, refs[:5]))
    o_gain = refs[5]
    own = dict(zip(names, refs[6:11]))
    first = dict(zip(names, refs[11:16]))
    second = dict(zip(names, refs[16:21]))
    gain_in, send, recv, local_sem, send_g, recv_g = refs[21:]
    x = lax.axis_index("fsdp")
    c = lax.axis_index("ctx")
    y, z = lax.rem(c, 4), c // 4
    where = {"x": x, "y": y, "z": z}

    def near(axis, step):
        if axis == "x":
            return {"fsdp": lax.rem(x + step + 4, 4)}
        if axis == "y":
            return {"ctx": 4 * z + lax.rem(y + step + 4, 4)}
        return {"ctx": 4 * lax.rem(z + step + 4, 4) + y}

    mirror = {"y": {"fsdp": y, "ctx": 4 * z + x}, "z": {"fsdp": z, "ctx": 4 * x + y}}

    barrier = pltpu.get_barrier_semaphore()
    for axis in "xyz":
        for step in (1, 2, 3):
            pl.semaphore_signal(barrier, inc=1, device_id=near(axis, step), device_id_type=MESH)
    for axis in "yz":
        pl.semaphore_signal(barrier, inc=1, device_id=mirror[axis], device_id_type=MESH)
    pl.semaphore_wait(barrier, 11)

    def ring(name):
        axis, d = RINGS[name]
        other = "z" if axis == "y" else "y"
        return names.index(name), axis, other, d, where[axis], where[other]

    def at(i, d, s):
        return lax.rem(i - d * s + 8, 4)

    def copy_first(name, s, q):
        f, axis, other, d, i, j = ring(name)
        p = at(j, d, 1 + q)
        return remote(
            own[name].at[at(i, d, 1 + s), p],
            first[name].at[s, p],
            send.at[f, 4 * s + q],
            recv.at[f, 4 * s + q],
            near(axis, d),
        )

    def copy_second(name, s):
        f, axis, other, d, i, j = ring(name)
        return remote(
            own[name].at[i, at(j, d, 1 + s)],
            second[name].at[s],
            send.at[f, 12 + s],
            recv.at[f, 12 + s],
            near(other, d),
        )

    def copy_mirror(name):
        f, axis, other, d, i, j = ring(name)
        return remote(
            own[name].at[i, j], held[name].at[x, j], send.at[f, 15], recv.at[f, 15], mirror[axis]
        )

    def copy_own(name):
        f, axis, other, d, i, j = ring(name)
        group = x if name in ("gate", "up", "qkv") else i
        return pltpu.make_async_copy(own[name].at[i, j], held[name].at[group, j], local_sem.at[f])

    def copy_small(name, s):
        f, axis, other, d, i, j = ring(name)
        place = held[name].at[i, at(j, d, s)]
        return remote(place, place, send.at[f, 16 + s], recv.at[f, 16 + s], near(other, d))

    def copy_big(name, s, q):
        f, axis, other, d, i, j = ring(name)
        place = held[name].at[at(i, d, s), at(j, d, q)]
        n = 20 + 4 * s + q
        return remote(place, place, send.at[f, n], recv.at[f, n], near(axis, d))

    def gain_copy(n, k):
        axis = "xyz"[n]
        if n == 0:
            src = gains.at[:, part(lax.rem(x + k, 4) * 384, 384)]
        else:
            src = gain_in.at[n, 0]
        return remote(src, gain_in.at[n, k], send_g.at[n, k], recv_g.at[n, k], near(axis, k))

    def gain_start(n):
        for k in (1, 2, 3):
            gain_copy(n, k).start()

    def gain_sum(n):
        mine = gains[:, part(x * 384, 384)] if n == 0 else gain_in[n, 0]
        for k in (1, 2, 3):
            gain_copy(n, k).wait()
        return mine + gain_in[n, 1] + gain_in[n, 2] + gain_in[n, 3]

    gain_start(0)

    total = mm_tn(att[...], dbr[...]).astype(BF)
    for g in range(4):
        for p in range(4):
            own["out"][g, p] = total[96 * g : 96 * g + 96, 384 * p : 384 * p + 384]

    def compute(s, carry):
        def group(name):
            f, axis, other, d, i, j = ring(name)
            return at(i, d, 1 + s)

        g = group("gate")
        own["gate"][g] = mm_tn(n2[:, part(g * 384, 384)], dgu[:, :1024]).astype(BF).reshape(4, 96, 1024)
        g = group("up")
        own["up"][g] = mm_tn(n2[:, part(g * 384, 384)], dgu[:, 1024:]).astype(BF).reshape(4, 96, 1024)
        g = group("down")
        own["down"][g] = mm_tn(hidden[:, part(g * 256, 256)], dyf[...]).astype(BF).reshape(4, 64, 1536)
        g = group("qkv")
        own["qkv"][g] = mm_tn(nf[:, part(g * 384, 384)], dqkv[...]).astype(BF).reshape(4, 96, 768)

        @pl.when(s == 0)
        def _():
            for q in range(4):
                for name in names:
                    copy_first(name, 0, q).start()

        return carry

    lax.fori_loop(0, 4, compute, 0)
    gain_in[1, 0] = gain_sum(0)
    gain_start(1)

    def add_first(t, carry):
        s, q = t // 4, lax.rem(t, 4)
        for name in names:
            f, axis, other, d, i, j = ring(name)
            copy_first(name, s, q).wait_recv()
            g, p = at(i, d, 2 + s), at(j, d, 1 + q)
            own[name][g, p] = own[name][g, p] + first[name][s, p]

            @pl.when(s < 2)
            def _(name=name):
                copy_first(name, s + 1, q).start()

            @pl.when(t == 8)
            def _(name=name):
                copy_second(name, 0).start()

        return carry

    lax.fori_loop(0, 12, add_first, 0)
    gain_in[2, 0] = gain_sum(1)
    gain_start(2)

    def add_second(s, carry):
        for name in names:
            f, axis, other, d, i, j = ring(name)
            copy_second(name, s).wait_recv()
            p = at(j, d, 2 + s)
            own[name][i, p] = own[name][i, p] + second[name][s]

            @pl.when(s < 2)
            def _(name=name):
                copy_second(name, s + 1).start()

        return carry

    lax.fori_loop(0, 3, add_second, 0)

    for name in ("gate", "up", "qkv"):
        axis = RINGS[name][0]

        @pl.when(where[axis] != x)
        def _(name=name):
            copy_mirror(name).start()

        @pl.when(where[axis] == x)
        def _(name=name):
            copy_own(name).start()

    for name in ("down", "out"):
        copy_own(name).start()
    for name in ("down", "out"):
        copy_own(name).wait()
    for name in ("gate", "up", "qkv"):
        axis = RINGS[name][0]

        @pl.when(where[axis] != x)
        def _(name=name):
            copy_mirror(name).wait()

        @pl.when(where[axis] == x)
        def _(name=name):
            copy_own(name).wait()

    def hand_small(q, carry):
        for name in names:

            @pl.when(q > 0)
            def _(name=name):
                copy_small(name, q - 1).wait_recv()

            @pl.when(q < 3)
            def _(name=name):
                copy_small(name, q).start()

            copy_big(name, 0, q).start()
        return carry

    lax.fori_loop(0, 4, hand_small, 0)

    def hand_big(t, carry):
        s, q = t // 4, lax.rem(t, 4)
        for name in names:
            copy_big(name, s, q).wait_recv()

            @pl.when(s < 2)
            def _(name=name):
                copy_big(name, s + 1, q).start()

        return carry

    lax.fori_loop(0, 12, hand_big, 0)
    o_gain[...] = gain_sum(2)

    def sent(t, carry):
        s, q = t // 4, lax.rem(t, 4)
        for name in names:
            copy_first(name, s, q).wait_send()
            copy_big(name, s, q).wait_send()
        return carry

    lax.fori_loop(0, 12, sent, 0)

    def sent_small(s, carry):
        for name in names:
            copy_second(name, s).wait_send()
            copy_small(name, s).wait_send()
        return carry

    lax.fori_loop(0, 3, sent_small, 0)


def reduce_grads(n2, nf, dgu, dqkv, att, dbr, hidden, dyf, gains, cid):
    vm = pl.BlockSpec(memory_space=pltpu.VMEM)
    hbm = pl.BlockSpec(memory_space=pl.ANY)
    dma = pltpu.SemaphoreType.DMA
    sizes = list(GRADS.values())
    return pl.pallas_call(
        grad_kernel,
        out_shape=[jax.ShapeDtypeStruct((4, 4) + s, BF) for s in sizes]
        + [jax.ShapeDtypeStruct((8, 384), F32)],
        in_specs=[vm] * 9,
        out_specs=[hbm] * 5 + [vm],
        scratch_shapes=[pltpu.VMEM((4, 4) + s, BF) for s in sizes]
        + [pltpu.VMEM((3, 4) + s, BF) for s in sizes]
        + [pltpu.VMEM((3,) + s, BF) for s in sizes]
        + [
            pltpu.VMEM((3, 4, 8, 384), F32),
            dma((5, 32)),
            dma((5, 32)),
            dma((5,)),
            dma((3, 4)),
            dma((3, 4)),
        ],
        name="reduce_grads",
        compiler_params=pltpu.CompilerParams(
            collective_id=cid, has_side_effects=True, vmem_limit_bytes=60 << 20
        ),
    )(n2, nf, dgu, dqkv, att, dbr, hidden, dyf, gains)


def widen_kernel(w_gate, w_up, w_down, w_qkv, w_out, gate, up, query, key, value, g_out, g_down):
    g_down[...] = w_down[...].astype(F32)
    keys, values = [], []
    for x in range(N_X):
        gate[:, 1024 * x : 1024 * x + 1024] = w_gate[x, 0].astype(F32)
        up[:, 1024 * x : 1024 * x + 1024] = w_up[x, 0].astype(F32)
        g_out[:, 384 * x : 384 * x + 384] = w_out[0, x].astype(F32)
        heads = w_qkv[x, 0].astype(F32)
        query[:, 384 * x : 384 * x + 384] = jnp.concatenate(
            [heads[:, :192], heads[:, 384:576]], axis=1
        )
        keys += [heads[:, 192:288], heads[:, 576:672]]
        values += [heads[:, 288:384], heads[:, 672:768]]
    key[...] = jnp.concatenate(keys, axis=1)
    value[...] = jnp.concatenate(values, axis=1)


def widen(gate, up, down, qkv, out):
    steps = 8

    def spec(r, cols):
        return pl.BlockSpec((r, cols), lambda i: (i, 0))

    def shape(r, cols):
        return jax.ShapeDtypeStruct((r, cols), F32)

    def blocks(cols):
        return pl.BlockSpec((4, 1, 48, cols), lambda i: (0, i // 2, i % 2, 0))

    return pl.pallas_call(
        widen_kernel,
        grid=(steps,),
        out_shape=[
            shape(384, FF),
            shape(384, FF),
            shape(384, 1536),
            shape(384, 768),
            shape(384, 768),
            shape(384, 1536),
            shape(1024, 1536),
        ],
        in_specs=[
            blocks(1024),
            blocks(1024),
            spec(128, 1536),
            blocks(768),
            pl.BlockSpec((1, 4, 48, 384), lambda i: (i // 2, 0, i % 2, 0)),
        ],
        out_specs=[
            spec(48, FF),
            spec(48, FF),
            spec(48, 1536),
            spec(48, 768),
            spec(48, 768),
            spec(48, 1536),
            spec(128, 1536),
        ],
        name="widen",
        compiler_params=pltpu.CompilerParams(vmem_limit_bytes=60 << 20),
    )(gate, up, down.reshape(1024, 1536), qkv, out)


X_GAIN, X_POS, X_IN, X_DY, X_QKV, X_GATE, X_UP, X_SUM1, X_N2, X_SUM2, X_SUM3, X_DBR, X_SUM4 = range(13)
C_POS, C_QKV, C_ATT, C_DATT, C_DQ, C_DKV = range(6)
SCALE = HEAD_SIZE ** (-0.5)


def spread(w, heads):
    blank = jnp.zeros((w.shape[0], 16), w.dtype)
    pieces = []
    for h in heads:
        pieces += [w[:, 96 * h : 96 * h + 48], blank, w[:, 96 * h + 48 : 96 * h + 96], blank]
    return pieces


def as_column(row):
    eye = lax.broadcasted_iota(jnp.int32, (128, 128), 0) == lax.broadcasted_iota(
        jnp.int32, (128, 128), 1
    )
    return jnp.sum(jnp.where(eye, jnp.broadcast_to(row, (128, 128)), 0.0), axis=1, keepdims=True)


def turn(u, cosine, sine):
    return u * cosine + pltpu.roll(u, 64, 1) * sine


def layer_kernel(
    xin,
    dyin,
    positions,
    freq,
    norm_attn,
    norm_mlp,
    wq,
    wk,
    wv,
    wo_in,
    wd_in,
    wg,
    wu,
    out,
    dx,
    nf,
    n2,
    dgu,
    dqkv,
    att,
    dbr,
    hidden,
    dyf,
    ggain,
    wsend,
    wqkv,
    wgf,
    wuf,
    wop,
    wd,
    relay_s,
    xall,
    gains,
    pos,
    gain,
    posx,
    posv,
    posc,
    posr,
    posk,
    cos_c,
    sin_c,
    cos_s,
    sin_s,
    qsend,
    qs,
    vt,
    kt,
    lse,
    osend,
    attp,
    mid,
    gate,
    up,
    own,
    psend,
    prec,
    prec3,
    dsend,
    das,
    dk,
    dv,
    dqs,
    dqp,
    xs,
    xr,
    cs,
    cr,
    ws,
    wr,
    ls,
    go,
):
    section = lax.axis_index("section")
    x = lax.axis_index("fsdp")
    c = lax.axis_index("ctx")
    y, z = lax.rem(c, 4), c // 4
    first, second = section == 0, section == 1
    my_rows = part(128 * x, 128)

    barrier = pltpu.get_barrier_semaphore()
    for k in range(1, 4):
        pl.semaphore_signal(
            barrier, inc=1, device_id={"fsdp": lax.rem(x + k, 4)}, device_id_type=MESH
        )
    for k in range(4):
        pl.semaphore_signal(
            barrier,
            inc=1,
            device_id={"section": 1 - section, "fsdp": lax.rem(x + k, 4)},
            device_id_type=MESH,
        )

    def greet(k, carry):
        pl.semaphore_signal(
            barrier, inc=1, device_id={"ctx": lax.rem(c + k, 16)}, device_id_type=MESH
        )
        return carry

    lax.fori_loop(1, 16, greet, 0)
    pl.semaphore_wait(barrier, 22)

    def ahead(k):
        return lax.rem(x + k, 4)

    def behind(k):
        return lax.rem(x - k + 4, 4)

    def over_x(e, k, src, dst):
        return remote(src, dst, xs.at[e, k], xr.at[e, k], {"fsdp": ahead(k)})

    def over_c(e, to, src, dst):
        k = lax.rem(to - c + 16, 16)
        return remote(src, dst, cs.at[e, k], cr.at[e, k], {"ctx": to})

    def piece(e, i, d, src, dst, flip=False):
        device = {"fsdp": lax.rem(x + d + 4, 4)}
        if flip:
            device["section"] = 1 - section
        return remote(src, dst, xs.at[e, i], xr.at[e, i], device)

    def half(ref, b, n):
        return ref.at[part(128 * b + 64 * n, 64)]

    def gather(e, i, src, ref, flip=False):
        if i == 6:
            return piece(e, 6, 0, src, ref.at[my_rows], True)
        if i >= 4:
            place = half(ref, lax.rem(x + (3 if i == 4 else 1), 4), i - 4)
            return piece(e, i, 1 if i == 4 else -1, place, place)
        n = i % 2
        return piece(e, i, 1 if i < 2 else -1, half(src, 0, n), half(ref, x, n), flip)

    def gather_start(e, src, ref, flip=False):
        for i in (0, 3, 1, 2):
            gather(e, i, src, ref, flip).start()

    def gather_pass(e, src, ref):
        for i, n in ((0, 4), (3, 5)):
            gather(e, i, src, ref).wait_recv()
            gather(e, n, src, ref).start()
        for i in (1, 2):
            gather(e, i, src, ref).wait_recv()

    def gather_far(e, src, ref):
        for i in (4, 5):
            gather(e, i, src, ref).wait_recv()

    def gather_sent(e, src, ref, forwarded=True, started=True, flip=False):
        for i in (0, 1, 2, 3) if started else ():
            gather(e, i, src, ref, flip).wait_send()
        for i in (4, 5) if forwarded else ():
            gather(e, i, src, ref).wait_send()

    def total(e, i):
        n = (X_SUM1, X_SUM2, X_SUM3, X_SUM4).index(e) % 2
        to = (2, 2, 1, 3, 1, 3)[i]
        h = (0, 1, 1, 0, 0, 1)[i]
        src = psend.at[n, lax.rem(x + to, 4), pl.ds(64 * h, 64)]
        if i < 2:
            dst = relay_s.at[n, i]
        else:
            dst = prec.at[n, 0 if to == 1 else 1, pl.ds(64 * h, 64)]
        return piece(e, i, (1, -1, 1, -1, 1, -1)[i], src, dst)

    def total_pass(e):
        n = (X_SUM1, X_SUM2, X_SUM3, X_SUM4).index(e) % 2
        for i in (0, 1):
            total(e, i).wait_recv()
            b, rows = lax.rem(x + (1, 3)[i], 4), slice(64 * i, 64 * i + 64)
            psend[n, b, rows] = psend[n, b, rows] + relay_s[n, i]
            total(e, 4 + i).start()

    def total_take(e):
        n = (X_SUM1, X_SUM2, X_SUM3, X_SUM4).index(e) % 2
        for i in (2, 3, 4, 5):
            total(e, i).wait_recv()
        return own[...] + prec[n, 0].astype(F32) + prec[n, 1].astype(F32)

    def total_sent(e):
        for i in range(6):
            total(e, i).wait_send()

    def quarter(n):
        return (z, y)[n % 2]

    def weight(n, i):
        dst = (wqkv, wqkv, wgf, wuf)[n]
        cols = (pl.ds(0, 512), pl.ds(512, 512), pl.ds(0, 1024), pl.ds(0, 1024))[n]
        q = quarter(n)
        if i < 3:
            to = lax.rem(x + i + 1, 4)
            rows = part(96 * q, 96)
            if n < 2:
                src = wsend.at[to, rows, cols]
            else:
                src = (wg, wu)[n - 2].at[rows, part(1024 * to, 1024)]
            place = dst.at[pl.ds(pl.multiple_of(384 * x + 96 * q, 96), 96), cols]
            device = {"fsdp": to}
        else:
            b = lax.rem(x + 1 + i % 3, 4)
            step = (1, -1, 1, -1)[i // 3 - 1]
            if i < 9:
                rows = pl.ds(pl.multiple_of(384 * b + 96 * q, 96), 96)
            else:
                far, h = lax.rem(q - step + 4, 4), i // 3 - 3
                rows = pl.ds(pl.multiple_of(384 * b + 96 * far + 48 * h, 48), 48)
            src = place = dst.at[rows, cols]
            r = lax.rem(q + step + 4, 4)
            device = {"ctx": 4 * r + y if n % 2 == 0 else 4 * z + r}
        return remote(src, place, ws.at[n, i], wr.at[n, i], device)

    def weight_each(which, items, act):
        for i in items:
            for n in which:
                act(weight(n, i))

    def begin(copy):
        copy.start()

    def arrive(copy):
        copy.wait_recv()

    def leave(copy):
        copy.wait_send()

    def weight_fetch(which):
        weight_each(which, (1, 0, 2), begin)

    def weight_share(which):
        weight_each(which, range(3), arrive)
        weight_each(which, range(3, 9), begin)

    def weight_pass(which):
        for k in range(3):
            weight_each(which, (3 + k,), arrive)
            weight_each(which, (9 + k,), begin)
        for k in range(3):
            weight_each(which, (6 + k,), arrive)
            weight_each(which, (12 + k,), begin)

    def weight_wait(which):
        weight_each(which, range(9, 15), arrive)

    heads, wide = (0, 1), (2, 3)

    def gain_copy(k):
        return over_x(X_GAIN, k, gains, gain.at[:, part(384 * x, 384)])

    def pos_copy(k):
        return over_x(X_POS, k, pos, posx.at[x])

    pos[...] = jnp.broadcast_to(
        jnp.concatenate([positions[0:1, :], positions[1:2, :]], axis=1).astype(F32), (8, 128)
    )
    gains[...] = jnp.broadcast_to(norm_attn[...].astype(F32), (8, 384))
    gains[1:2, :] = norm_mlp[...].astype(F32)
    for k in (2, 1, 3):
        pos_copy(k).start()
        gain_copy(k).start()
    gain[:, part(384 * x, 384)] = gains[...]
    posx[x] = pos[...]

    @pl.when(first)
    def _():
        gather_start(X_IN, xin, xall)
        xall[my_rows, :] = xin[...]

    def local_copies():
        yield pltpu.make_async_copy(
            wg.at[:, part(1024 * x, 1024)], wgf.at[part(384 * x, 384)], ls.at[0]
        )
        yield pltpu.make_async_copy(
            wu.at[:, part(1024 * x, 1024)], wuf.at[part(384 * x, 384)], ls.at[1]
        )
        yield pltpu.make_async_copy(wd_in, wd, ls.at[2])
        for h in range(4):
            yield pltpu.make_async_copy(
                wo_in.at[pl.ds(96 * h, 96)], wop.at[pl.ds(128 * h, 96)], ls.at[3 + h]
            )

    for b in range(4):
        pieces = []
        for j in range(2):
            pieces += spread(wq[:, 384 * b + 192 * j : 384 * b + 192 * j + 192], (0, 1))
            pieces += spread(wk[:, 96 * (2 * b + j) : 96 * (2 * b + j) + 96], (0,))
            pieces += [
                wv[:, 96 * (2 * b + j) : 96 * (2 * b + j) + 96],
                jnp.zeros((384, 32), BF),
            ]
        wsend[b] = jnp.concatenate(pieces, axis=1)

    @pl.when(first)
    def _():
        weight_fetch(heads)

    for copy in local_copies():
        copy.start()
    wqkv[part(384 * x, 384), :] = wsend[x]
    for h in range(4):
        wop[128 * h + 96 : 128 * h + 128, :] = jnp.zeros((32, WIDTH), BF)

    lane = lax.broadcasted_iota(jnp.int32, (1, 128), 1)
    sign = jnp.where(lane < 64, -1.0, 1.0)
    for k in (1, 3, 2):
        pos_copy(k).wait()
    for b in range(4):
        block = posx[b]
        posv[b, 0] = block
        posv[b, 1] = pltpu.roll(block, 64, 1)

    def pos_to(to):
        return over_c(C_POS, to, posv.at[to // 4, lax.rem(to, 4) // 2], posc.at[c])

    def send_pos(k, carry):
        pos_to(lax.rem(c + k, 16)).start()
        return carry

    lax.fori_loop(1, 16, send_pos, 0)
    posc[c] = posv[c // 4, lax.rem(c, 4) // 2]
    for b in range(4):
        angle = as_column(posx[b][0:1, :]) * freq[0:1, :]
        cos_c[128 * b : 128 * b + 128, :] = jnp.cos(angle)
        sin_c[128 * b : 128 * b + 128, :] = jnp.sin(angle) * sign

    def await_pos(k, carry):
        pos_to(lax.rem(c + k, 16)).wait()
        return carry

    lax.fori_loop(1, 16, await_pos, 0)

    def tables(i, carry):
        row = jnp.where(lane < 64, posc[2 * i][0:1, :], pltpu.roll(posc[2 * i + 1], 64, 1)[0:1, :])
        block = part(128 * i, 128)
        posr[0:1, block] = row
        column = as_column(row)
        posk[block, :] = jnp.broadcast_to(column, (128, 128))
        angle = column * freq[0:1, :]
        cos_s[block, :] = jnp.cos(angle)
        sin_s[block, :] = jnp.sin(angle) * sign
        return carry

    @pl.when(first)
    def _():
        weight_share(heads)
        weight_fetch(wide)

    lax.fori_loop(0, 8, tables, 0)
    for k in (1, 3, 2):
        gain_copy(k).wait()

    @pl.when(first)
    def _():
        weight_pass(heads)
        gather_pass(X_IN, xin, xall)
        gather_far(X_IN, xin, xall)
        weight_wait(heads)
        pl.semaphore_signal(go, inc=1, device_id={"section": 1}, device_id_type=MESH)

    @pl.when(second)
    def _():
        gather_start(X_DY, dyin, dyf)
        dyf[my_rows, :] = dyin[...]
        gather_pass(X_DY, dyin, dyf)
        pl.semaphore_wait(go, 1)
        weight_fetch(heads + wide)
        weight_share(heads + wide)
        weight_pass(heads + wide)
        weight_wait(heads + wide)

    gain_attn, gain_mlp = gain[0:1, :], gain[1:2, :]

    def to_pair(ref, e, b, i, width, dst):
        src = ref.at[part(128 * b + 64 * (i // 2), 64), pl.ds(width * (i % 2), width)]
        return over_c(e, 4 * b + i, src, dst.at[part(64 * c, 64)])

    def in_order(n):
        return behind(jnp.where(n == 2, 3, jnp.where(n == 3, 2, n)))

    def project(n, carry):
        b = in_order(n)
        rows = part(128 * b, 128)

        @pl.when(jnp.logical_and(second, n == 0))
        def _():
            gather(X_IN, 6, out, xall).wait_recv()

        @pl.when(jnp.logical_and(second, n == 1))
        def _():
            gather_pass(X_IN, xin, xall)

        @pl.when(jnp.logical_and(second, n == 3))
        def _():
            gather_far(X_IN, xin, xall)

        value = xall[rows, :].astype(F32)
        normed = (
            value
            * lax.rsqrt(jnp.mean(value * value, axis=-1, keepdims=True) + EPSILON)
            * gain_attn
        ).astype(BF)
        nf[rows, :] = normed
        u = mm(normed, wqkv[...])
        cosine, sine = cos_c[rows, :], sin_c[rows, :]
        for h in range(8):
            head = u[:, 128 * h : 128 * h + 128]
            if h % 4 != 3:
                head = turn(head, cosine, sine)
            qsend[rows, 128 * h : 128 * h + 128] = head.astype(BF)
        for i in range(4):

            @pl.when(4 * b + i != c)
            def _(i=i):
                to_pair(qsend, C_QKV, b, i, 512, qs).start()

            @pl.when(4 * b + i == c)
            def _(i=i):
                qs[part(64 * c, 64), :] = qsend[
                    part(128 * b + 64 * (i // 2), 64), 512 * (i % 2) : 512 * (i % 2) + 512
                ]

        return carry

    lax.fori_loop(0, 4, project, 0)

    @pl.when(first)
    def _():
        weight_share(wide)


    def await_qkv(k, carry):
        place = qs.at[part(64 * lax.rem(c - k + 16, 16), 64)]
        over_c(C_QKV, lax.rem(c + k, 16), place, place).wait_recv()
        return carry

    lax.fori_loop(1, 16, await_qkv, 0)

    vt[...] = qs[:, 384:512].T
    kt[...] = qs[:, 256:384].T

    def masked(q, cols):
        st = mm_nt(qs[:, 256:384], q) * SCALE
        return jnp.where(posk[:, 0:1] <= posr[0:1, cols], st, -1e30)

    def att_place():
        return attp.at[part(64 * (c // 2), 64), part(256 * lax.rem(c, 2), 256)]

    def att_to(to):
        return over_c(C_ATT, to, osend.at[part(64 * to, 64)], att_place())

    def attend(n, carry):
        rows = part(256 * n, 256)

        for g in range(2):
            st = masked(qs[rows, 128 * g : 128 * g + 128], rows)
            top = jnp.max(st, axis=0, keepdims=True)
            e = jnp.exp(st - top)
            total = jnp.sum(e, axis=0, keepdims=True)
            lse[g : g + 1, rows] = top + jnp.log(total)
            pt = (e * (1.0 / total)).astype(BF)
            osend[rows, 128 * g : 128 * g + 128] = mm(vt[...], pt).T.astype(BF)
        for i in range(4):
            to = 4 * n + i

            @pl.when(to != c)
            def _(to=to):
                att_to(to).start()

            @pl.when(to == c)
            def _(to=to):
                attp[part(64 * (c // 2), 64), part(256 * lax.rem(c, 2), 256)] = osend[
                    part(64 * to, 64), :
                ]

        return carry

    lax.fori_loop(0, 4, attend, 0)

    def await_att(b):
        for i in range(4):
            to = 4 * b + i

            @pl.when(to != c)
            def _(to=to, i=i):
                k = lax.rem(c - to + 16, 16)
                place = attp.at[part(64 * (2 * b + i // 2), 64), pl.ds(256 * (i % 2), 256)]
                remote(place, place, cs.at[C_ATT, k], cr.at[C_ATT, k], {"ctx": lax.rem(c + k, 16)}).wait_recv()

    def give(e, n, b, value):
        place = psend.at[(X_SUM1, X_SUM2, X_SUM3, X_SUM4).index(e) % 2, b]

        @pl.when(n < 3)
        def _():
            place[...] = value.astype(BF)

        @pl.when(n == 0)
        def _():
            total(e, 0).start()
            total(e, 1).start()

        @pl.when(n == 1)
        def _():
            total(e, 2).start()

        @pl.when(n == 2)
        def _():
            total(e, 3).start()
            total_pass(e)

        @pl.when(n == 3)
        def _():
            own[...] = value

    def far_first(n):
        return lax.rem(x + jnp.where(n == 0, 2, jnp.where(n == 1, 1, jnp.where(n == 2, 3, 0))), 4)

    def combine(n, carry):
        b = far_first(n)
        await_att(b)
        give(X_SUM1, n, b, mm(attp[part(128 * b, 128), :], wop[...]))
        return carry

    @pl.when(first)
    def _():
        weight_pass(wide)

    for copy in local_copies():
        copy.wait()
    lax.fori_loop(0, 4, combine, 0)
    middle = xall[my_rows, :].astype(F32) + total_take(X_SUM1)
    mid[...] = middle
    n2[my_rows, :] = (
        middle * lax.rsqrt(jnp.mean(middle * middle, axis=-1, keepdims=True) + EPSILON) * gain_mlp
    ).astype(BF)
    n2_own = n2.at[my_rows]
    gather_start(X_N2, n2_own, n2)

    @pl.when(first)
    def _():
        weight_wait(wide)

    def pair(blocks, ref):
        return jnp.concatenate([ref[part(128 * b, 128), :] for b in blocks], axis=0)

    def far_copy(d, b):
        return piece(X_SUM2, d, d, psend.at[1, b], prec3.at[d - 1])

    def feed(ds):
        blocks = [lax.rem(x + d, 4) for d in ds]
        a = pair(blocks, n2)
        ga, u = mm(a, wgf[...]), mm(a, wuf[...])
        h = (ga * (1.0 / (1.0 + jnp.exp(-ga))) * u).astype(BF)
        result = mm(h, wd[...])
        for n, (d, b) in enumerate(zip(ds, blocks)):
            rows, cut = part(128 * b, 128), slice(128 * n, 128 * n + 128)
            gate[rows, :] = ga[cut]
            up[rows, :] = u[cut]
            hidden[rows, :] = h[cut]
            if d == 0:
                own[...] = result[cut]
            else:
                psend[1, b] = result[cut].astype(BF)
                far_copy(d, b).start()

    gather_pass(X_N2, n2_own, n2)
    feed((1, 3))
    gather_far(X_N2, n2_own, n2)
    feed((2, 0))
    result = mid[...] + own[...]
    for d in (1, 3, 2):
        far_copy(d, lax.rem(x + d, 4)).wait_recv()
        result = result + prec3[d - 1].astype(F32)
    out[...] = result.astype(BF)

    @pl.when(first)
    def _():
        gather_sent(X_IN, xin, xall, forwarded=False)
        gather(X_IN, 6, out, xall).start()
        gather_start(X_IN, out, xall, True)

    @pl.when(first)
    def _():
        gather_pass(X_DY, dx, dyf)
        gather(X_DY, 6, dx, dyf).wait_recv()

    gather_far(X_DY, dx, dyf)

    def feed_back(ds):
        blocks = [lax.rem(x + d, 4) for d in ds]
        dh = mm_nt(pair(blocks, dyf), wd[...])
        ga, u = pair(blocks, gate), pair(blocks, up)
        s = 1.0 / (1.0 + jnp.exp(-ga))
        dga = (dh * u * (s * (1.0 + ga * (1.0 - s)))).astype(BF)
        du = (dh * (ga * s)).astype(BF)
        result = mm_nt(dga, wgf[...]) + mm_nt(du, wuf[...])
        for n, (d, b) in enumerate(zip(ds, blocks)):
            rows, cut = part(128 * b, 128), slice(128 * n, 128 * n + 128)
            dgu[rows, 0:1024] = dga[cut]
            dgu[rows, 1024:2048] = du[cut]
            if d == 0:
                own[...] = result[cut]
            else:
                psend[0, b] = result[cut].astype(BF)
                for i in {2: (0, 1), 1: (2,), 3: (3,)}[d]:
                    total(X_SUM3, i).start()

    total_sent(X_SUM1)
    feed_back((2, 1))
    feed_back((3, 0))
    total_pass(X_SUM3)

    def norm_back(value, grad, gain_row):
        r = lax.rsqrt(jnp.mean(value * value, axis=-1, keepdims=True) + EPSILON)
        unit = value * r
        t = grad * gain_row
        back = r * (t - unit * jnp.mean(t * unit, axis=-1, keepdims=True))
        return back, jnp.sum(grad * unit, axis=0, keepdims=True)

    back, g_mlp = norm_back(mid[...], total_take(X_SUM3), gain_mlp)
    dmid = dyf[my_rows, :].astype(F32) + back
    mid[...] = dmid
    ggain[...] = jnp.zeros_like(ggain)
    ggain[1:2, :] = g_mlp
    dbr[my_rows, :] = dmid.astype(BF)
    dbr_own = dbr.at[my_rows]
    gather_start(X_DBR, dbr_own, dbr)

    def branch(n, carry):
        b = in_order(n)
        rows = part(128 * b, 128)

        @pl.when(n == 1)
        def _():
            gather_pass(X_DBR, dbr_own, dbr)

        @pl.when(n == 3)
        def _():
            gather_far(X_DBR, dbr_own, dbr)

        dsend[rows, :] = mm_nt(dbr[rows, :], wop[...]).astype(BF)
        for i in range(4):

            @pl.when(4 * b + i != c)
            def _(i=i):
                to_pair(dsend, C_DATT, b, i, 256, das).start()

            @pl.when(4 * b + i == c)
            def _(i=i):
                das[part(64 * c, 64), :] = dsend[
                    part(128 * b + 64 * (i // 2), 64), 256 * (i % 2) : 256 * (i % 2) + 256
                ]

        return carry

    lax.fori_loop(0, 4, branch, 0)

    def await_das(k, carry):
        place = das.at[part(64 * lax.rem(c - k + 16, 16), 64)]
        over_c(C_DATT, lax.rem(c + k, 16), place, place).wait_recv()
        return carry

    lax.fori_loop(1, 16, await_das, 0)
    dk[...] = jnp.zeros_like(dk)
    dv[...] = jnp.zeros_like(dv)

    def grad_place(h):
        return dqp.at[part(64 * (c // 2), 64), part(512 * lax.rem(c, 2) + 256 * h, 256)]

    def grad_to(e, to):
        h = e - C_DQ
        return over_c(e, to, dqs.at[part(64 * to, 64), pl.ds(256 * h, 256)], grad_place(h))

    def attend_back(n, carry):
        rows = part(256 * n, 256)
        for g in range(2):
            cols = slice(128 * g, 128 * g + 128)
            q, da = qs[rows, cols], das[rows, cols]
            p = jnp.exp(masked(q, rows) - lse[g : g + 1, rows])
            dp = mm_nt(qs[:, 384:512], da)
            dv[...] += mm(p.astype(BF), da)
            ds = (p * (dp - jnp.sum(p * dp, axis=0, keepdims=True))).astype(BF)
            dk[...] += mm(ds, q)
            dq = mm(kt[...], ds).T * SCALE
            dqs[rows, cols] = turn(dq, cos_s[rows, :], -sin_s[rows, :]).astype(BF)
        for i in range(4):
            to = 4 * n + i

            @pl.when(to != c)
            def _(to=to):
                grad_to(C_DQ, to).start()

            @pl.when(to == c)
            def _(to=to):
                grad_place(0)[...] = dqs[part(64 * to, 64), 0:256]

        return carry

    lax.fori_loop(0, 4, attend_back, 0)
    dqs[:, 256:384] = turn(dk[...] * SCALE, cos_s[...], -sin_s[...]).astype(BF)
    dqs[:, 384:512] = dv[...].astype(BF)

    def send_dkv(k, carry):
        grad_to(C_DKV, lax.rem(c + k, 16)).start()
        return carry

    lax.fori_loop(1, 16, send_dkv, 0)
    grad_place(1)[...] = dqs[part(64 * c, 64), 256:512]

    def await_dqkv(b):
        for i in range(4):
            to = 4 * b + i

            @pl.when(to != c)
            def _(to=to, i=i):
                k = lax.rem(c - to + 16, 16)
                for h in range(2):
                    place = dqp.at[
                        part(64 * (2 * b + i // 2), 64), pl.ds(512 * (i % 2) + 256 * h, 256)
                    ]
                    e = C_DQ + h
                    remote(
                        place, place, cs.at[e, k], cr.at[e, k], {"ctx": lax.rem(c + k, 16)}
                    ).wait_recv()

    for d in (1, 2, 3):
        far_copy(d, lax.rem(x + d, 4)).wait_send()

    def input_grad(n, carry):
        b = far_first(n)
        await_dqkv(b)
        give(X_SUM4, n, b, mm_nt(dqp[part(128 * b, 128), :], wqkv[...]))
        return carry

    lax.fori_loop(0, 4, input_grad, 0)
    back, g_attn = norm_back(xall[my_rows, :].astype(F32), total_take(X_SUM4), gain_attn)
    dx[...] = (mid[...] + back).astype(BF)
    ggain[0:1, :] = g_attn

    @pl.when(second)
    def _():
        gather_sent(X_DY, dyin, dyf, forwarded=False)
        gather(X_DY, 6, dx, dyf).start()
        gather_start(X_DY, dx, dyf, True)

    for n in range(2):
        rows = slice(256 * n, 256 * n + 256)
        att[rows, :] = jnp.concatenate(
            [attp[rows, 128 * h : 128 * h + 96] for h in range(4)], axis=1
        )
        pieces = []
        for h in range(8):
            if h % 4 == 3:
                pieces.append(dqp[rows, 128 * h : 128 * h + 96])
            else:
                pieces.append(dqp[rows, 128 * h : 128 * h + 48])
                pieces.append(dqp[rows, 128 * h + 64 : 128 * h + 112])
        dqkv[rows, :] = jnp.concatenate(pieces, axis=1)

    def sent_c(k, carry):
        to = lax.rem(c + k, 16)
        place = qs.at[part(64 * to, 64)]
        over_c(C_QKV, to, place, place).wait_send()
        att_to(to).wait_send()
        place = das.at[part(64 * to, 64)]
        over_c(C_DATT, to, place, place).wait_send()
        grad_to(C_DQ, to).wait_send()
        grad_to(C_DKV, to).wait_send()
        return carry

    lax.fori_loop(1, 16, sent_c, 0)
    total_sent(X_SUM3)
    total_sent(X_SUM4)
    weight_each(heads + wide, range(15), leave)
    gather_sent(X_N2, n2_own, n2)
    gather_sent(X_DBR, dbr_own, dbr)
    gather_sent(X_IN, xin, xall, started=False)
    gather_sent(X_DY, dyin, dyf, started=False)

    @pl.when(first)
    def _():
        gather_sent(X_IN, xin, xall, forwarded=False)
        gather(X_IN, 6, out, xall).wait_send()

    @pl.when(second)
    def _():
        gather_sent(X_DY, dyin, dyf, forwarded=False)
        gather(X_DY, 6, dx, dyf).wait_send()


def run_layer(xin, dyin, positions, freq, norm_attn, norm_mlp, wq, wk, wv, wo, wd, wg, wu, cid):
    vm = pl.BlockSpec(memory_space=pltpu.VMEM)
    hbm = pl.BlockSpec(memory_space=pl.ANY)
    dma = pltpu.SemaphoreType.DMA
    shapes = [
        ((128, WIDTH), BF),
        ((128, WIDTH), BF),
        ((512, WIDTH), BF),
        ((512, WIDTH), BF),
        ((512, 2048), BF),
        ((512, 768), BF),
        ((512, 384), BF),
        ((512, WIDTH), BF),
        ((512, 1024), BF),
        ((512, WIDTH), BF),
        ((8, WIDTH), F32),
    ]
    scratch = [
        ((4, 384, 1024), BF),
        ((WIDTH, 1024), BF),
        ((WIDTH, 1024), BF),
        ((WIDTH, 1024), BF),
        ((512, WIDTH), BF),
        ((1024, WIDTH), BF),
        ((2, 2, 64, WIDTH), BF),
        ((512, WIDTH), BF),
        ((8, 384), F32),
        ((8, 128), F32),
        ((8, WIDTH), F32),
        ((4, 8, 128), F32),
        ((4, 2, 8, 128), F32),
        ((16, 8, 128), F32),
        ((8, 1024), F32),
        ((1024, 128), F32),
        ((512, 128), F32),
        ((512, 128), F32),
        ((1024, 128), F32),
        ((1024, 128), F32),
        ((512, 1024), BF),
        ((1024, 512), BF),
        ((128, 1024), BF),
        ((128, 1024), BF),
        ((8, 1024), F32),
        ((1024, 256), BF),
        ((512, 512), BF),
        ((128, WIDTH), F32),
        ((512, 1024), F32),
        ((512, 1024), F32),
        ((128, WIDTH), F32),
        ((2, 4, 128, WIDTH), BF),
        ((2, 2, 128, WIDTH), BF),
        ((3, 128, WIDTH), BF),
        ((512, 512), BF),
        ((1024, 256), BF),
        ((1024, 128), F32),
        ((1024, 128), F32),
        ((1024, 512), BF),
        ((512, 1024), BF),
    ]
    return pl.pallas_call(
        layer_kernel,
        out_shape=[jax.ShapeDtypeStruct(s, d) for s, d in shapes],
        in_specs=[vm] * 9 + [hbm] * 4,
        out_specs=[vm] * len(shapes),
        scratch_shapes=[pltpu.VMEM(s, d) for s, d in scratch]
        + [dma((13, 7)), dma((13, 7)), dma((6, 16)), dma((6, 16)), dma((4, 15)), dma((4, 15)), dma((7,)), pltpu.SemaphoreType.REGULAR],
        name="layer",
        compiler_params=pltpu.CompilerParams(
            collective_id=cid, has_side_effects=True, vmem_limit_bytes=63 << 20
        ),
    )(xin, dyin, positions, freq, norm_attn, norm_mlp, wq, wk, wv, wo, wd, wg, wu)


def local(
    inputs,
    positions,
    out_grad,
    norm_attn,
    w_query,
    key_weight,
    value_weight,
    output_weight,
    norm_mlp,
    w_gate,
    w_up,
    w_down,
):
    lane = np.arange(128)
    index = np.where(lane < 64, lane, lane - 64)
    freq = np.where(index < 48, THETA ** (-2.0 * index / HEAD_SIZE), 0.0).astype(np.float32)
    freq = jnp.asarray(np.broadcast_to(freq[None], (8, 128)))
    out, dx, nf, n2, dgu, dqkv, att, dbr, hidden, dyf, ggain = run_layer(
        inputs.reshape(128, WIDTH),
        out_grad.reshape(128, WIDTH),
        positions,
        freq,
        norm_attn,
        norm_mlp,
        w_query[0],
        key_weight[0],
        value_weight[0],
        output_weight[0],
        w_down[0],
        w_gate[0],
        w_up[0],
        0,
    )
    *summed, g_gain = reduce_grads(n2, nf, dgu, dqkv, att, dbr, hidden, dyf, ggain, 1)
    g_gate, g_up, g_query, g_key, g_value, g_out, g_down = widen(*summed)
    return (
        out.reshape(1, 2, 64, WIDTH),
        dx.reshape(1, 2, 64, WIDTH),
        g_gain[0:1],
        g_query[None],
        g_key[None],
        g_value[None],
        g_out[None],
        g_gain[1:2],
        g_gate[None],
        g_up[None],
        g_down[None],
    )


def solution(mesh):
    rows = P("section", "fsdp", None)
    return jax.shard_map(
        local,
        mesh=mesh,
        in_specs=(
            P("fsdp", "ctx", None),
            P("fsdp", "ctx"),
            P("fsdp", "ctx", None),
            P("section", "fsdp"),
            rows,
            rows,
            rows,
            rows,
            P("section", "fsdp"),
            rows,
            rows,
            rows,
        ),
        out_specs=(
            P("section", "fsdp", "ctx", None),
            P("section", "fsdp", "ctx", None),
            P("section", "fsdp"),
            rows,
            rows,
            rows,
            rows,
            P("section", "fsdp"),
            rows,
            rows,
            rows,
        ),
        check_vma=False,
    )
```

```python
import jax
import jax.numpy as jnp
import numpy as np
from jax import lax
from jax.experimental import pallas as pl
from jax.experimental.pallas import tpu as pltpu
from jax.sharding import PartitionSpec as P

QUERY_HEADS = 16
KEY_VALUE_HEADS = 8
HEAD_SIZE = 96
WIDTH = 1536
FF = 4096
THETA = 100000.0
EPSILON = 1e-05
MESH = pl.DeviceIdType.MESH
N_X = 4
N_C = 16
BF = jnp.bfloat16
F32 = jnp.float32


def mm(a, b):
    return jnp.dot(a, b, preferred_element_type=F32)


def mm_tn(a, b):
    return lax.dot_general(a, b, (((0,), (0,)), ((), ())), preferred_element_type=F32)


def mm_nt(a, b):
    return lax.dot_general(a, b, (((1,), (1,)), ((), ())), preferred_element_type=F32)


def remote(src, dst, send, recv, device):
    return pltpu.make_async_remote_copy(
        src_ref=src, dst_ref=dst, send_sem=send, recv_sem=recv, device_id=device, device_id_type=MESH
    )


def part(start, size):
    return pl.ds(pl.multiple_of(start, size), size)


def widen_kernel(w_gate, w_up, w_down, w_out, w_a, w_b, gains, gate, up, query, key, value, g_out, g_down, g_attn, g_mlp):
    g_attn[...] = gains[0:1, :]
    g_mlp[...] = gains[1:2, :]
    g_down[...] = w_down[...].astype(F32)
    keys, values = [], []
    for x in range(N_X):
        gate[:, 1024 * x : 1024 * x + 1024] = w_gate[x, 0].astype(F32)
        up[:, 1024 * x : 1024 * x + 1024] = w_up[x, 0].astype(F32)
        g_out[:, 384 * x : 384 * x + 384] = w_out[0, x].astype(F32)
        a, b = w_a[x, 0].astype(F32), w_b[x, 0].astype(F32)
        query[:, 384 * x : 384 * x + 384] = jnp.concatenate([a[:, :192], b[:, :192]], axis=1)
        keys += [a[:, 192:288], b[:, 192:288]]
        values += [a[:, 288:], b[:, 288:]]
    key[...] = jnp.concatenate(keys, axis=1)
    value[...] = jnp.concatenate(values, axis=1)


def widen(gate, up, down, out, heads_a, heads_b, gains):
    steps = 8

    def spec(r, cols):
        return pl.BlockSpec((r, cols), lambda i: (i, 0))

    def shape(r, cols):
        return jax.ShapeDtypeStruct((r, cols), F32)

    def blocks(cols):
        return pl.BlockSpec((4, 1, 48, cols), lambda i: (0, i // 2, i % 2, 0))

    return pl.pallas_call(
        widen_kernel,
        grid=(steps,),
        out_shape=[
            shape(384, FF),
            shape(384, FF),
            shape(384, 1536),
            shape(384, 768),
            shape(384, 768),
            shape(384, 1536),
            shape(1024, 1536),
            shape(1, 384),
            shape(1, 384),
        ],
        in_specs=[
            blocks(1024),
            blocks(1024),
            spec(128, 1536),
            pl.BlockSpec((1, 4, 48, 384), lambda i: (i // 2, 0, i % 2, 0)),
            blocks(384),
            blocks(384),
            pl.BlockSpec((8, 384), lambda i: (0, 0)),
        ],
        out_specs=[
            spec(48, FF),
            spec(48, FF),
            spec(48, 1536),
            spec(48, 768),
            spec(48, 768),
            spec(48, 1536),
            spec(128, 1536),
            pl.BlockSpec((1, 384), lambda i: (0, 0)),
            pl.BlockSpec((1, 384), lambda i: (0, 0)),
        ],
        name="widen",
        compiler_params=pltpu.CompilerParams(vmem_limit_bytes=60 << 20),
    )(gate, up, down.reshape(1024, 1536), out, heads_a, heads_b, gains)


X_GAIN, X_POS, X_IN, X_DY, X_QKV, X_GATE, X_UP, X_SUM1, X_N2, X_SUM2, X_SUM3, X_DBR, X_SUM4 = range(13)
C_POS, C_QKV, C_ATT, C_DATT, C_DQ, C_DKV = range(6)
SCALE = HEAD_SIZE ** (-0.5)
FLOWS = {
    "gate": ("y", 1, 96, 1024),
    "up": ("y", -1, 96, 1024),
    "down": ("z", 1, 64, 1536),
    "out": ("z", -1, 96, 384),
    "heads_a": ("y", 1, 96, 384),
    "heads_b": ("z", -1, 96, 384),
}
NAMES = list(FLOWS)
EARLY, LATE = NAMES[:4], NAMES[4:]
SMALL = NAMES[3:]


def spread(w, heads):
    blank = jnp.zeros((w.shape[0], 16), w.dtype)
    pieces = []
    for h in heads:
        pieces += [w[:, 96 * h : 96 * h + 48], blank, w[:, 96 * h + 48 : 96 * h + 96], blank]
    return pieces


def as_column(row):
    eye = lax.broadcasted_iota(jnp.int32, (128, 128), 0) == lax.broadcasted_iota(
        jnp.int32, (128, 128), 1
    )
    return jnp.sum(jnp.where(eye, jnp.broadcast_to(row, (128, 128)), 0.0), axis=1, keepdims=True)


def turn(u, cosine, sine):
    return u * cosine + pltpu.roll(u, 64, 1) * sine


def layer_kernel(
    xin,
    dyin,
    positions,
    freq,
    norm_attn,
    norm_mlp,
    wq,
    wk,
    wv,
    wo_in,
    wd_in,
    wg,
    wu,
    out,
    dx,
    h_gate,
    h_up,
    h_down,
    h_out,
    h_heads_a,
    h_heads_b,
    o_gain,
    nf,
    rows2,
    dgu,
    dqkv,
    att,
    dbr,
    hidden,
    ggain,
    arrive_down,
    arrive_out,
    arrive_a,
    arrive_b,
    second_out,
    second_a,
    second_b,
    gain_in,
    wsend,
    wqkv,
    wgf,
    wuf,
    wop,
    wd,
    relay_s,
    xall,
    gains,
    pos,
    gain,
    posx,
    posv,
    posc,
    posr,
    posk,
    cos_c,
    sin_c,
    cos_s,
    sin_s,
    qsend,
    qs,
    vt,
    kt,
    lse,
    osend,
    attp,
    mid,
    gate,
    up,
    own,
    psend,
    prec,
    prec3,
    dsend,
    das,
    dk,
    dv,
    dqs,
    dqp,
    xs,
    xr,
    cs,
    cr,
    ws,
    wr,
    ls,
    go,
    fs,
    fr,
    gs,
    gr,
    os,
):
    section = lax.axis_index("section")
    x = lax.axis_index("fsdp")
    c = lax.axis_index("ctx")
    y, z = lax.rem(c, 4), c // 4
    first, second = section == 0, section == 1
    my_rows = part(128 * x, 128)
    n2, dyf = rows2.at[0], rows2.at[1]
    where = {"x": x, "y": y, "z": z}

    def near(axis, step):
        if axis == "x":
            return {"fsdp": lax.rem(x + step + 4, 4)}
        if axis == "y":
            return {"ctx": 4 * z + lax.rem(y + step + 4, 4)}
        return {"ctx": 4 * lax.rem(z + step + 4, 4) + y}

    mirror = {"y": {"fsdp": y, "ctx": 4 * z + x}, "z": {"fsdp": z, "ctx": 4 * x + y}}

    barrier = pltpu.get_barrier_semaphore()
    for k in range(1, 4):
        pl.semaphore_signal(
            barrier, inc=1, device_id={"fsdp": lax.rem(x + k, 4)}, device_id_type=MESH
        )
    for k in range(4):
        pl.semaphore_signal(
            barrier,
            inc=1,
            device_id={"section": 1 - section, "fsdp": lax.rem(x + k, 4)},
            device_id_type=MESH,
        )

    def greet(k, carry):
        pl.semaphore_signal(
            barrier, inc=1, device_id={"ctx": lax.rem(c + k, 16)}, device_id_type=MESH
        )
        return carry

    lax.fori_loop(1, 16, greet, 0)
    for axis in "yz":
        pl.semaphore_signal(barrier, inc=1, device_id=mirror[axis], device_id_type=MESH)
    pl.semaphore_wait(barrier, 24)

    def ahead(k):
        return lax.rem(x + k, 4)

    def behind(k):
        return lax.rem(x - k + 4, 4)

    def over_x(e, k, src, dst):
        return remote(src, dst, xs.at[e, k], xr.at[e, k], {"fsdp": ahead(k)})

    def over_c(e, to, src, dst):
        k = lax.rem(to - c + 16, 16)
        return remote(src, dst, cs.at[e, k], cr.at[e, k], {"ctx": to})

    def piece(e, i, d, src, dst, flip=False):
        device = {"fsdp": lax.rem(x + d + 4, 4)}
        if flip:
            device["section"] = 1 - section
        return remote(src, dst, xs.at[e, i], xr.at[e, i], device)

    def half(ref, b, n):
        return ref.at[part(128 * b + 64 * n, 64)]

    def gather(e, i, src, ref, flip=False):
        if i == 6:
            return piece(e, 6, 0, src, ref.at[my_rows], True)
        if i >= 4:
            place = half(ref, lax.rem(x + (3 if i == 4 else 1), 4), i - 4)
            return piece(e, i, 1 if i == 4 else -1, place, place)
        n = i % 2
        return piece(e, i, 1 if i < 2 else -1, half(src, 0, n), half(ref, x, n), flip)

    def gather_start(e, src, ref, flip=False):
        for i in (0, 3, 1, 2):
            gather(e, i, src, ref, flip).start()

    def gather_pass(e, src, ref):
        for i, n in ((0, 4), (3, 5)):
            gather(e, i, src, ref).wait_recv()
            gather(e, n, src, ref).start()
        for i in (1, 2):
            gather(e, i, src, ref).wait_recv()

    def gather_far(e, src, ref):
        for i in (4, 5):
            gather(e, i, src, ref).wait_recv()

    def gather_sent(e, src, ref, forwarded=True, started=True, flip=False):
        for i in (0, 1, 2, 3) if started else ():
            gather(e, i, src, ref, flip).wait_send()
        for i in (4, 5) if forwarded else ():
            gather(e, i, src, ref).wait_send()

    def total(e, i):
        n = (X_SUM1, X_SUM2, X_SUM3, X_SUM4).index(e) % 2
        to = (2, 2, 1, 3, 1, 3)[i]
        h = (0, 1, 1, 0, 0, 1)[i]
        src = psend.at[n, lax.rem(x + to, 4), pl.ds(64 * h, 64)]
        if i < 2:
            dst = relay_s.at[n, i]
        else:
            dst = prec.at[n, 0 if to == 1 else 1, pl.ds(64 * h, 64)]
        return piece(e, i, (1, -1, 1, -1, 1, -1)[i], src, dst)

    def total_pass(e):
        n = (X_SUM1, X_SUM2, X_SUM3, X_SUM4).index(e) % 2
        for i in (0, 1):
            total(e, i).wait_recv()
            b, rows = lax.rem(x + (1, 3)[i], 4), slice(64 * i, 64 * i + 64)
            psend[n, b, rows] = psend[n, b, rows] + relay_s[n, i]
            total(e, 4 + i).start()

    def total_take(e):
        n = (X_SUM1, X_SUM2, X_SUM3, X_SUM4).index(e) % 2
        for i in (2, 3, 4, 5):
            total(e, i).wait_recv()
        return own[...] + prec[n, 0].astype(F32) + prec[n, 1].astype(F32)

    def total_sent(e):
        for i in range(6):
            total(e, i).wait_send()

    def quarter(n):
        return (z, y)[n % 2]

    def weight(n, i):
        dst = (wqkv, wqkv, wgf, wuf)[n]
        cols = (pl.ds(0, 512), pl.ds(512, 512), pl.ds(0, 1024), pl.ds(0, 1024))[n]
        q = quarter(n)
        if i < 3:
            to = lax.rem(x + i + 1, 4)
            rows = part(96 * q, 96)
            if n < 2:
                src = wsend.at[to, rows, cols]
            else:
                src = (wg, wu)[n - 2].at[rows, part(1024 * to, 1024)]
            place = dst.at[pl.ds(pl.multiple_of(384 * x + 96 * q, 96), 96), cols]
            device = {"fsdp": to}
        else:
            b = lax.rem(x + 1 + i % 3, 4)
            step = (1, -1, 1, -1)[i // 3 - 1]
            if i < 9:
                rows = pl.ds(pl.multiple_of(384 * b + 96 * q, 96), 96)
            else:
                far, h = lax.rem(q - step + 4, 4), i // 3 - 3
                rows = pl.ds(pl.multiple_of(384 * b + 96 * far + 48 * h, 48), 48)
            src = place = dst.at[rows, cols]
            r = lax.rem(q + step + 4, 4)
            device = {"ctx": 4 * r + y if n % 2 == 0 else 4 * z + r}
        return remote(src, place, ws.at[n, i], wr.at[n, i], device)

    def fetch_to(n, b):
        i, q = lax.rem(b - x + 3, 4), quarter(n)
        cols = pl.ds(512 * n, 512)
        rows = pl.ds(pl.multiple_of(384 * x + 96 * q, 96), 96)
        src = wsend.at[b, part(96 * q, 96), cols]
        return remote(src, wqkv.at[rows, cols], ws.at[n, i], wr.at[n, i], {"fsdp": b})

    def weight_each(which, items, act):
        for i in items:
            for n in which:
                act(weight(n, i))

    def begin(copy):
        copy.start()

    def arrive(copy):
        copy.wait_recv()

    def leave(copy):
        copy.wait_send()

    def weight_fetch(which):
        weight_each(which, (1, 0, 2), begin)

    def weight_share(which):
        weight_each(which, range(3), arrive)
        weight_each(which, range(3, 9), begin)

    def weight_pass(which):
        for k in range(3):
            weight_each(which, (3 + k,), arrive)
            weight_each(which, (9 + k,), begin)
        for k in range(3):
            weight_each(which, (6 + k,), arrive)
            weight_each(which, (12 + k,), begin)

    def weight_wait(which):
        weight_each(which, range(9, 15), arrive)

    heads, wide = (0, 1), (2, 3)

    def gain_copy(k):
        return over_x(X_GAIN, k, gains, gain.at[:, part(384 * x, 384)])

    def pos_copy(k):
        return over_x(X_POS, k, pos, posx.at[x])

    pos[...] = jnp.broadcast_to(
        jnp.concatenate([positions[0:1, :], positions[1:2, :]], axis=1).astype(F32), (8, 128)
    )
    gains[...] = jnp.broadcast_to(norm_attn[...].astype(F32), (8, 384))
    gains[1:2, :] = norm_mlp[...].astype(F32)
    for k in (2, 1, 3):
        pos_copy(k).start()
        gain_copy(k).start()
    gain[:, part(384 * x, 384)] = gains[...]
    posx[x] = pos[...]

    def local_copies():
        yield pltpu.make_async_copy(
            wg.at[:, part(1024 * x, 1024)], wgf.at[part(384 * x, 384)], ls.at[0]
        )
        yield pltpu.make_async_copy(
            wu.at[:, part(1024 * x, 1024)], wuf.at[part(384 * x, 384)], ls.at[1]
        )
        yield pltpu.make_async_copy(wd_in, wd, ls.at[2])
        for h in range(4):
            yield pltpu.make_async_copy(
                wo_in.at[pl.ds(96 * h, 96)], wop.at[pl.ds(128 * h, 96)], ls.at[3 + h]
            )

    def head_columns(b, j, rows):
        w_q = wq[rows, 384 * b + 192 * j : 384 * b + 192 * j + 192]
        w_k = wk[rows, 96 * (2 * b + j) : 96 * (2 * b + j) + 96]
        w_v = wv[rows, 96 * (2 * b + j) : 96 * (2 * b + j) + 96]
        blank = jnp.zeros((w_v.shape[0], 32), BF)
        return jnp.concatenate(spread(w_q, (0, 1)) + spread(w_k, (0,)) + [w_v, blank], axis=1)

    for b in range(4):

        @pl.when(b != x)
        def _(b=b):
            for j in heads:
                rows = part(96 * quarter(j), 96)
                wsend[b, rows, 512 * j : 512 * j + 512] = head_columns(b, j, rows)

                @pl.when(first)
                def _(j=j):
                    fetch_to(j, b).start()

    @pl.when(first)
    def _():
        gather_start(X_IN, xin, xall)
        xall[my_rows, :] = xin[...]

    for b in range(4):

        @pl.when(b == x)
        def _(b=b):
            for j in heads:
                wqkv[384 * b : 384 * b + 384, 512 * j : 512 * j + 512] = head_columns(
                    b, j, slice(0, 384)
                )

    for copy in local_copies():
        copy.start()
    for h in range(4):
        wop[128 * h + 96 : 128 * h + 128, :] = jnp.zeros((32, WIDTH), BF)

    lane = lax.broadcasted_iota(jnp.int32, (1, 128), 1)
    sign = jnp.where(lane < 64, -1.0, 1.0)
    for k in (1, 3, 2):
        pos_copy(k).wait()
    for b in range(4):
        block = posx[b]
        posv[b, 0] = block
        posv[b, 1] = pltpu.roll(block, 64, 1)

    def pos_to(to):
        return over_c(C_POS, to, posv.at[to // 4, lax.rem(to, 4) // 2], posc.at[c])

    def send_pos(k, carry):
        pos_to(lax.rem(c + k, 16)).start()
        return carry

    lax.fori_loop(1, 16, send_pos, 0)
    posc[c] = posv[c // 4, lax.rem(c, 4) // 2]

    @pl.when(first)
    def _():
        weight_share(heads)

    for b in range(4):
        angle = as_column(posx[b][0:1, :]) * freq[0:1, :]
        cos_c[128 * b : 128 * b + 128, :] = jnp.cos(angle)
        sin_c[128 * b : 128 * b + 128, :] = jnp.sin(angle) * sign

    def tables():
        def await_pos(k, carry):
            pos_to(lax.rem(c + k, 16)).wait()
            return carry

        def table(i, carry):
            row = jnp.where(
                lane < 64, posc[2 * i][0:1, :], pltpu.roll(posc[2 * i + 1], 64, 1)[0:1, :]
            )
            block = part(128 * i, 128)
            posr[0:1, block] = row
            column = as_column(row)
            posk[block, :] = jnp.broadcast_to(column, (128, 128))
            angle = column * freq[0:1, :]
            cos_s[block, :] = jnp.cos(angle)
            sin_s[block, :] = jnp.sin(angle) * sign
            return carry

        lax.fori_loop(1, 16, await_pos, 0)
        lax.fori_loop(0, 8, table, 0)

    for k in (1, 3, 2):
        gain_copy(k).wait()

    @pl.when(first)
    def _():
        weight_pass(heads)
        gather_pass(X_IN, xin, xall)
        weight_fetch(wide)
        weight_wait(heads)

    @pl.when(second)
    def _():
        tables()
        gather_start(X_DY, dyin, dyf)
        dyf[my_rows, :] = dyin[...]
        gather_pass(X_DY, dyin, dyf)
        pl.semaphore_wait(go, 1)
        weight_fetch(heads + wide)
        weight_share(heads + wide)
        weight_pass(heads + wide)
        weight_wait(heads + wide)

    gain_attn, gain_mlp = gain[0:1, :], gain[1:2, :]

    def to_pair(ref, e, b, i, width, dst):
        src = ref.at[part(128 * b + 64 * (i // 2), 64), pl.ds(width * (i % 2), width)]
        return over_c(e, 4 * b + i, src, dst.at[part(64 * c, 64)])

    def in_order(n):
        return behind(jnp.where(n == 2, 3, jnp.where(n == 3, 2, n)))

    def project(n, carry):
        b = in_order(n)
        rows = part(128 * b, 128)

        @pl.when(jnp.logical_and(second, n == 0))
        def _():
            gather(X_IN, 6, out, xall).wait_recv()

        @pl.when(jnp.logical_and(second, n == 1))
        def _():
            gather_pass(X_IN, xin, xall)

        @pl.when(n == 3)
        def _():
            gather_far(X_IN, xin, xall)

        value = xall[rows, :].astype(F32)
        normed = (
            value
            * lax.rsqrt(jnp.mean(value * value, axis=-1, keepdims=True) + EPSILON)
            * gain_attn
        ).astype(BF)
        nf[rows, :] = normed
        u = mm(normed, wqkv[...])
        cosine, sine = cos_c[rows, :], sin_c[rows, :]
        for h in range(8):
            head = u[:, 128 * h : 128 * h + 128]
            if h % 4 != 3:
                head = turn(head, cosine, sine)
            qsend[rows, 128 * h : 128 * h + 128] = head.astype(BF)
        for i in range(4):

            @pl.when(4 * b + i != c)
            def _(i=i):
                to_pair(qsend, C_QKV, b, i, 512, qs).start()

            @pl.when(4 * b + i == c)
            def _(i=i):
                qs[part(64 * c, 64), :] = qsend[
                    part(128 * b + 64 * (i // 2), 64), 512 * (i % 2) : 512 * (i % 2) + 512
                ]

        return carry

    lax.fori_loop(0, 4, project, 0)

    @pl.when(first)
    def _():
        tables()

    weight_each(heads, range(3), leave)


    def await_qkv(k, carry):
        place = qs.at[part(64 * lax.rem(c - k + 16, 16), 64)]
        over_c(C_QKV, lax.rem(c + k, 16), place, place).wait_recv()
        return carry

    lax.fori_loop(1, 16, await_qkv, 0)

    @pl.when(first)
    def _():
        weight_share(wide)
        pl.semaphore_signal(go, inc=1, device_id={"section": 1}, device_id_type=MESH)

    vt[...] = qs[:, 384:512].T
    kt[...] = qs[:, 256:384].T

    def masked(q, cols):
        st = mm_nt(qs[:, 256:384], q) * SCALE
        return jnp.where(posk[:, 0:1] <= posr[0:1, cols], st, -1e30)

    def att_place():
        return attp.at[part(64 * (c // 2), 64), part(256 * lax.rem(c, 2), 256)]

    def att_to(to):
        return over_c(C_ATT, to, osend.at[part(64 * to, 64)], att_place())

    def attend(n, carry):
        rows = part(256 * n, 256)

        for g in range(2):
            st = masked(qs[rows, 128 * g : 128 * g + 128], rows)
            top = jnp.max(st, axis=0, keepdims=True)
            e = jnp.exp(st - top)
            total = jnp.sum(e, axis=0, keepdims=True)
            lse[g : g + 1, rows] = top + jnp.log(total)
            pt = (e * (1.0 / total)).astype(BF)
            osend[rows, 128 * g : 128 * g + 128] = mm(vt[...], pt).T.astype(BF)
        for i in range(4):
            to = 4 * n + i

            @pl.when(to != c)
            def _(to=to):
                att_to(to).start()

            @pl.when(to == c)
            def _(to=to):
                attp[part(64 * (c // 2), 64), part(256 * lax.rem(c, 2), 256)] = osend[
                    part(64 * to, 64), :
                ]

        return carry

    lax.fori_loop(0, 4, attend, 0)

    @pl.when(first)
    def _():
        weight_pass(wide)


    def await_att(b):
        for i in range(4):
            to = 4 * b + i

            @pl.when(to != c)
            def _(to=to, i=i):
                k = lax.rem(c - to + 16, 16)
                place = attp.at[part(64 * (2 * b + i // 2), 64), pl.ds(256 * (i % 2), 256)]
                remote(place, place, cs.at[C_ATT, k], cr.at[C_ATT, k], {"ctx": lax.rem(c + k, 16)}).wait_recv()

    def give(e, n, b, value):
        place = psend.at[(X_SUM1, X_SUM2, X_SUM3, X_SUM4).index(e) % 2, b]

        @pl.when(n < 3)
        def _():
            place[...] = value.astype(BF)

        @pl.when(n == 0)
        def _():
            total(e, 0).start()
            total(e, 1).start()

        @pl.when(n == 1)
        def _():
            total(e, 2).start()

        @pl.when(n == 2)
        def _():
            total(e, 3).start()
            total_pass(e)

        @pl.when(n == 3)
        def _():
            own[...] = value

    def far_first(n):
        return lax.rem(x + jnp.where(n == 0, 2, jnp.where(n == 1, 1, jnp.where(n == 2, 3, 0))), 4)

    def combine(n, carry):
        b = far_first(n)
        await_att(b)
        give(X_SUM1, n, b, mm(attp[part(128 * b, 128), :], wop[...]))
        return carry

    for copy in local_copies():
        copy.wait()
    lax.fori_loop(0, 4, combine, 0)
    middle = xall[my_rows, :].astype(F32) + total_take(X_SUM1)
    mid[...] = middle
    n2[my_rows, :] = (
        middle * lax.rsqrt(jnp.mean(middle * middle, axis=-1, keepdims=True) + EPSILON) * gain_mlp
    ).astype(BF)
    n2_own = n2.at[my_rows]
    gather_start(X_N2, n2_own, n2)

    @pl.when(first)
    def _():
        weight_wait(wide)

    def pair(blocks, ref):
        return jnp.concatenate([ref[part(128 * b, 128), :] for b in blocks], axis=0)

    def far_copy(d, b):
        return piece(X_SUM2, d, d, psend.at[1, b], prec3.at[d - 1])

    def feed(ds):
        blocks = [lax.rem(x + d, 4) for d in ds]
        a = pair(blocks, n2)
        ga, u = mm(a, wgf[...]), mm(a, wuf[...])
        h = (ga * (1.0 / (1.0 + jnp.exp(-ga))) * u).astype(BF)
        result = mm(h, wd[...])
        for n, (d, b) in enumerate(zip(ds, blocks)):
            rows, cut = part(128 * b, 128), slice(128 * n, 128 * n + 128)
            gate[rows, :] = ga[cut].astype(BF)
            up[rows, :] = u[cut].astype(BF)
            hidden[rows, :] = h[cut]
            if d == 0:
                own[...] = result[cut]
            else:
                psend[1, b] = result[cut].astype(BF)
                far_copy(d, b).start()

    gather_pass(X_N2, n2_own, n2)
    feed((1, 3))
    gather_far(X_N2, n2_own, n2)
    feed((2, 0))
    result = mid[...] + own[...]
    for d in (1, 3, 2):
        far_copy(d, lax.rem(x + d, 4)).wait_recv()
        result = result + prec3[d - 1].astype(F32)
    out[...] = result.astype(BF)

    @pl.when(first)
    def _():
        gather_sent(X_IN, xin, xall, forwarded=False)
        gather(X_IN, 6, out, xall).start()
        gather_start(X_IN, out, xall, True)

    held = dict(zip(NAMES, (h_gate, h_up, h_down, h_out, h_heads_a, h_heads_b)))

    def ring(name):
        axis, d, _, _ = FLOWS[name]
        other = "z" if axis == "y" else "y"
        return NAMES.index(name), axis, other, d, where[axis], where[other]

    def at(i, d, s):
        return lax.rem(i - d * s + 8, 4)

    def partial(name, g, p):
        if name == "down":
            return wd.at[part(256 * g + 64 * p, 64)]
        if name == "out":
            return wop.at[part(96 * g, 96), part(384 * p, 384)]
        rows = pl.ds(pl.multiple_of(384 * g + 96 * p, 96), 96)
        if name in LATE:
            return wqkv.at[rows, pl.ds(384 * LATE.index(name), 384)]
        return (wgf if name == "gate" else wuf).at[rows]

    def arrival(name, s, q):
        n = 4 * (s - 1) + q
        if name == "gate":
            return wsend.at[s, part(96 * q, 96)]
        if name == "up":
            return wsend.at[3, part(96 * q, 96)] if s == 0 else dgu.at[part(96 * n, 96)]
        if name == "down":
            return arrive_down.at[q] if s == 0 else n2.at[part(64 * n, 64)]
        return arrive_out.at[s, q]

    def arrival2(name, s):
        if name in ("gate", "up"):
            return (gate if name == "gate" else up).at[part(96 * s, 96)]
        if name == "down":
            return prec3.at[s, pl.ds(0, 64)]
        return (second_out, second_a, second_b)[SMALL.index(name)].at[s]

    def flow(name, n, src, dst, device):
        f = NAMES.index(name)
        return remote(src, dst, fs.at[f, n], fr.at[f, n], device)

    def copy_first(name, s, q):
        f, axis, other, d, i, j = ring(name)
        src = partial(name, at(i, d, 1 + s), at(j, d, 1 + q))
        return flow(name, 4 * s + q, src, arrival(name, s, q), near(axis, d))

    def copy_second(name, s):
        f, axis, other, d, i, j = ring(name)
        src = partial(name, i, at(j, d, 1 + s))
        return flow(name, 12 + s, src, arrival2(name, s), near(other, d))

    def copy_mirror(name):
        f, axis, other, d, i, j = ring(name)
        n = 6 if name in LATE else 15
        return flow(name, n, partial(name, i, j), held[name].at[x, j], mirror[axis])

    def copy_own(name):
        f, axis, other, d, i, j = ring(name)
        group = i if name in ("down", "out") else x
        return pltpu.make_async_copy(partial(name, i, j), held[name].at[group, j], os.at[f])

    def copy_small(name, s):
        f, axis, other, d, i, j = ring(name)
        place = held[name].at[i, at(j, d, s)]
        return flow(name, 16 + s, place, place, near(other, d))

    def copy_big(name, s, q):
        f, axis, other, d, i, j = ring(name)
        place = held[name].at[at(i, d, s), at(j, d, q)]
        return flow(name, 20 + 4 * s + q, place, place, near(axis, d))

    def first_start(names):
        def body(q, carry):
            for name in names:
                copy_first(name, 0, q).start()
            return carry

        lax.fori_loop(0, 4, body, 0)

    def first_step(names, s):
        def body(q, carry):
            for name in names:
                f, axis, other, d, i, j = ring(name)
                copy_first(name, s, q).wait_recv()
                place = partial(name, at(i, d, 2 + s), at(j, d, 1 + q))
                place[...] = place[...] + arrival(name, s, q)[...]
                if s < 2:
                    copy_first(name, s + 1, q).start()
                else:

                    @pl.when(q == 0)
                    def _(name=name):
                        copy_second(name, 0).start()

            return carry

        lax.fori_loop(0, 4, body, 0)

    def second_step(names, s):
        for name in names:
            f, axis, other, d, i, j = ring(name)
            copy_second(name, s).wait_recv()
            place = partial(name, i, at(j, d, 2 + s))
            place[...] = place[...] + arrival2(name, s)[...]
            if s < 2:
                copy_second(name, s + 1).start()

    def mirror_step(names, act):
        for name in names:
            if name in ("down", "out"):
                act(copy_own(name))
                continue
            axis = FLOWS[name][0]

            @pl.when(where[axis] != x)
            def _(name=name):
                act(copy_mirror(name))

            @pl.when(where[axis] == x)
            def _(name=name):
                act(copy_own(name))

    def finish_copy(copy):
        copy.wait()

    def small_step(names, q):
        for name in names:
            if q > 0:
                copy_small(name, q - 1).wait_recv()
            if q < 3:
                copy_small(name, q).start()
        for name in names:
            copy_big(name, 0, q).start()

    def big_step(names, s, low, high):
        def body(q, carry):
            for name in names:
                copy_big(name, s, q).wait_recv()
                if s < 2:
                    copy_big(name, s + 1, q).start()
            return carry

        lax.fori_loop(low, high, body, 0)

    def gain_sum_copy(n, k):
        axis = "xyz"[n]
        if n == 0:
            src = ggain.at[:, part(lax.rem(x + k, 4) * 384, 384)]
        else:
            src = gain_in.at[n, 0]
        return remote(src, gain_in.at[n, k], gs.at[n, k], gr.at[n, k], near(axis, k))

    def gain_start(n):
        for k in (1, 2, 3):
            gain_sum_copy(n, k).start()

    def gain_sum(n):
        mine = ggain[:, part(x * 384, 384)] if n == 0 else gain_in[n, 0]
        for k in (1, 2, 3):
            gain_sum_copy(n, k).wait()
        return mine + gain_in[n, 1] + gain_in[n, 2] + gain_in[n, 3]

    def late(name, n):
        f, axis, other, d, i, j = ring(name)
        cols = pl.ds(384 * LATE.index(name), 384)
        k = (n if n < 6 else n - 1) % 3 + 1
        if n < 3:
            src = wqkv.at[part(384 * lax.rem(i + k, 4), 384), cols]
            return flow(name, n, src, (arrive_a, arrive_b)[f - 4].at[k - 1], near(axis, k))
        if n < 6:
            src = partial(name, i, lax.rem(j + k, 4))
            return flow(name, n, src, arrival2(name, k - 1), near(other, k))
        if n < 10:
            place = held[name].at[i, j]
            return flow(name, n, place, place, near(other, k))
        place = held[name].at[i]
        return flow(name, n, place, place, near(axis, k))

    def late_each(items, act):
        for n in items:
            for name in LATE:
                act(late(name, n))

    def late_first():
        late_each(range(3), arrive)
        for name in LATE:
            f, axis, other, d, i, j = ring(name)
            rows, cols = part(384 * i, 384), pl.ds(384 * LATE.index(name), 384)
            got = (arrive_a, arrive_b)[f - 4]
            sums = wqkv[rows, cols].astype(F32)
            for k in range(3):
                sums = sums + got[k].astype(F32)
            wqkv[rows, cols] = sums.astype(BF)
        late_each(range(3, 6), begin)

    def late_second():
        late_each(range(3, 6), arrive)
        for name in LATE:
            f, axis, other, d, i, j = ring(name)
            place = partial(name, i, j)
            sums = place[...].astype(F32)
            for k in range(3):
                sums = sums + arrival2(name, k)[...].astype(F32)
            place[...] = sums.astype(BF)
        mirror_step(LATE, begin)

    def late_small():
        mirror_step(LATE, finish_copy)
        late_each(range(7, 10), begin)

    def late_big():
        late_each(range(7, 10), arrive)
        late_each(range(10, 13), begin)

    def feed_grads(s, carry):
        rows = part(384 * at(y, 1, 1 + s), 384)
        wgf[rows, :] = mm_tn(n2[:, rows], dgu[0:512, :]).astype(BF)
        rows = part(384 * at(y, -1, 1 + s), 384)
        wuf[rows, :] = mm_tn(n2[:, rows], dgu[512:1024, :]).astype(BF)
        rows = part(256 * at(z, 1, 1 + s), 256)
        wd[rows, :] = mm_tn(hidden[:, rows], dyf[...]).astype(BF)

        @pl.when(s == 0)
        def _():
            first_start(EARLY[:3])

        return carry

    @pl.when(first)
    def _():
        gather_pass(X_DY, dx, dyf)
        gather(X_DY, 6, dx, dyf).wait_recv()

    gather_far(X_DY, dx, dyf)

    def feed_back(ds):
        blocks = [lax.rem(x + d, 4) for d in ds]
        dh = mm_nt(pair(blocks, dyf), wd[...])
        ga, u = pair(blocks, gate).astype(F32), pair(blocks, up).astype(F32)
        s = 1.0 / (1.0 + jnp.exp(-ga))
        dga = (dh * u * (s * (1.0 + ga * (1.0 - s)))).astype(BF)
        du = (dh * (ga * s)).astype(BF)
        result = mm_nt(dga, wgf[...]) + mm_nt(du, wuf[...])
        for n, (d, b) in enumerate(zip(ds, blocks)):
            rows, cut = part(128 * b, 128), slice(128 * n, 128 * n + 128)
            dgu[rows, :] = dga[cut]
            dgu[part(512 + 128 * b, 128), :] = du[cut]
            if d == 0:
                own[...] = result[cut]
            else:
                psend[0, b] = result[cut].astype(BF)
                for i in {2: (0, 1), 1: (2,), 3: (3,)}[d]:
                    total(X_SUM3, i).start()

    total_sent(X_SUM1)
    feed_back((2, 1))
    feed_back((3, 0))
    total_pass(X_SUM3)
    weight_each(heads, range(3, 15), leave)
    weight_each(wide, range(15), leave)
    gather_sent(X_N2, n2_own, n2)
    gather_sent(X_DY, dyin, dyf, started=False)
    for d in (1, 2, 3):
        far_copy(d, lax.rem(x + d, 4)).wait_send()
    lax.fori_loop(0, 4, feed_grads, 0)
    def norm_back(value, grad, gain_row):
        r = lax.rsqrt(jnp.mean(value * value, axis=-1, keepdims=True) + EPSILON)
        unit = value * r
        t = grad * gain_row
        back = r * (t - unit * jnp.mean(t * unit, axis=-1, keepdims=True))
        return back, jnp.sum(grad * unit, axis=0, keepdims=True)

    back, g_mlp = norm_back(mid[...], total_take(X_SUM3), gain_mlp)
    dmid = dyf[my_rows, :].astype(F32) + back
    mid[...] = dmid
    ggain[...] = jnp.zeros_like(ggain)
    ggain[1:2, :] = g_mlp
    dbr[my_rows, :] = dmid.astype(BF)
    dbr_own = dbr.at[my_rows]
    gather_start(X_DBR, dbr_own, dbr)

    def branch(n, carry):
        b = in_order(n)
        rows = part(128 * b, 128)

        @pl.when(n == 1)
        def _():
            gather_pass(X_DBR, dbr_own, dbr)

        @pl.when(n == 3)
        def _():
            gather_far(X_DBR, dbr_own, dbr)

        dsend[rows, :] = mm_nt(dbr[rows, :], wop[...]).astype(BF)
        for i in range(4):

            @pl.when(4 * b + i != c)
            def _(i=i):
                to_pair(dsend, C_DATT, b, i, 256, das).start()

            @pl.when(4 * b + i == c)
            def _(i=i):
                das[part(64 * c, 64), :] = dsend[
                    part(128 * b + 64 * (i // 2), 64), 256 * (i % 2) : 256 * (i % 2) + 256
                ]

        return carry

    lax.fori_loop(0, 4, branch, 0)
    for n in range(2):
        rows = slice(256 * n, 256 * n + 256)
        att[rows, :] = jnp.concatenate(
            [attp[rows, 128 * h : 128 * h + 96] for h in range(4)], axis=1
        )
    wop[0:384, :] = mm_tn(att[...], dbr[...]).astype(BF)
    first_start(("out",))

    def await_das(k, carry):
        place = das.at[part(64 * lax.rem(c - k + 16, 16), 64)]
        over_c(C_DATT, lax.rem(c + k, 16), place, place).wait_recv()
        return carry

    lax.fori_loop(1, 16, await_das, 0)
    first_step(EARLY, 0)
    dk[...] = jnp.zeros_like(dk)
    dv[...] = jnp.zeros_like(dv)

    def grad_place(h):
        return dqp.at[part(64 * (c // 2), 64), part(512 * lax.rem(c, 2) + 256 * h, 256)]

    def grad_to(e, to):
        h = e - C_DQ
        return over_c(e, to, dqs.at[part(64 * to, 64), pl.ds(256 * h, 256)], grad_place(h))

    def attend_back(n, carry):
        rows = part(256 * n, 256)
        for g in range(2):
            cols = slice(128 * g, 128 * g + 128)
            q, da = qs[rows, cols], das[rows, cols]
            p = jnp.exp(masked(q, rows) - lse[g : g + 1, rows])
            dp = mm_nt(qs[:, 384:512], da)
            dv[...] += mm(p.astype(BF), da)
            ds = (p * (dp - jnp.sum(p * dp, axis=0, keepdims=True))).astype(BF)
            dk[...] += mm(ds, q)
            dq = mm(kt[...], ds).T * SCALE
            dqs[rows, cols] = turn(dq, cos_s[rows, :], -sin_s[rows, :]).astype(BF)
        for i in range(4):
            to = 4 * n + i

            @pl.when(to != c)
            def _(to=to):
                grad_to(C_DQ, to).start()

            @pl.when(to == c)
            def _(to=to):
                grad_place(0)[...] = dqs[part(64 * to, 64), 0:256]

        return carry

    lax.fori_loop(0, 4, attend_back, 0)
    dqs[:, 256:384] = turn(dk[...] * SCALE, cos_s[...], -sin_s[...]).astype(BF)
    dqs[:, 384:512] = dv[...].astype(BF)

    def send_dkv(k, carry):
        grad_to(C_DKV, lax.rem(c + k, 16)).start()
        return carry

    lax.fori_loop(1, 16, send_dkv, 0)
    grad_place(1)[...] = dqs[part(64 * c, 64), 256:512]
    first_step(EARLY, 1)

    def await_dqkv(b):
        for i in range(4):
            to = 4 * b + i

            @pl.when(to != c)
            def _(to=to, i=i):
                k = lax.rem(c - to + 16, 16)
                for h in range(2):
                    place = dqp.at[
                        part(64 * (2 * b + i // 2), 64), pl.ds(512 * (i % 2) + 256 * h, 256)
                    ]
                    e = C_DQ + h
                    remote(
                        place, place, cs.at[e, k], cr.at[e, k], {"ctx": lax.rem(c + k, 16)}
                    ).wait_recv()

    def input_grad(n, carry):
        b = far_first(n)
        await_dqkv(b)
        give(X_SUM4, n, b, mm_nt(dqp[part(128 * b, 128), :], wqkv[...]))
        return carry

    lax.fori_loop(0, 4, input_grad, 0)
    for n in range(2):
        rows = slice(256 * n, 256 * n + 256)
        pieces = []
        for h in range(8):
            if h % 4 == 3:
                pieces.append(dqp[rows, 128 * h : 128 * h + 96])
            else:
                pieces.append(dqp[rows, 128 * h : 128 * h + 48])
                pieces.append(dqp[rows, 128 * h + 64 : 128 * h + 112])
        dqkv[rows, :] = jnp.concatenate(pieces, axis=1)

    def head_grads(g, carry):
        rows = part(384 * g, 384)
        wqkv[rows, 0:768] = mm_tn(nf[:, rows], dqkv[...]).astype(BF)
        return carry

    lax.fori_loop(0, 4, head_grads, 0)
    late_each(range(3), begin)
    back, g_attn = norm_back(xall[my_rows, :].astype(F32), total_take(X_SUM4), gain_attn)
    dx[...] = (mid[...] + back).astype(BF)
    ggain[0:1, :] = g_attn

    @pl.when(second)
    def _():
        gather_sent(X_DY, dyin, dyf, forwarded=False)
        gather(X_DY, 6, dx, dyf).start()
        gather_start(X_DY, dx, dyf, True)

    gain_start(0)
    first_step(EARLY, 2)
    second_step(EARLY, 0)
    gain_in[1, 0] = gain_sum(0)
    gain_start(1)
    second_step(EARLY, 1)
    late_first()
    second_step(EARLY, 2)
    mirror_step(EARLY, begin)
    gain_in[2, 0] = gain_sum(1)
    gain_start(2)
    late_second()
    mirror_step(EARLY, finish_copy)
    small_step(EARLY, 0)
    late_small()
    small_step(EARLY, 1)
    late_big()
    small_step(EARLY, 2)
    small_step(EARLY, 3)
    for n in range(3):
        big_step(EARLY, n, 0, 4)
    late_each(range(10, 13), arrive)
    o_gain[...] = gain_sum(2)

    def sent_c(k, carry):
        to = lax.rem(c + k, 16)
        place = qs.at[part(64 * to, 64)]
        over_c(C_QKV, to, place, place).wait_send()
        att_to(to).wait_send()
        place = das.at[part(64 * to, 64)]
        over_c(C_DATT, to, place, place).wait_send()
        grad_to(C_DQ, to).wait_send()
        grad_to(C_DKV, to).wait_send()
        return carry

    lax.fori_loop(1, 16, sent_c, 0)
    total_sent(X_SUM3)
    total_sent(X_SUM4)
    gather_sent(X_DBR, dbr_own, dbr)
    gather_sent(X_IN, xin, xall, started=False)

    def sent_first(q, carry):
        for name in EARLY:
            for n in range(3):
                copy_first(name, n, q).wait_send()
                copy_big(name, n, q).wait_send()
        return carry

    lax.fori_loop(0, 4, sent_first, 0)
    late_each((0, 1, 2, 3, 4, 5, 7, 8, 9, 10, 11, 12), leave)
    for name in EARLY:
        for n in range(3):
            copy_second(name, n).wait_send()
            copy_small(name, n).wait_send()

    @pl.when(first)
    def _():
        gather_sent(X_IN, xin, xall, forwarded=False)
        gather(X_IN, 6, out, xall).wait_send()

    @pl.when(second)
    def _():
        gather_sent(X_DY, dyin, dyf, forwarded=False)
        gather(X_DY, 6, dx, dyf).wait_send()


def run_layer(xin, dyin, positions, freq, norm_attn, norm_mlp, wq, wk, wv, wo, wd, wg, wu, cid):
    vm = pl.BlockSpec(memory_space=pltpu.VMEM)
    hbm = pl.BlockSpec(memory_space=pl.ANY)
    dma = pltpu.SemaphoreType.DMA
    shapes = [
        ((128, WIDTH), BF),
        ((128, WIDTH), BF),
        *(((4, 4, r, w), BF) for _, _, r, w in FLOWS.values()),
        ((8, 384), F32),
    ]
    scratch = [
        ((512, WIDTH), BF),
        ((2, 512, WIDTH), BF),
        ((1024, 1024), BF),
        ((512, 768), BF),
        ((512, 384), BF),
        ((512, WIDTH), BF),
        ((512, 1024), BF),
        ((8, WIDTH), F32),
        ((4, 64, WIDTH), BF),
        ((3, 4, 96, 384), BF),
        *(((3, 384, 384), BF),) * 2,
        *(((3, 96, 384), BF),) * 3,
        ((3, 4, 8, 384), F32),
        ((4, 384, 1024), BF),
        ((WIDTH, 1024), BF),
        ((WIDTH, 1024), BF),
        ((WIDTH, 1024), BF),
        ((512, WIDTH), BF),
        ((1024, WIDTH), BF),
        ((2, 2, 64, WIDTH), BF),
        ((512, WIDTH), BF),
        ((8, 384), F32),
        ((8, 128), F32),
        ((8, WIDTH), F32),
        ((4, 8, 128), F32),
        ((4, 2, 8, 128), F32),
        ((16, 8, 128), F32),
        ((8, 1024), F32),
        ((1024, 128), F32),
        ((512, 128), F32),
        ((512, 128), F32),
        ((1024, 128), F32),
        ((1024, 128), F32),
        ((512, 1024), BF),
        ((1024, 512), BF),
        ((128, 1024), BF),
        ((128, 1024), BF),
        ((8, 1024), F32),
        ((1024, 256), BF),
        ((512, 512), BF),
        ((128, WIDTH), F32),
        ((512, 1024), BF),
        ((512, 1024), BF),
        ((128, WIDTH), F32),
        ((2, 4, 128, WIDTH), BF),
        ((2, 2, 128, WIDTH), BF),
        ((3, 128, WIDTH), BF),
        ((512, 512), BF),
        ((1024, 256), BF),
        ((1024, 128), F32),
        ((1024, 128), F32),
        ((1024, 512), BF),
        ((512, 1024), BF),
    ]
    return pl.pallas_call(
        layer_kernel,
        out_shape=[jax.ShapeDtypeStruct(s, d) for s, d in shapes],
        in_specs=[vm] * 9 + [hbm] * 4,
        out_specs=[vm] * 2 + [hbm] * len(FLOWS) + [vm],
        scratch_shapes=[pltpu.VMEM(s, d) for s, d in scratch]
        + [dma((13, 7)), dma((13, 7)), dma((6, 16)), dma((6, 16)), dma((4, 15)), dma((4, 15)), dma((7,)), pltpu.SemaphoreType.REGULAR]
        + [dma((6, 32)), dma((6, 32)), dma((3, 4)), dma((3, 4)), dma((6,))],
        name="layer",
        compiler_params=pltpu.CompilerParams(
            collective_id=cid, has_side_effects=True, vmem_limit_bytes=63 << 20
        ),
    )(xin, dyin, positions, freq, norm_attn, norm_mlp, wq, wk, wv, wo, wd, wg, wu)


def local(
    inputs,
    positions,
    out_grad,
    norm_attn,
    w_query,
    key_weight,
    value_weight,
    output_weight,
    norm_mlp,
    w_gate,
    w_up,
    w_down,
):
    lane = np.arange(128)
    index = np.where(lane < 64, lane, lane - 64)
    freq = np.where(index < 48, THETA ** (-2.0 * index / HEAD_SIZE), 0.0).astype(np.float32)
    freq = jnp.asarray(np.broadcast_to(freq[None], (8, 128)))
    out, dx, *summed, g_gain = run_layer(
        inputs.reshape(128, WIDTH),
        out_grad.reshape(128, WIDTH),
        positions,
        freq,
        norm_attn,
        norm_mlp,
        w_query[0],
        key_weight[0],
        value_weight[0],
        output_weight[0],
        w_down[0],
        w_gate[0],
        w_up[0],
        0,
    )
    g_gate, g_up, g_query, g_key, g_value, g_out, g_down, g_attn, g_mlp = widen(*summed, g_gain)
    return (
        out.reshape(1, 2, 64, WIDTH),
        dx.reshape(1, 2, 64, WIDTH),
        g_attn,
        g_query[None],
        g_key[None],
        g_value[None],
        g_out[None],
        g_mlp,
        g_gate[None],
        g_up[None],
        g_down[None],
    )


def solution(mesh):
    rows = P("section", "fsdp", None)
    return jax.shard_map(
        local,
        mesh=mesh,
        in_specs=(
            P("fsdp", "ctx", None),
            P("fsdp", "ctx"),
            P("fsdp", "ctx", None),
            P("section", "fsdp"),
            rows,
            rows,
            rows,
            rows,
            P("section", "fsdp"),
            rows,
            rows,
            rows,
        ),
        out_specs=(
            P("section", "fsdp", "ctx", None),
            P("section", "fsdp", "ctx", None),
            P("section", "fsdp"),
            rows,
            rows,
            rows,
            rows,
            P("section", "fsdp"),
            rows,
            rows,
            rows,
        ),
        check_vma=False,
    )
```

```python
import jax
import jax.numpy as jnp
import numpy as np
from jax import lax
from jax.experimental import pallas as pl
from jax.experimental.pallas import tpu as pltpu
from jax.sharding import PartitionSpec as P

QUERY_HEADS = 16
KEY_VALUE_HEADS = 8
HEAD_SIZE = 96
WIDTH = 1536
FF = 4096
THETA = 100000.0
EPSILON = 1e-05
MESH = pl.DeviceIdType.MESH
N_X = 4
N_C = 16
BF = jnp.bfloat16
F32 = jnp.float32


def mm(a, b):
    return jnp.dot(a, b, preferred_element_type=F32)


def mm_tn(a, b):
    return lax.dot_general(a, b, (((0,), (0,)), ((), ())), preferred_element_type=F32)


def mm_nt(a, b):
    return lax.dot_general(a, b, (((1,), (1,)), ((), ())), preferred_element_type=F32)


def remote(src, dst, send, recv, device):
    return pltpu.make_async_remote_copy(
        src_ref=src, dst_ref=dst, send_sem=send, recv_sem=recv, device_id=device, device_id_type=MESH
    )


def part(start, size):
    return pl.ds(pl.multiple_of(start, size), size)


def widen_kernel(w_gate, w_up, w_down, w_out, w_a, w_b, gains, gate, up, query, key, value, g_out, g_down, g_attn, g_mlp):
    g_attn[...] = gains[0:1, :]
    g_mlp[...] = gains[1:2, :]
    g_down[...] = w_down[...].astype(F32)
    keys, values = [], []
    for x in range(N_X):
        gate[:, 1024 * x : 1024 * x + 1024] = w_gate[x, 0].astype(F32)
        up[:, 1024 * x : 1024 * x + 1024] = w_up[x, 0].astype(F32)
        g_out[:, 384 * x : 384 * x + 384] = w_out[0, x].astype(F32)
        a, b = w_a[x, 0].astype(F32), w_b[x, 0].astype(F32)
        query[:, 384 * x : 384 * x + 384] = jnp.concatenate([a[:, :192], b[:, :192]], axis=1)
        keys += [a[:, 192:288], b[:, 192:288]]
        values += [a[:, 288:], b[:, 288:]]
    key[...] = jnp.concatenate(keys, axis=1)
    value[...] = jnp.concatenate(values, axis=1)


def widen(gate, up, down, out, heads_a, heads_b, gains):
    steps = 8

    def spec(r, cols):
        return pl.BlockSpec((r, cols), lambda i: (i, 0))

    def shape(r, cols):
        return jax.ShapeDtypeStruct((r, cols), F32)

    def blocks(cols):
        return pl.BlockSpec((4, 1, 48, cols), lambda i: (0, i // 2, i % 2, 0))

    return pl.pallas_call(
        widen_kernel,
        grid=(steps,),
        out_shape=[
            shape(384, FF),
            shape(384, FF),
            shape(384, 1536),
            shape(384, 768),
            shape(384, 768),
            shape(384, 1536),
            shape(1024, 1536),
            shape(1, 384),
            shape(1, 384),
        ],
        in_specs=[
            blocks(1024),
            blocks(1024),
            spec(128, 1536),
            pl.BlockSpec((1, 4, 48, 384), lambda i: (i // 2, 0, i % 2, 0)),
            blocks(384),
            blocks(384),
            pl.BlockSpec((8, 384), lambda i: (0, 0)),
        ],
        out_specs=[
            spec(48, FF),
            spec(48, FF),
            spec(48, 1536),
            spec(48, 768),
            spec(48, 768),
            spec(48, 1536),
            spec(128, 1536),
            pl.BlockSpec((1, 384), lambda i: (0, 0)),
            pl.BlockSpec((1, 384), lambda i: (0, 0)),
        ],
        name="widen",
        compiler_params=pltpu.CompilerParams(vmem_limit_bytes=60 << 20),
    )(gate, up, down.reshape(1024, 1536), out, heads_a, heads_b, gains)


X_GAIN, X_POS, X_IN, X_DY, X_QKV, X_GATE, X_UP, X_SUM1, X_N2, X_SUM2, X_SUM3, X_DBR, X_SUM4 = range(13)
C_POS, C_QKV, C_ATT, C_DATT, C_DQ, C_DKV = range(6)
SCALE = HEAD_SIZE ** (-0.5)
SCALE2 = SCALE * 1.4426950408889634
FLOWS = {
    "gate": ("y", 1, "gate", 0, 96, 896),
    "up": ("y", -1, "up", 0, 96, 896),
    "down": ("z", 1, "down", 0, 64, 1280),
    "out": ("z", -1, "out", 0, 96, 384),
    "gate_rest": ("z", -1, "gate", 896, 96, 128),
    "up_rest": ("z", -1, "up", 896, 96, 128),
    "down_rest": ("z", -1, "down", 1280, 64, 256),
    "heads_a": ("y", 1, "heads_a", 0, 96, 384),
    "heads_b": ("z", -1, "heads_b", 0, 96, 384),
}
ARRAYS = {
    "gate": (96, 1024),
    "up": (96, 1024),
    "down": (64, 1536),
    "out": (96, 384),
    "heads_a": (96, 384),
    "heads_b": (96, 384),
}
NAMES = list(FLOWS)
EARLY, LATE = NAMES[:7], NAMES[7:]


def spread(w, heads):
    blank = jnp.zeros((w.shape[0], 16), w.dtype)
    pieces = []
    for h in heads:
        pieces += [w[:, 96 * h : 96 * h + 48], blank, w[:, 96 * h + 48 : 96 * h + 96], blank]
    return pieces


def as_column(row):
    eye = lax.broadcasted_iota(jnp.int32, (128, 128), 0) == lax.broadcasted_iota(
        jnp.int32, (128, 128), 1
    )
    return jnp.sum(jnp.where(eye, jnp.broadcast_to(row, (128, 128)), 0.0), axis=1, keepdims=True)


def turn(u, cosine, sine):
    return u * cosine + pltpu.roll(u, 64, 1) * sine


def layer_kernel(
    xin,
    dyin,
    positions,
    freq,
    norm_attn,
    norm_mlp,
    wq,
    wk,
    wv,
    wo_in,
    wd_in,
    wg,
    wu,
    out,
    dx,
    h_gate,
    h_up,
    h_down,
    h_out,
    h_heads_a,
    h_heads_b,
    o_gain,
    nf,
    rows2,
    dgu,
    dqkv,
    att,
    dbr,
    hidden,
    ggain,
    arrive_down,
    arrive_out,
    arrive_a,
    arrive_b,
    second_out,
    second_a,
    second_b,
    gain_in,
    wsend,
    wqkv,
    wgf,
    wuf,
    wop,
    wd,
    relay_s,
    xall,
    gains,
    pos,
    gain,
    posx,
    posv,
    posc,
    posr,
    posk,
    cos_c,
    sin_c,
    cos_s,
    sin_s,
    qsend,
    qs,
    vt,
    kt,
    lse,
    osend,
    attp,
    mid,
    gate,
    up,
    own,
    psend,
    prec,
    prec3,
    dsend,
    das,
    dk,
    dv,
    dqs,
    dqp,
    xs,
    xr,
    cs,
    cr,
    ws,
    wr,
    ls,
    go,
    fs,
    fr,
    gs,
    gr,
    os,
):
    section = lax.axis_index("section")
    x = lax.axis_index("fsdp")
    c = lax.axis_index("ctx")
    y, z = lax.rem(c, 4), c // 4
    first, second = section == 0, section == 1
    my_rows = part(128 * x, 128)
    n2, dyf = rows2.at[0], rows2.at[1]
    where = {"x": x, "y": y, "z": z}

    def near(axis, step):
        if axis == "x":
            return {"fsdp": lax.rem(x + step + 4, 4)}
        if axis == "y":
            return {"ctx": 4 * z + lax.rem(y + step + 4, 4)}
        return {"ctx": 4 * lax.rem(z + step + 4, 4) + y}

    mirror = {"y": {"fsdp": y, "ctx": 4 * z + x}, "z": {"fsdp": z, "ctx": 4 * x + y}}

    barrier = pltpu.get_barrier_semaphore()
    for k in range(1, 4):
        pl.semaphore_signal(
            barrier, inc=1, device_id={"fsdp": lax.rem(x + k, 4)}, device_id_type=MESH
        )
    for k in range(4):
        pl.semaphore_signal(
            barrier,
            inc=1,
            device_id={"section": 1 - section, "fsdp": lax.rem(x + k, 4)},
            device_id_type=MESH,
        )

    def greet(k, carry):
        pl.semaphore_signal(
            barrier, inc=1, device_id={"ctx": lax.rem(c + k, 16)}, device_id_type=MESH
        )
        return carry

    lax.fori_loop(1, 16, greet, 0)
    for axis in "yz":
        pl.semaphore_signal(barrier, inc=1, device_id=mirror[axis], device_id_type=MESH)
    pl.semaphore_wait(barrier, 24)

    def ahead(k):
        return lax.rem(x + k, 4)

    def behind(k):
        return lax.rem(x - k + 4, 4)

    def over_x(e, k, src, dst):
        return remote(src, dst, xs.at[e, k], xr.at[e, k], {"fsdp": ahead(k)})

    def over_c(e, to, src, dst):
        k = lax.rem(to - c + 16, 16)
        return remote(src, dst, cs.at[e, k], cr.at[e, k], {"ctx": to})

    def piece(e, i, d, src, dst, flip=False):
        device = {"fsdp": lax.rem(x + d + 4, 4)}
        if flip:
            device["section"] = 1 - section
        return remote(src, dst, xs.at[e, i], xr.at[e, i], device)

    def half(ref, b, n):
        return ref.at[part(128 * b + 64 * n, 64)]

    def gather(e, i, src, ref, flip=False):
        if i == 6:
            return piece(e, 6, 0, src, ref.at[my_rows], True)
        if i >= 4:
            place = half(ref, lax.rem(x + (3 if i == 4 else 1), 4), i - 4)
            return piece(e, i, 1 if i == 4 else -1, place, place)
        n = i % 2
        return piece(e, i, 1 if i < 2 else -1, half(src, 0, n), half(ref, x, n), flip)

    def gather_start(e, src, ref, flip=False):
        for i in (0, 3, 1, 2):
            gather(e, i, src, ref, flip).start()

    def gather_pass(e, src, ref):
        for i, n in ((0, 4), (3, 5)):
            gather(e, i, src, ref).wait_recv()
            gather(e, n, src, ref).start()
        for i in (1, 2):
            gather(e, i, src, ref).wait_recv()

    def gather_far(e, src, ref):
        for i in (4, 5):
            gather(e, i, src, ref).wait_recv()

    def gather_sent(e, src, ref, forwarded=True, started=True, flip=False):
        for i in (0, 1, 2, 3) if started else ():
            gather(e, i, src, ref, flip).wait_send()
        for i in (4, 5) if forwarded else ():
            gather(e, i, src, ref).wait_send()

    def total(e, i):
        n = (X_SUM1, X_SUM2, X_SUM3, X_SUM4).index(e) % 2
        to = (2, 2, 1, 3, 1, 3)[i]
        h = (0, 1, 1, 0, 0, 1)[i]
        src = psend.at[n, lax.rem(x + to, 4), pl.ds(64 * h, 64)]
        if i < 2:
            dst = relay_s.at[n, i]
        else:
            dst = prec.at[n, 0 if to == 1 else 1, pl.ds(64 * h, 64)]
        return piece(e, i, (1, -1, 1, -1, 1, -1)[i], src, dst)

    def total_pass(e):
        n = (X_SUM1, X_SUM2, X_SUM3, X_SUM4).index(e) % 2
        for i in (0, 1):
            total(e, i).wait_recv()
            b, rows = lax.rem(x + (1, 3)[i], 4), slice(64 * i, 64 * i + 64)
            psend[n, b, rows] = psend[n, b, rows] + relay_s[n, i]
            total(e, 4 + i).start()

    def total_take(e):
        n = (X_SUM1, X_SUM2, X_SUM3, X_SUM4).index(e) % 2
        for i in (2, 3, 4, 5):
            total(e, i).wait_recv()
        return own[...] + prec[n, 0].astype(F32) + prec[n, 1].astype(F32)

    def total_sent(e):
        for i in range(6):
            total(e, i).wait_send()

    def quarter(n):
        return (z, y)[n % 2]

    def weight(n, i):
        dst = (wqkv, wqkv, wgf, wuf)[n]
        cols = (pl.ds(0, 512), pl.ds(512, 512), pl.ds(0, 1024), pl.ds(0, 1024))[n]
        q = quarter(n)
        if i < 3:
            to = lax.rem(x + i + 1, 4)
            rows = part(96 * q, 96)
            if n < 2:
                src = wsend.at[to, rows, cols]
            else:
                src = (wg, wu)[n - 2].at[rows, part(1024 * to, 1024)]
            place = dst.at[pl.ds(pl.multiple_of(384 * x + 96 * q, 96), 96), cols]
            device = {"fsdp": to}
        else:
            b = lax.rem(x + 1 + i % 3, 4)
            step = (1, -1, 1, -1)[i // 3 - 1]
            if i < 9:
                rows = pl.ds(pl.multiple_of(384 * b + 96 * q, 96), 96)
            else:
                far, h = lax.rem(q - step + 4, 4), i // 3 - 3
                rows = pl.ds(pl.multiple_of(384 * b + 96 * far + 48 * h, 48), 48)
            src = place = dst.at[rows, cols]
            r = lax.rem(q + step + 4, 4)
            device = {"ctx": 4 * r + y if n % 2 == 0 else 4 * z + r}
        return remote(src, place, ws.at[n, i], wr.at[n, i], device)

    def fetch_to(n, b):
        i, q = lax.rem(b - x + 3, 4), quarter(n)
        cols = pl.ds(512 * n, 512)
        rows = pl.ds(pl.multiple_of(384 * x + 96 * q, 96), 96)
        src = wsend.at[b, part(96 * q, 96), cols]
        return remote(src, wqkv.at[rows, cols], ws.at[n, i], wr.at[n, i], {"fsdp": b})

    def weight_each(which, items, act):
        for i in items:
            for n in which:
                act(weight(n, i))

    def begin(copy):
        copy.start()

    def arrive(copy):
        copy.wait_recv()

    def leave(copy):
        copy.wait_send()

    def weight_fetch(which):
        weight_each(which, (1, 0, 2), begin)

    def weight_share(which):
        weight_each(which, range(3), arrive)
        weight_each(which, range(3, 9), begin)

    def weight_pass(which):
        for k in range(3):
            weight_each(which, (3 + k,), arrive)
            weight_each(which, (9 + k,), begin)
        for k in range(3):
            weight_each(which, (6 + k,), arrive)
            weight_each(which, (12 + k,), begin)

    def weight_wait(which):
        weight_each(which, range(9, 15), arrive)

    heads, wide = (0, 1), (2, 3)

    def gain_copy(k):
        return over_x(X_GAIN, k, gains, gain.at[:, part(384 * x, 384)])

    def pos_copy(k):
        return over_x(X_POS, k, pos, posx.at[x])

    pos[...] = jnp.broadcast_to(
        jnp.concatenate([positions[0:1, :], positions[1:2, :]], axis=1).astype(F32), (8, 128)
    )
    gains[...] = jnp.broadcast_to(norm_attn[...].astype(F32), (8, 384))
    gains[1:2, :] = norm_mlp[...].astype(F32)
    for k in (2, 1, 3):
        pos_copy(k).start()
        gain_copy(k).start()
    gain[:, part(384 * x, 384)] = gains[...]
    posx[x] = pos[...]

    def local_copies():
        yield pltpu.make_async_copy(
            wg.at[:, part(1024 * x, 1024)], wgf.at[part(384 * x, 384)], ls.at[0]
        )
        yield pltpu.make_async_copy(
            wu.at[:, part(1024 * x, 1024)], wuf.at[part(384 * x, 384)], ls.at[1]
        )
        yield pltpu.make_async_copy(wd_in, wd, ls.at[2])
        for h in range(4):
            yield pltpu.make_async_copy(
                wo_in.at[pl.ds(96 * h, 96)], wop.at[pl.ds(128 * h, 96)], ls.at[3 + h]
            )

    def head_columns(b, j, rows):
        w_q = wq[rows, 384 * b + 192 * j : 384 * b + 192 * j + 192]
        w_k = wk[rows, 96 * (2 * b + j) : 96 * (2 * b + j) + 96]
        w_v = wv[rows, 96 * (2 * b + j) : 96 * (2 * b + j) + 96]
        blank = jnp.zeros((w_v.shape[0], 32), BF)
        return jnp.concatenate(spread(w_q, (0, 1)) + spread(w_k, (0,)) + [w_v, blank], axis=1)

    for b in range(4):

        @pl.when(b != x)
        def _(b=b):
            for j in heads:
                rows = part(96 * quarter(j), 96)
                wsend[b, rows, 512 * j : 512 * j + 512] = head_columns(b, j, rows)

                @pl.when(first)
                def _(j=j):
                    fetch_to(j, b).start()

    @pl.when(first)
    def _():
        gather_start(X_IN, xin, xall)
        xall[my_rows, :] = xin[...]

    for b in range(4):

        @pl.when(b == x)
        def _(b=b):
            for j in heads:
                wqkv[384 * b : 384 * b + 384, 512 * j : 512 * j + 512] = head_columns(
                    b, j, slice(0, 384)
                )

    for copy in local_copies():
        copy.start()
    for h in range(4):
        wop[128 * h + 96 : 128 * h + 128, :] = jnp.zeros((32, WIDTH), BF)

    lane = lax.broadcasted_iota(jnp.int32, (1, 128), 1)
    sign = jnp.where(lane < 64, -1.0, 1.0)
    for k in (1, 3, 2):
        pos_copy(k).wait()
    for b in range(4):
        block = posx[b]
        posv[b, 0] = block
        posv[b, 1] = pltpu.roll(block, 64, 1)

    def pos_to(to):
        return over_c(C_POS, to, posv.at[to // 4, lax.rem(to, 4) // 2], posc.at[c])

    def send_pos(k, carry):
        pos_to(lax.rem(c + k, 16)).start()
        return carry

    lax.fori_loop(1, 16, send_pos, 0)
    posc[c] = posv[c // 4, lax.rem(c, 4) // 2]

    @pl.when(first)
    def _():
        weight_share(heads)

    for b in range(4):
        angle = as_column(posx[b][0:1, :]) * freq[0:1, :]
        cos_c[128 * b : 128 * b + 128, :] = jnp.cos(angle)
        sin_c[128 * b : 128 * b + 128, :] = jnp.sin(angle) * sign

    def tables():
        def await_pos(k, carry):
            pos_to(lax.rem(c + k, 16)).wait()
            return carry

        def table(i, carry):
            row = jnp.where(
                lane < 64, posc[2 * i][0:1, :], pltpu.roll(posc[2 * i + 1], 64, 1)[0:1, :]
            )
            block = part(128 * i, 128)
            posr[0:1, block] = row
            column = as_column(row)
            posk[block, :] = jnp.broadcast_to(column, (128, 128))
            angle = column * freq[0:1, :]
            cos_s[block, :] = jnp.cos(angle)
            sin_s[block, :] = jnp.sin(angle) * sign
            return carry

        lax.fori_loop(1, 16, await_pos, 0)
        lax.fori_loop(0, 8, table, 0)

    for k in (1, 3, 2):
        gain_copy(k).wait()

    @pl.when(first)
    def _():
        weight_pass(heads)
        gather_pass(X_IN, xin, xall)
        weight_fetch(wide)
        weight_wait(heads)

    @pl.when(second)
    def _():
        tables()
        gather_start(X_DY, dyin, dyf)
        dyf[my_rows, :] = dyin[...]
        gather_pass(X_DY, dyin, dyf)
        pl.semaphore_wait(go, 1)
        weight_fetch(heads + wide)
        weight_share(heads + wide)
        weight_pass(heads + wide)
        weight_wait(heads + wide)

    gain_attn, gain_mlp = gain[0:1, :], gain[1:2, :]

    def to_pair(ref, e, b, i, width, dst):
        src = ref.at[part(128 * b + 64 * (i // 2), 64), pl.ds(width * (i % 2), width)]
        return over_c(e, 4 * b + i, src, dst.at[part(64 * c, 64)])

    def in_order(n):
        return behind(jnp.where(n == 2, 3, jnp.where(n == 3, 2, n)))

    def project(n, carry):
        b = in_order(n)
        rows = part(128 * b, 128)

        @pl.when(jnp.logical_and(second, n == 0))
        def _():
            gather(X_IN, 6, out, xall).wait_recv()

        @pl.when(jnp.logical_and(second, n == 1))
        def _():
            gather_pass(X_IN, xin, xall)

        @pl.when(n == 3)
        def _():
            gather_far(X_IN, xin, xall)

        value = xall[rows, :].astype(F32)
        normed = (
            value
            * lax.rsqrt(jnp.mean(value * value, axis=-1, keepdims=True) + EPSILON)
            * gain_attn
        ).astype(BF)
        nf[rows, :] = normed
        u = mm(normed, wqkv[...])
        cosine, sine = cos_c[rows, :], sin_c[rows, :]
        for h in range(8):
            head = u[:, 128 * h : 128 * h + 128]
            if h % 4 != 3:
                head = turn(head, cosine, sine)
            qsend[rows, 128 * h : 128 * h + 128] = head.astype(BF)
        for i in range(4):

            @pl.when(4 * b + i != c)
            def _(i=i):
                to_pair(qsend, C_QKV, b, i, 512, qs).start()

            @pl.when(4 * b + i == c)
            def _(i=i):
                qs[part(64 * c, 64), :] = qsend[
                    part(128 * b + 64 * (i // 2), 64), 512 * (i % 2) : 512 * (i % 2) + 512
                ]

        return carry

    lax.fori_loop(0, 4, project, 0)

    @pl.when(first)
    def _():
        tables()

    weight_each(heads, range(3), leave)


    def await_qkv(k, carry):
        place = qs.at[part(64 * lax.rem(c - k + 16, 16), 64)]
        over_c(C_QKV, lax.rem(c + k, 16), place, place).wait_recv()
        return carry

    lax.fori_loop(1, 16, await_qkv, 0)

    @pl.when(first)
    def _():
        weight_share(wide)
        pl.semaphore_signal(go, inc=1, device_id={"section": 1}, device_id_type=MESH)

    vt[...] = qs[:, 384:512].T
    kt[...] = qs[:, 256:384].T

    def masked(q, cols):
        st = mm_nt(qs[:, 256:384], q)
        return jnp.where(posk[:, 0:1] <= posr[0:1, cols], st, -1e30)

    def att_place():
        return attp.at[part(64 * (c // 2), 64), part(256 * lax.rem(c, 2), 256)]

    def att_to(to):
        return over_c(C_ATT, to, osend.at[part(64 * to, 64)], att_place())

    def attend(n, carry):
        rows = part(256 * n, 256)

        for g in range(2):
            st = masked(qs[rows, 128 * g : 128 * g + 128], rows)
            top = jnp.max(st, axis=0, keepdims=True)
            e = jnp.exp2((st - top) * SCALE2)
            sums = jnp.sum(e, axis=0, keepdims=True)
            lse[g : g + 1, rows] = top * SCALE2 + jnp.log2(sums)
            result = mm(vt[...], e.astype(BF)) * (1.0 / sums)
            osend[rows, 128 * g : 128 * g + 128] = result.T.astype(BF)
        for i in range(4):
            to = 4 * n + i

            @pl.when(to != c)
            def _(to=to):
                att_to(to).start()

            @pl.when(to == c)
            def _(to=to):
                attp[part(64 * (c // 2), 64), part(256 * lax.rem(c, 2), 256)] = osend[
                    part(64 * to, 64), :
                ]

        return carry

    lax.fori_loop(0, 4, attend, 0)

    @pl.when(first)
    def _():
        weight_pass(wide)


    def await_att(b):
        for i in range(4):
            to = 4 * b + i

            @pl.when(to != c)
            def _(to=to, i=i):
                k = lax.rem(c - to + 16, 16)
                place = attp.at[part(64 * (2 * b + i // 2), 64), pl.ds(256 * (i % 2), 256)]
                remote(place, place, cs.at[C_ATT, k], cr.at[C_ATT, k], {"ctx": lax.rem(c + k, 16)}).wait_recv()

    def give(e, n, b, value):
        place = psend.at[(X_SUM1, X_SUM2, X_SUM3, X_SUM4).index(e) % 2, b]

        @pl.when(n < 3)
        def _():
            place[...] = value.astype(BF)

        @pl.when(n == 0)
        def _():
            total(e, 0).start()
            total(e, 1).start()

        @pl.when(n == 1)
        def _():
            total(e, 2).start()

        @pl.when(n == 2)
        def _():
            total(e, 3).start()
            total_pass(e)

        @pl.when(n == 3)
        def _():
            own[...] = value

    def far_first(n):
        return lax.rem(x + jnp.where(n == 0, 2, jnp.where(n == 1, 1, jnp.where(n == 2, 3, 0))), 4)

    def combine(n, carry):
        b = far_first(n)
        await_att(b)
        give(X_SUM1, n, b, mm(attp[part(128 * b, 128), :], wop[...]))
        return carry

    for copy in local_copies():
        copy.wait()
    lax.fori_loop(0, 4, combine, 0)
    middle = xall[my_rows, :].astype(F32) + total_take(X_SUM1)
    mid[...] = middle
    n2[my_rows, :] = (
        middle * lax.rsqrt(jnp.mean(middle * middle, axis=-1, keepdims=True) + EPSILON) * gain_mlp
    ).astype(BF)
    n2_own = n2.at[my_rows]
    gather_start(X_N2, n2_own, n2)

    @pl.when(first)
    def _():
        weight_wait(wide)

    def pair(blocks, ref):
        return jnp.concatenate([ref[part(128 * b, 128), :] for b in blocks], axis=0)

    def far_copy(d, b):
        return piece(X_SUM2, d, d, psend.at[1, b], prec3.at[d - 1])

    def feed(ds):
        blocks = [lax.rem(x + d, 4) for d in ds]
        a = pair(blocks, n2)
        ga, u = mm(a, wgf[...]), mm(a, wuf[...])
        h = (ga * (1.0 / (1.0 + jnp.exp(-ga))) * u).astype(BF)
        result = mm(h, wd[...])
        for n, (d, b) in enumerate(zip(ds, blocks)):
            rows, cut = part(128 * b, 128), slice(128 * n, 128 * n + 128)
            gate[rows, :] = ga[cut].astype(BF)
            up[rows, :] = u[cut].astype(BF)
            hidden[rows, :] = h[cut]
            if d == 0:
                own[...] = result[cut]
            else:
                psend[1, b] = result[cut].astype(BF)
                far_copy(d, b).start()

    gather_pass(X_N2, n2_own, n2)
    feed((1, 3))
    gather_far(X_N2, n2_own, n2)
    feed((2, 0))
    result = mid[...] + own[...]
    for d in (1, 3, 2):
        far_copy(d, lax.rem(x + d, 4)).wait_recv()
        result = result + prec3[d - 1].astype(F32)
    out[...] = result.astype(BF)

    @pl.when(first)
    def _():
        gather_sent(X_IN, xin, xall, forwarded=False)
        gather(X_IN, 6, out, xall).start()
        gather_start(X_IN, out, xall, True)

    held = dict(zip(ARRAYS, (h_gate, h_up, h_down, h_out, h_heads_a, h_heads_b)))

    def ring(name):
        axis, d = FLOWS[name][:2]
        other = "z" if axis == "y" else "y"
        return NAMES.index(name), axis, other, d, where[axis], where[other]

    def at(i, d, s):
        return lax.rem(i - d * s + 8, 4)

    def columns(name):
        return pl.ds(FLOWS[name][3], FLOWS[name][5])

    def place_of(name, g, p):
        return held[FLOWS[name][2]].at[g, p, :, columns(name)]

    def partial(name, g, p):
        array, cols = FLOWS[name][2], columns(name)
        if array == "down":
            return wd.at[part(256 * g + 64 * p, 64), cols]
        if array == "out":
            return wop.at[part(96 * g, 96), part(384 * p, 384)]
        rows = pl.ds(pl.multiple_of(384 * g + 96 * p, 96), 96)
        if name in LATE:
            return wqkv.at[rows, pl.ds(384 * LATE.index(name), 384)]
        return (wgf if array == "gate" else wuf).at[rows, cols]

    def arrival(name, s, q):
        n = 4 * (s - 1) + q
        array, cols = FLOWS[name][2], columns(name)
        if array == "gate":
            return wsend.at[s, part(96 * q, 96), cols]
        if array == "up":
            slot = wsend.at[3, part(96 * q, 96), cols]
            return slot if s == 0 else dgu.at[part(96 * n, 96), cols]
        if array == "down":
            return arrive_down.at[q, :, cols] if s == 0 else n2.at[part(64 * n, 64), cols]
        return arrive_out.at[s, q]

    def arrival2(name, s):
        array, cols = FLOWS[name][2], columns(name)
        if array in ("gate", "up"):
            return (gate if array == "gate" else up).at[part(96 * s, 96), cols]
        if array == "down":
            return prec3.at[s, pl.ds(0, 64), cols]
        return {"out": second_out, "heads_a": second_a, "heads_b": second_b}[array].at[s]

    def flow(name, n, src, dst, device):
        f = NAMES.index(name)
        return remote(src, dst, fs.at[f, n], fr.at[f, n], device)

    def copy_first(name, s, q):
        f, axis, other, d, i, j = ring(name)
        src = partial(name, at(i, d, 1 + s), at(j, d, 1 + q))
        return flow(name, 4 * s + q, src, arrival(name, s, q), near(axis, d))

    def copy_second(name, s):
        f, axis, other, d, i, j = ring(name)
        src = partial(name, i, at(j, d, 1 + s))
        return flow(name, 12 + s, src, arrival2(name, s), near(other, d))

    def copy_mirror(name):
        f, axis, other, d, i, j = ring(name)
        n = 6 if name in LATE else 15
        return flow(name, n, partial(name, i, j), place_of(name, x, j), mirror[axis])

    def copy_own(name):
        f, axis, other, d, i, j = ring(name)
        group = i if FLOWS[name][2] in ("down", "out") else x
        return pltpu.make_async_copy(partial(name, i, j), place_of(name, group, j), os.at[f])

    def copy_small(name, s):
        f, axis, other, d, i, j = ring(name)
        place = place_of(name, i, at(j, d, s))
        return flow(name, 16 + s, place, place, near(other, d))

    def copy_big(name, s, q):
        f, axis, other, d, i, j = ring(name)
        place = place_of(name, at(i, d, s), at(j, d, q))
        return flow(name, 20 + 4 * s + q, place, place, near(axis, d))

    def first_start(names):
        def body(q, carry):
            for name in names:
                copy_first(name, 0, q).start()
            return carry

        lax.fori_loop(0, 4, body, 0)

    def first_step(names, s):
        def body(q, carry):
            for name in names:
                f, axis, other, d, i, j = ring(name)
                copy_first(name, s, q).wait_recv()
                place = partial(name, at(i, d, 2 + s), at(j, d, 1 + q))
                place[...] = place[...] + arrival(name, s, q)[...]
                if s < 2:
                    copy_first(name, s + 1, q).start()
                else:

                    @pl.when(q == 0)
                    def _(name=name):
                        copy_second(name, 0).start()

            return carry

        lax.fori_loop(0, 4, body, 0)

    def second_step(names, s):
        for name in names:
            f, axis, other, d, i, j = ring(name)
            copy_second(name, s).wait_recv()
            place = partial(name, i, at(j, d, 2 + s))
            place[...] = place[...] + arrival2(name, s)[...]
            if s < 2:
                copy_second(name, s + 1).start()

    def mirror_step(names, act):
        for name in names:
            if FLOWS[name][2] in ("down", "out"):
                act(copy_own(name))
                continue
            axis = FLOWS[name][0]

            @pl.when(where[axis] != x)
            def _(name=name):
                act(copy_mirror(name))

            @pl.when(where[axis] == x)
            def _(name=name):
                act(copy_own(name))

    def finish_copy(copy):
        copy.wait()

    def small_step(names, q):
        for name in names:
            if q > 0:
                copy_small(name, q - 1).wait_recv()
            if q < 3:
                copy_small(name, q).start()
        for name in names:
            copy_big(name, 0, q).start()

    def big_step(names, s, low, high):
        def body(q, carry):
            for name in names:
                copy_big(name, s, q).wait_recv()
                if s < 2:
                    copy_big(name, s + 1, q).start()
            return carry

        lax.fori_loop(low, high, body, 0)

    def gain_sum_copy(n, k):
        axis = "xyz"[n]
        if n == 0:
            src = ggain.at[:, part(lax.rem(x + k, 4) * 384, 384)]
        else:
            src = gain_in.at[n, 0]
        return remote(src, gain_in.at[n, k], gs.at[n, k], gr.at[n, k], near(axis, k))

    def gain_start(n):
        for k in (1, 2, 3):
            gain_sum_copy(n, k).start()

    def gain_sum(n):
        mine = ggain[:, part(x * 384, 384)] if n == 0 else gain_in[n, 0]
        for k in (1, 2, 3):
            gain_sum_copy(n, k).wait()
        return mine + gain_in[n, 1] + gain_in[n, 2] + gain_in[n, 3]

    def late(name, n):
        f, axis, other, d, i, j = ring(name)
        cols = pl.ds(384 * LATE.index(name), 384)
        k = (n if n < 6 else n - 1) % 3 + 1
        if n < 3:
            src = wqkv.at[part(384 * lax.rem(i + k, 4), 384), cols]
            return flow(name, n, src, (arrive_a, arrive_b)[LATE.index(name)].at[k - 1], near(axis, k))
        if n < 6:
            src = partial(name, i, lax.rem(j + k, 4))
            return flow(name, n, src, arrival2(name, k - 1), near(other, k))
        if n < 10:
            place = held[name].at[i, j]
            return flow(name, n, place, place, near(other, k))
        place = held[name].at[i]
        return flow(name, n, place, place, near(axis, k))

    def late_each(items, act):
        for n in items:
            for name in LATE:
                act(late(name, n))

    def late_first():
        late_each(range(3), arrive)
        for name in LATE:
            f, axis, other, d, i, j = ring(name)
            rows, cols = part(384 * i, 384), pl.ds(384 * LATE.index(name), 384)
            got = (arrive_a, arrive_b)[LATE.index(name)]
            sums = wqkv[rows, cols].astype(F32)
            for k in range(3):
                sums = sums + got[k].astype(F32)
            wqkv[rows, cols] = sums.astype(BF)
        late_each(range(3, 6), begin)

    def late_second():
        late_each(range(3, 6), arrive)
        for name in LATE:
            f, axis, other, d, i, j = ring(name)
            place = partial(name, i, j)
            sums = place[...].astype(F32)
            for k in range(3):
                sums = sums + arrival2(name, k)[...].astype(F32)
            place[...] = sums.astype(BF)
        mirror_step(LATE, begin)

    def late_small():
        mirror_step(LATE, finish_copy)
        late_each(range(7, 10), begin)

    def late_big():
        late_each(range(7, 10), arrive)
        late_each(range(10, 13), begin)

    def feed_grads(s, carry):
        rows = part(384 * at(y, 1, 1 + s), 384)
        wgf[rows, :] = mm_tn(n2[:, rows], dgu[0:512, :]).astype(BF)
        rows = part(384 * at(y, -1, 1 + s), 384)
        wuf[rows, :] = mm_tn(n2[:, rows], dgu[512:1024, :]).astype(BF)
        rows = part(256 * at(z, 1, 1 + s), 256)
        wd[rows, :] = mm_tn(hidden[:, rows], dyf[...]).astype(BF)

        @pl.when(s == 0)
        def _():
            first_start(("gate", "up", "down"))

        return carry

    @pl.when(first)
    def _():
        gather_pass(X_DY, dx, dyf)
        gather(X_DY, 6, dx, dyf).wait_recv()

    gather_far(X_DY, dx, dyf)

    def feed_back(ds):
        blocks = [lax.rem(x + d, 4) for d in ds]
        dh = mm_nt(pair(blocks, dyf), wd[...])
        ga, u = pair(blocks, gate).astype(F32), pair(blocks, up).astype(F32)
        s = 1.0 / (1.0 + jnp.exp(-ga))
        dga = (dh * u * (s * (1.0 + ga * (1.0 - s)))).astype(BF)
        du = (dh * (ga * s)).astype(BF)
        result = mm_nt(dga, wgf[...]) + mm_nt(du, wuf[...])
        for n, (d, b) in enumerate(zip(ds, blocks)):
            rows, cut = part(128 * b, 128), slice(128 * n, 128 * n + 128)
            dgu[rows, :] = dga[cut]
            dgu[part(512 + 128 * b, 128), :] = du[cut]
            if d == 0:
                own[...] = result[cut]
            else:
                psend[0, b] = result[cut].astype(BF)
                for i in {2: (0, 1), 1: (2,), 3: (3,)}[d]:
                    total(X_SUM3, i).start()

    total_sent(X_SUM1)
    feed_back((2, 1))
    feed_back((3, 0))
    total_pass(X_SUM3)
    weight_each(heads, range(3, 15), leave)
    weight_each(wide, range(15), leave)
    gather_sent(X_N2, n2_own, n2)
    gather_sent(X_DY, dyin, dyf, started=False)
    for d in (1, 2, 3):
        far_copy(d, lax.rem(x + d, 4)).wait_send()
    lax.fori_loop(0, 4, feed_grads, 0)
    first_start(("gate_rest", "up_rest", "down_rest"))
    def norm_back(value, grad, gain_row):
        r = lax.rsqrt(jnp.mean(value * value, axis=-1, keepdims=True) + EPSILON)
        unit = value * r
        t = grad * gain_row
        back = r * (t - unit * jnp.mean(t * unit, axis=-1, keepdims=True))
        return back, jnp.sum(grad * unit, axis=0, keepdims=True)

    back, g_mlp = norm_back(mid[...], total_take(X_SUM3), gain_mlp)
    dmid = dyf[my_rows, :].astype(F32) + back
    mid[...] = dmid
    ggain[...] = jnp.zeros_like(ggain)
    ggain[1:2, :] = g_mlp
    dbr[my_rows, :] = dmid.astype(BF)
    dbr_own = dbr.at[my_rows]
    gather_start(X_DBR, dbr_own, dbr)

    def branch(n, carry):
        b = in_order(n)
        rows = part(128 * b, 128)

        @pl.when(n == 1)
        def _():
            gather_pass(X_DBR, dbr_own, dbr)

        @pl.when(n == 3)
        def _():
            gather_far(X_DBR, dbr_own, dbr)

        dsend[rows, :] = mm_nt(dbr[rows, :], wop[...]).astype(BF)
        for i in range(4):

            @pl.when(4 * b + i != c)
            def _(i=i):
                to_pair(dsend, C_DATT, b, i, 256, das).start()

            @pl.when(4 * b + i == c)
            def _(i=i):
                das[part(64 * c, 64), :] = dsend[
                    part(128 * b + 64 * (i // 2), 64), 256 * (i % 2) : 256 * (i % 2) + 256
                ]

        return carry

    lax.fori_loop(0, 4, branch, 0)
    for n in range(2):
        rows = slice(256 * n, 256 * n + 256)
        att[rows, :] = jnp.concatenate(
            [attp[rows, 128 * h : 128 * h + 96] for h in range(4)], axis=1
        )
    wop[0:384, :] = mm_tn(att[...], dbr[...]).astype(BF)
    first_start(("out",))

    def await_das(k, carry):
        place = das.at[part(64 * lax.rem(c - k + 16, 16), 64)]
        over_c(C_DATT, lax.rem(c + k, 16), place, place).wait_recv()
        return carry

    lax.fori_loop(1, 16, await_das, 0)
    first_step(EARLY, 0)
    dk[...] = jnp.zeros_like(dk)
    dv[...] = jnp.zeros_like(dv)

    def grad_place(h):
        return dqp.at[part(64 * (c // 2), 64), part(512 * lax.rem(c, 2) + 256 * h, 256)]

    def grad_to(e, to):
        h = e - C_DQ
        return over_c(e, to, dqs.at[part(64 * to, 64), pl.ds(256 * h, 256)], grad_place(h))

    def attend_back(n, carry):
        rows = part(256 * n, 256)
        for g in range(2):
            cols = slice(128 * g, 128 * g + 128)
            q, da = qs[rows, cols], das[rows, cols]
            p = jnp.exp2(masked(q, rows) * SCALE2 - lse[g : g + 1, rows])
            dp = mm_nt(qs[:, 384:512], da)
            dv[...] += mm(p.astype(BF), da)
            ds = (p * (dp - jnp.sum(p * dp, axis=0, keepdims=True))).astype(BF)
            dk[...] += mm(ds, q)
            dq = mm(kt[...], ds).T * SCALE
            dqs[rows, cols] = turn(dq, cos_s[rows, :], -sin_s[rows, :]).astype(BF)
        for i in range(4):
            to = 4 * n + i

            @pl.when(to != c)
            def _(to=to):
                grad_to(C_DQ, to).start()

            @pl.when(to == c)
            def _(to=to):
                grad_place(0)[...] = dqs[part(64 * to, 64), 0:256]

        return carry

    lax.fori_loop(0, 4, attend_back, 0)
    dqs[:, 256:384] = turn(dk[...] * SCALE, cos_s[...], -sin_s[...]).astype(BF)
    dqs[:, 384:512] = dv[...].astype(BF)

    def send_dkv(k, carry):
        grad_to(C_DKV, lax.rem(c + k, 16)).start()
        return carry

    lax.fori_loop(1, 16, send_dkv, 0)
    grad_place(1)[...] = dqs[part(64 * c, 64), 256:512]
    first_step(EARLY, 1)

    def await_dqkv(b):
        for i in range(4):
            to = 4 * b + i

            @pl.when(to != c)
            def _(to=to, i=i):
                k = lax.rem(c - to + 16, 16)
                for h in range(2):
                    place = dqp.at[
                        part(64 * (2 * b + i // 2), 64), pl.ds(512 * (i % 2) + 256 * h, 256)
                    ]
                    e = C_DQ + h
                    remote(
                        place, place, cs.at[e, k], cr.at[e, k], {"ctx": lax.rem(c + k, 16)}
                    ).wait_recv()

    def input_grad(n, carry):
        b = far_first(n)
        await_dqkv(b)
        give(X_SUM4, n, b, mm_nt(dqp[part(128 * b, 128), :], wqkv[...]))
        return carry

    lax.fori_loop(0, 4, input_grad, 0)
    @pl.when(first)
    def _():
        first_step(EARLY, 2)

    for n in range(2):
        rows = slice(256 * n, 256 * n + 256)
        pieces = []
        for h in range(8):
            if h % 4 == 3:
                pieces.append(dqp[rows, 128 * h : 128 * h + 96])
            else:
                pieces.append(dqp[rows, 128 * h : 128 * h + 48])
                pieces.append(dqp[rows, 128 * h + 64 : 128 * h + 112])
        dqkv[rows, :] = jnp.concatenate(pieces, axis=1)

    def head_grads(g, carry):
        rows = part(384 * g, 384)
        wqkv[rows, 0:768] = mm_tn(nf[:, rows], dqkv[...]).astype(BF)
        return carry

    lax.fori_loop(0, 4, head_grads, 0)
    late_each(range(3), begin)
    back, g_attn = norm_back(xall[my_rows, :].astype(F32), total_take(X_SUM4), gain_attn)
    dx[...] = (mid[...] + back).astype(BF)
    ggain[0:1, :] = g_attn

    @pl.when(second)
    def _():
        gather_sent(X_DY, dyin, dyf, forwarded=False)
        gather(X_DY, 6, dx, dyf).start()
        gather_start(X_DY, dx, dyf, True)

    gain_start(0)

    @pl.when(second)
    def _():
        first_step(EARLY, 2)

    second_step(EARLY, 0)
    gain_in[1, 0] = gain_sum(0)
    gain_start(1)
    second_step(EARLY, 1)
    late_first()
    second_step(EARLY, 2)
    mirror_step(EARLY, begin)
    gain_in[2, 0] = gain_sum(1)
    gain_start(2)
    late_second()
    mirror_step(EARLY, finish_copy)
    small_step(EARLY, 0)
    late_small()
    small_step(EARLY, 1)
    late_big()
    small_step(EARLY, 2)
    small_step(EARLY, 3)
    for n in range(3):
        big_step(EARLY, n, 0, 4)
    late_each(range(10, 13), arrive)
    o_gain[...] = gain_sum(2)

    def sent_c(k, carry):
        to = lax.rem(c + k, 16)
        place = qs.at[part(64 * to, 64)]
        over_c(C_QKV, to, place, place).wait_send()
        att_to(to).wait_send()
        place = das.at[part(64 * to, 64)]
        over_c(C_DATT, to, place, place).wait_send()
        grad_to(C_DQ, to).wait_send()
        grad_to(C_DKV, to).wait_send()
        return carry

    lax.fori_loop(1, 16, sent_c, 0)
    total_sent(X_SUM3)
    total_sent(X_SUM4)
    gather_sent(X_DBR, dbr_own, dbr)
    gather_sent(X_IN, xin, xall, started=False)

    def sent_first(q, carry):
        for name in EARLY:
            for n in range(3):
                copy_first(name, n, q).wait_send()
                copy_big(name, n, q).wait_send()
        return carry

    lax.fori_loop(0, 4, sent_first, 0)
    late_each((0, 1, 2, 3, 4, 5, 7, 8, 9, 10, 11, 12), leave)
    for name in EARLY:
        for n in range(3):
            copy_second(name, n).wait_send()
            copy_small(name, n).wait_send()

    @pl.when(first)
    def _():
        gather_sent(X_IN, xin, xall, forwarded=False)
        gather(X_IN, 6, out, xall).wait_send()

    @pl.when(second)
    def _():
        gather_sent(X_DY, dyin, dyf, forwarded=False)
        gather(X_DY, 6, dx, dyf).wait_send()


def run_layer(xin, dyin, positions, freq, norm_attn, norm_mlp, wq, wk, wv, wo, wd, wg, wu, cid):
    vm = pl.BlockSpec(memory_space=pltpu.VMEM)
    hbm = pl.BlockSpec(memory_space=pl.ANY)
    dma = pltpu.SemaphoreType.DMA
    shapes = [
        ((128, WIDTH), BF),
        ((128, WIDTH), BF),
        *(((4, 4) + shape, BF) for shape in ARRAYS.values()),
        ((8, 384), F32),
    ]
    scratch = [
        ((512, WIDTH), BF),
        ((2, 512, WIDTH), BF),
        ((1024, 1024), BF),
        ((512, 768), BF),
        ((512, 384), BF),
        ((512, WIDTH), BF),
        ((512, 1024), BF),
        ((8, WIDTH), F32),
        ((4, 64, WIDTH), BF),
        ((3, 4, 96, 384), BF),
        *(((3, 384, 384), BF),) * 2,
        *(((3, 96, 384), BF),) * 3,
        ((3, 4, 8, 384), F32),
        ((4, 384, 1024), BF),
        ((WIDTH, 1024), BF),
        ((WIDTH, 1024), BF),
        ((WIDTH, 1024), BF),
        ((512, WIDTH), BF),
        ((1024, WIDTH), BF),
        ((2, 2, 64, WIDTH), BF),
        ((512, WIDTH), BF),
        ((8, 384), F32),
        ((8, 128), F32),
        ((8, WIDTH), F32),
        ((4, 8, 128), F32),
        ((4, 2, 8, 128), F32),
        ((16, 8, 128), F32),
        ((8, 1024), F32),
        ((1024, 128), F32),
        ((512, 128), F32),
        ((512, 128), F32),
        ((1024, 128), F32),
        ((1024, 128), F32),
        ((512, 1024), BF),
        ((1024, 512), BF),
        ((128, 1024), BF),
        ((128, 1024), BF),
        ((8, 1024), F32),
        ((1024, 256), BF),
        ((512, 512), BF),
        ((128, WIDTH), F32),
        ((512, 1024), BF),
        ((512, 1024), BF),
        ((128, WIDTH), F32),
        ((2, 4, 128, WIDTH), BF),
        ((2, 2, 128, WIDTH), BF),
        ((3, 128, WIDTH), BF),
        ((512, 512), BF),
        ((1024, 256), BF),
        ((1024, 128), F32),
        ((1024, 128), F32),
        ((1024, 512), BF),
        ((512, 1024), BF),
    ]
    return pl.pallas_call(
        layer_kernel,
        out_shape=[jax.ShapeDtypeStruct(s, d) for s, d in shapes],
        in_specs=[vm] * 9 + [hbm] * 4,
        out_specs=[vm] * 2 + [hbm] * len(ARRAYS) + [vm],
        scratch_shapes=[pltpu.VMEM(s, d) for s, d in scratch]
        + [dma((13, 7)), dma((13, 7)), dma((6, 16)), dma((6, 16)), dma((4, 15)), dma((4, 15)), dma((7,)), pltpu.SemaphoreType.REGULAR]
        + [dma((9, 32)), dma((9, 32)), dma((3, 4)), dma((3, 4)), dma((9,))],
        name="layer",
        compiler_params=pltpu.CompilerParams(
            collective_id=cid, has_side_effects=True, vmem_limit_bytes=63 << 20
        ),
    )(xin, dyin, positions, freq, norm_attn, norm_mlp, wq, wk, wv, wo, wd, wg, wu)


def local(
    inputs,
    positions,
    out_grad,
    norm_attn,
    w_query,
    key_weight,
    value_weight,
    output_weight,
    norm_mlp,
    w_gate,
    w_up,
    w_down,
):
    lane = np.arange(128)
    index = np.where(lane < 64, lane, lane - 64)
    freq = np.where(index < 48, THETA ** (-2.0 * index / HEAD_SIZE), 0.0).astype(np.float32)
    freq = jnp.asarray(np.broadcast_to(freq[None], (8, 128)))
    out, dx, *summed, g_gain = run_layer(
        inputs.reshape(128, WIDTH),
        out_grad.reshape(128, WIDTH),
        positions,
        freq,
        norm_attn,
        norm_mlp,
        w_query[0],
        key_weight[0],
        value_weight[0],
        output_weight[0],
        w_down[0],
        w_gate[0],
        w_up[0],
        0,
    )
    g_gate, g_up, g_query, g_key, g_value, g_out, g_down, g_attn, g_mlp = widen(*summed, g_gain)
    return (
        out.reshape(1, 2, 64, WIDTH),
        dx.reshape(1, 2, 64, WIDTH),
        g_attn,
        g_query[None],
        g_key[None],
        g_value[None],
        g_out[None],
        g_mlp,
        g_gate[None],
        g_up[None],
        g_down[None],
    )


def solution(mesh):
    rows = P("section", "fsdp", None)
    return jax.shard_map(
        local,
        mesh=mesh,
        in_specs=(
            P("fsdp", "ctx", None),
            P("fsdp", "ctx"),
            P("fsdp", "ctx", None),
            P("section", "fsdp"),
            rows,
            rows,
            rows,
            rows,
            P("section", "fsdp"),
            rows,
            rows,
            rows,
        ),
        out_specs=(
            P("section", "fsdp", "ctx", None),
            P("section", "fsdp", "ctx", None),
            P("section", "fsdp"),
            rows,
            rows,
            rows,
            rows,
            P("section", "fsdp"),
            rows,
            rows,
            rows,
        ),
        check_vma=False,
    )
```

```python
import jax
import jax.numpy as jnp
from jax import lax
from jax.experimental import pallas as pl
from jax.experimental.pallas import tpu as pltpu
from jax.sharding import PartitionSpec as P

QUERY_HEADS = 16
KEY_VALUE_HEADS = 8
HEAD_SIZE = 96
WIDTH = 1536
FF = 4096
THETA = 100000.0
EPSILON = 1e-05
MESH = pl.DeviceIdType.MESH
N_X = 4
N_C = 16
BF = jnp.bfloat16
F32 = jnp.float32


def mm(a, b):
    return jnp.dot(a, b, preferred_element_type=F32)


def mm_tn(a, b):
    return lax.dot_general(a, b, (((0,), (0,)), ((), ())), preferred_element_type=F32)


def mm_nt(a, b):
    return lax.dot_general(a, b, (((1,), (1,)), ((), ())), preferred_element_type=F32)


def remote(src, dst, send, recv, device):
    return pltpu.make_async_remote_copy(
        src_ref=src, dst_ref=dst, send_sem=send, recv_sem=recv, device_id=device, device_id_type=MESH
    )


def part(start, size):
    return pl.ds(pl.multiple_of(start, size), size)


def widen_kernel(w_gate, w_up, w_down, w_out, w_a, w_b, gains, gate, up, query, key, value, g_out, g_down, g_attn, g_mlp):
    g_attn[...] = gains[0:1, :]
    g_mlp[...] = gains[1:2, :]
    g_down[...] = w_down[...].astype(F32)
    keys, values = [], []
    for x in range(N_X):
        gate[:, 1024 * x : 1024 * x + 1024] = w_gate[x, 0].astype(F32)
        up[:, 1024 * x : 1024 * x + 1024] = w_up[x, 0].astype(F32)
        g_out[:, 384 * x : 384 * x + 384] = w_out[0, x].astype(F32)
        a, b = w_a[x, 0].astype(F32), w_b[x, 0].astype(F32)
        query[:, 384 * x : 384 * x + 384] = jnp.concatenate([a[:, :192], b[:, :192]], axis=1)
        keys += [a[:, 192:288], b[:, 192:288]]
        values += [a[:, 288:], b[:, 288:]]
    key[...] = jnp.concatenate(keys, axis=1)
    value[...] = jnp.concatenate(values, axis=1)


def widen(gate, up, down, out, heads_a, heads_b, gains):
    steps = 8

    def spec(r, cols):
        return pl.BlockSpec((r, cols), lambda i: (i, 0))

    def shape(r, cols):
        return jax.ShapeDtypeStruct((r, cols), F32)

    def blocks(cols):
        return pl.BlockSpec((4, 1, 48, cols), lambda i: (0, i // 2, i % 2, 0))

    return pl.pallas_call(
        widen_kernel,
        grid=(steps,),
        out_shape=[
            shape(384, FF),
            shape(384, FF),
            shape(384, 1536),
            shape(384, 768),
            shape(384, 768),
            shape(384, 1536),
            shape(1024, 1536),
            shape(1, 384),
            shape(1, 384),
        ],
        in_specs=[
            blocks(1024),
            blocks(1024),
            spec(128, 1536),
            pl.BlockSpec((1, 4, 48, 384), lambda i: (i // 2, 0, i % 2, 0)),
            blocks(384),
            blocks(384),
            pl.BlockSpec((8, 384), lambda i: (0, 0)),
        ],
        out_specs=[
            spec(48, FF),
            spec(48, FF),
            spec(48, 1536),
            spec(48, 768),
            spec(48, 768),
            spec(48, 1536),
            spec(128, 1536),
            pl.BlockSpec((1, 384), lambda i: (0, 0)),
            pl.BlockSpec((1, 384), lambda i: (0, 0)),
        ],
        name="widen",
        compiler_params=pltpu.CompilerParams(vmem_limit_bytes=60 << 20),
    )(gate, up, down.reshape(1024, 1536), out, heads_a, heads_b, gains)


X_GAIN, X_POS, X_IN, X_DY, X_QKV, X_GATE, X_UP, X_SUM1, X_N2, X_SUM2, X_SUM3, X_DBR, X_SUM4 = range(13)
C_POS, C_QKV, C_ATT, C_DATT, C_DQ, C_DKV = range(6)
SCALE = HEAD_SIZE ** (-0.5)
SCALE2 = SCALE * 1.4426950408889634
STEP2 = -2.0 / HEAD_SIZE * 16.609640474436812
FLOWS = {
    "gate": ("y", 1, "gate", 0, 96, 896),
    "up": ("y", -1, "up", 0, 96, 896),
    "down": ("z", 1, "down", 0, 64, 1280),
    "out": ("z", -1, "out", 0, 96, 384),
    "gate_rest": ("z", -1, "gate", 896, 96, 128),
    "up_rest": ("z", -1, "up", 896, 96, 128),
    "down_rest": ("z", -1, "down", 1280, 64, 256),
    "heads_a": ("y", 1, "heads_a", 0, 96, 384),
    "heads_b": ("z", -1, "heads_b", 0, 96, 384),
}
ARRAYS = {
    "gate": (96, 1024),
    "up": (96, 1024),
    "down": (64, 1536),
    "out": (96, 384),
    "heads_a": (96, 384),
    "heads_b": (96, 384),
}
NAMES = list(FLOWS)
EARLY, LATE = NAMES[:7], NAMES[7:]
STAY = ("down", "out", "down_rest")


def spread(w, heads):
    blank = jnp.zeros((w.shape[0], 16), w.dtype)
    pieces = []
    for h in heads:
        pieces += [w[:, 96 * h : 96 * h + 48], blank, w[:, 96 * h + 48 : 96 * h + 96], blank]
    return pieces


def as_column(row):
    eye = lax.broadcasted_iota(jnp.int32, (128, 128), 0) == lax.broadcasted_iota(
        jnp.int32, (128, 128), 1
    )
    return jnp.sum(jnp.where(eye, jnp.broadcast_to(row, (128, 128)), 0.0), axis=1, keepdims=True)


def turn(u, cosine, sine):
    return u * cosine + pltpu.roll(u, 64, 1) * sine


def layer_kernel(
    xin,
    dyin,
    positions,
    norm_attn,
    norm_mlp,
    wq,
    wk,
    wv,
    wo_in,
    wd_in,
    wg,
    wu,
    out,
    dx,
    h_gate,
    h_up,
    h_down,
    h_out,
    h_heads_a,
    h_heads_b,
    o_gain,
    nf,
    rows2,
    dgu,
    dqkv,
    att,
    dbr,
    hidden,
    ggain,
    arrive_down,
    arrive_out,
    arrive_a,
    arrive_b,
    second_out,
    second_a,
    second_b,
    gain_in,
    wsend,
    wqkv,
    wgf,
    wuf,
    wop,
    wd,
    relay_s,
    xall,
    gains,
    pos,
    gain,
    posx,
    posv,
    posc,
    posr,
    posk,
    cos_c,
    sin_c,
    cos_s,
    sin_s,
    qsend,
    qs,
    vt,
    kt,
    lse,
    osend,
    attp,
    mid,
    gate,
    up,
    own,
    psend,
    prec,
    prec3,
    dsend,
    das,
    dk,
    dv,
    dqs,
    dqp,
    xs,
    xr,
    cs,
    cr,
    ws,
    wr,
    ls,
    go,
    fs,
    fr,
    gs,
    gr,
    os,
):
    section = lax.axis_index("section")
    x = lax.axis_index("fsdp")
    c = lax.axis_index("ctx")
    y, z = lax.rem(c, 4), c // 4
    first, second = section == 0, section == 1
    my_rows = part(128 * x, 128)
    n2, dyf = rows2.at[0], rows2.at[1]
    where = {"x": x, "y": y, "z": z}

    def near(axis, step):
        if axis == "x":
            return {"fsdp": lax.rem(x + step + 4, 4)}
        if axis == "y":
            return {"ctx": 4 * z + lax.rem(y + step + 4, 4)}
        return {"ctx": 4 * lax.rem(z + step + 4, 4) + y}


    barrier = pltpu.get_barrier_semaphore()
    for k in range(1, 4):
        pl.semaphore_signal(
            barrier, inc=1, device_id={"fsdp": lax.rem(x + k, 4)}, device_id_type=MESH
        )
    for k in range(4):
        pl.semaphore_signal(
            barrier,
            inc=1,
            device_id={"section": 1 - section, "fsdp": lax.rem(x + k, 4)},
            device_id_type=MESH,
        )

    def greet(k, carry):
        pl.semaphore_signal(
            barrier, inc=1, device_id={"ctx": lax.rem(c + k, 16)}, device_id_type=MESH
        )
        return carry

    lax.fori_loop(1, 16, greet, 0)
    pl.semaphore_wait(barrier, 22)

    def ahead(k):
        return lax.rem(x + k, 4)

    def behind(k):
        return lax.rem(x - k + 4, 4)

    def over_x(e, k, src, dst):
        return remote(src, dst, xs.at[e, k], xr.at[e, k], {"fsdp": ahead(k)})

    def over_c(e, to, src, dst):
        k = lax.rem(to - c + 16, 16)
        return remote(src, dst, cs.at[e, k], cr.at[e, k], {"ctx": to})

    def piece(e, i, d, src, dst, flip=False):
        device = {"fsdp": lax.rem(x + d + 4, 4)}
        if flip:
            device["section"] = 1 - section
        return remote(src, dst, xs.at[e, i], xr.at[e, i], device)

    def half(ref, b, n):
        return ref.at[part(128 * b + 64 * n, 64)]

    def gather(e, i, src, ref, flip=False):
        if i == 6:
            return piece(e, 6, 0, src, ref.at[my_rows], True)
        if i >= 4:
            place = half(ref, lax.rem(x + (3 if i == 4 else 1), 4), i - 4)
            return piece(e, i, 1 if i == 4 else -1, place, place)
        n = i % 2
        return piece(e, i, 1 if i < 2 else -1, half(src, 0, n), half(ref, x, n), flip)

    def gather_start(e, src, ref, flip=False):
        for i in (0, 3, 1, 2):
            gather(e, i, src, ref, flip).start()

    def gather_pass(e, src, ref):
        for i, n in ((0, 4), (3, 5)):
            gather(e, i, src, ref).wait_recv()
            gather(e, n, src, ref).start()
        for i in (1, 2):
            gather(e, i, src, ref).wait_recv()

    def gather_far(e, src, ref):
        for i in (4, 5):
            gather(e, i, src, ref).wait_recv()

    def gather_sent(e, src, ref, forwarded=True, started=True, flip=False):
        for i in (0, 1, 2, 3) if started else ():
            gather(e, i, src, ref, flip).wait_send()
        for i in (4, 5) if forwarded else ():
            gather(e, i, src, ref).wait_send()

    def total(e, i):
        n = (X_SUM1, X_SUM2, X_SUM3, X_SUM4).index(e) % 2
        to = (2, 2, 1, 3, 1, 3)[i]
        h = (0, 1, 1, 0, 0, 1)[i]
        src = psend.at[n, lax.rem(x + to, 4), pl.ds(64 * h, 64)]
        if i < 2:
            dst = relay_s.at[n, i]
        else:
            dst = prec.at[n, 0 if to == 1 else 1, pl.ds(64 * h, 64)]
        return piece(e, i, (1, -1, 1, -1, 1, -1)[i], src, dst)

    def total_pass(e):
        n = (X_SUM1, X_SUM2, X_SUM3, X_SUM4).index(e) % 2
        for i in (0, 1):
            total(e, i).wait_recv()
            b, rows = lax.rem(x + (1, 3)[i], 4), slice(64 * i, 64 * i + 64)
            psend[n, b, rows] = psend[n, b, rows] + relay_s[n, i]
            total(e, 4 + i).start()

    def total_take(e):
        n = (X_SUM1, X_SUM2, X_SUM3, X_SUM4).index(e) % 2
        for i in (2, 3, 4, 5):
            total(e, i).wait_recv()
        return own[...] + prec[n, 0].astype(F32) + prec[n, 1].astype(F32)

    def total_sent(e):
        for i in range(6):
            total(e, i).wait_send()

    def quarter(n):
        return (z, y)[n % 2]

    def weight(n, i):
        dst = (wqkv, wqkv, wgf, wuf)[n]
        cols = (pl.ds(0, 512), pl.ds(512, 512), pl.ds(0, 1024), pl.ds(0, 1024))[n]
        q = quarter(n)
        if i < 3:
            to = lax.rem(x + i + 1, 4)
            rows = part(96 * q, 96)
            if n < 2:
                src = wsend.at[to, rows, cols]
            else:
                src = (wg, wu)[n - 2].at[rows, part(1024 * to, 1024)]
            place = dst.at[pl.ds(pl.multiple_of(384 * x + 96 * q, 96), 96), cols]
            device = {"fsdp": to}
        else:
            b = lax.rem(x + 1 + i % 3, 4)
            step = (1, -1, 1, -1)[i // 3 - 1]
            if i < 9:
                rows = pl.ds(pl.multiple_of(384 * b + 96 * q, 96), 96)
            else:
                far, h = lax.rem(q - step + 4, 4), i // 3 - 3
                rows = pl.ds(pl.multiple_of(384 * b + 96 * far + 48 * h, 48), 48)
            src = place = dst.at[rows, cols]
            r = lax.rem(q + step + 4, 4)
            device = {"ctx": 4 * r + y if n % 2 == 0 else 4 * z + r}
        return remote(src, place, ws.at[n, i], wr.at[n, i], device)

    def fetch_to(n, b):
        i, q = lax.rem(b - x + 3, 4), quarter(n)
        cols = pl.ds(512 * n, 512)
        rows = pl.ds(pl.multiple_of(384 * x + 96 * q, 96), 96)
        src = wsend.at[b, part(96 * q, 96), cols]
        return remote(src, wqkv.at[rows, cols], ws.at[n, i], wr.at[n, i], {"fsdp": b})

    def weight_each(which, items, act):
        for i in items:
            for n in which:
                act(weight(n, i))

    def begin(copy):
        copy.start()

    def arrive(copy):
        copy.wait_recv()

    def leave(copy):
        copy.wait_send()

    def weight_fetch(which):
        weight_each(which, (1, 0, 2), begin)

    def weight_share(which):
        weight_each(which, range(3), arrive)
        weight_each(which, range(3, 9), begin)

    def weight_pass(which):
        for k in range(3):
            weight_each(which, (3 + k,), arrive)
            weight_each(which, (9 + k,), begin)
        for k in range(3):
            weight_each(which, (6 + k,), arrive)
            weight_each(which, (12 + k,), begin)

    def weight_wait(which):
        weight_each(which, range(9, 15), arrive)

    heads, wide = (0, 1), (2, 3)

    def gain_copy(k):
        return over_x(X_GAIN, k, gains, gain.at[:, part(384 * x, 384)])

    def pos_copy(k):
        return over_x(X_POS, k, pos, posx.at[x])

    pos[...] = jnp.broadcast_to(
        jnp.concatenate([positions[0:1, :], positions[1:2, :]], axis=1).astype(F32), (8, 128)
    )
    gains[...] = jnp.broadcast_to(norm_attn[...].astype(F32), (8, 384))
    gains[1:2, :] = norm_mlp[...].astype(F32)
    for k in (2, 1, 3):
        pos_copy(k).start()
        gain_copy(k).start()
    gain[:, part(384 * x, 384)] = gains[...]
    posx[x] = pos[...]

    def local_copies():
        yield pltpu.make_async_copy(
            wg.at[:, part(1024 * x, 1024)], wgf.at[part(384 * x, 384)], ls.at[0]
        )
        yield pltpu.make_async_copy(
            wu.at[:, part(1024 * x, 1024)], wuf.at[part(384 * x, 384)], ls.at[1]
        )
        yield pltpu.make_async_copy(wd_in, wd, ls.at[2])
        for h in range(4):
            yield pltpu.make_async_copy(
                wo_in.at[pl.ds(96 * h, 96)], wop.at[pl.ds(128 * h, 96)], ls.at[3 + h]
            )

    def head_columns(b, j, rows):
        w_q = wq[rows, 384 * b + 192 * j : 384 * b + 192 * j + 192]
        w_k = wk[rows, 96 * (2 * b + j) : 96 * (2 * b + j) + 96]
        w_v = wv[rows, 96 * (2 * b + j) : 96 * (2 * b + j) + 96]
        blank = jnp.zeros((w_v.shape[0], 32), BF)
        return jnp.concatenate(spread(w_q, (0, 1)) + spread(w_k, (0,)) + [w_v, blank], axis=1)

    for b in range(4):

        @pl.when(b != x)
        def _(b=b):
            for j in heads:
                rows = part(96 * quarter(j), 96)
                wsend[b, rows, 512 * j : 512 * j + 512] = head_columns(b, j, rows)

                @pl.when(first)
                def _(j=j):
                    fetch_to(j, b).start()

    @pl.when(first)
    def _():
        gather_start(X_IN, xin, xall)
        xall[my_rows, :] = xin[...]

    for b in range(4):

        @pl.when(b == x)
        def _(b=b):
            for j in heads:
                wqkv[384 * b : 384 * b + 384, 512 * j : 512 * j + 512] = head_columns(
                    b, j, slice(0, 384)
                )

    for copy in local_copies():
        copy.start()
    for h in range(4):
        wop[128 * h + 96 : 128 * h + 128, :] = jnp.zeros((32, WIDTH), BF)

    lane = lax.broadcasted_iota(jnp.int32, (1, 128), 1)
    sign = jnp.where(lane < 64, -1.0, 1.0)
    index = jnp.where(lane < 64, lane, lane - 64)
    freq = jnp.where(index < 48, jnp.exp2(index.astype(F32) * STEP2), 0.0)
    for k in (1, 3, 2):
        pos_copy(k).wait()
    for b in range(4):
        block = posx[b]
        posv[b, 0] = block
        posv[b, 1] = pltpu.roll(block, 64, 1)

    def pos_to(to):
        return over_c(C_POS, to, posv.at[to // 4, lax.rem(to, 4) // 2], posc.at[c])

    def send_pos(k, carry):
        pos_to(lax.rem(c + k, 16)).start()
        return carry

    lax.fori_loop(1, 16, send_pos, 0)
    posc[c] = posv[c // 4, lax.rem(c, 4) // 2]

    @pl.when(first)
    def _():
        weight_share(heads)

    for b in range(4):
        angle = as_column(posx[b][0:1, :]) * freq
        cos_c[128 * b : 128 * b + 128, :] = jnp.cos(angle)
        sin_c[128 * b : 128 * b + 128, :] = jnp.sin(angle) * sign

    def tables():
        def await_pos(k, carry):
            pos_to(lax.rem(c + k, 16)).wait()
            return carry

        def table(i, carry):
            row = jnp.where(
                lane < 64, posc[2 * i][0:1, :], pltpu.roll(posc[2 * i + 1], 64, 1)[0:1, :]
            )
            block = part(128 * i, 128)
            posr[0:1, block] = row
            column = as_column(row)
            posk[block, :] = jnp.broadcast_to(column, (128, 128))
            angle = column * freq
            cos_s[block, :] = jnp.cos(angle)
            sin_s[block, :] = jnp.sin(angle) * sign
            return carry

        lax.fori_loop(1, 16, await_pos, 0)
        lax.fori_loop(0, 8, table, 0)

    for k in (1, 3, 2):
        gain_copy(k).wait()

    @pl.when(first)
    def _():
        weight_pass(heads)
        gather_pass(X_IN, xin, xall)
        weight_fetch(wide)
        weight_wait(heads)

    @pl.when(second)
    def _():
        tables()
        gather_start(X_DY, dyin, dyf)
        dyf[my_rows, :] = dyin[...]
        gather_pass(X_DY, dyin, dyf)
        pl.semaphore_wait(go, 1)
        weight_fetch(heads + wide)
        weight_share(heads + wide)
        weight_pass(heads + wide)
        weight_wait(heads + wide)

    gain_attn, gain_mlp = gain[0:1, :], gain[1:2, :]

    def to_pair(ref, e, b, i, width, dst):
        src = ref.at[part(128 * b + 64 * (i // 2), 64), pl.ds(width * (i % 2), width)]
        return over_c(e, 4 * b + i, src, dst.at[part(64 * c, 64)])

    def in_order(n):
        return behind(jnp.where(n == 2, 3, jnp.where(n == 3, 2, n)))

    def project(n, carry):
        b = in_order(n)
        rows = part(128 * b, 128)

        @pl.when(jnp.logical_and(second, n == 0))
        def _():
            gather(X_IN, 6, out, xall).wait_recv()

        @pl.when(jnp.logical_and(second, n == 1))
        def _():
            gather_pass(X_IN, xin, xall)

        @pl.when(n == 3)
        def _():
            gather_far(X_IN, xin, xall)

        value = xall[rows, :].astype(F32)
        normed = (
            value
            * lax.rsqrt(jnp.mean(value * value, axis=-1, keepdims=True) + EPSILON)
            * gain_attn
        ).astype(BF)
        nf[rows, :] = normed
        u = mm(normed, wqkv[...])
        cosine, sine = cos_c[rows, :], sin_c[rows, :]
        for h in range(8):
            head = u[:, 128 * h : 128 * h + 128]
            if h % 4 != 3:
                head = turn(head, cosine, sine)
            qsend[rows, 128 * h : 128 * h + 128] = head.astype(BF)
        for i in range(4):

            @pl.when(4 * b + i != c)
            def _(i=i):
                to_pair(qsend, C_QKV, b, i, 512, qs).start()

            @pl.when(4 * b + i == c)
            def _(i=i):
                qs[part(64 * c, 64), :] = qsend[
                    part(128 * b + 64 * (i // 2), 64), 512 * (i % 2) : 512 * (i % 2) + 512
                ]

        return carry

    lax.fori_loop(0, 4, project, 0)

    @pl.when(first)
    def _():
        tables()

    weight_each(heads, range(3), leave)


    def await_qkv(k, carry):
        place = qs.at[part(64 * lax.rem(c - k + 16, 16), 64)]
        over_c(C_QKV, lax.rem(c + k, 16), place, place).wait_recv()
        return carry

    lax.fori_loop(1, 16, await_qkv, 0)

    @pl.when(first)
    def _():
        weight_share(wide)
        pl.semaphore_signal(go, inc=1, device_id={"section": 1}, device_id_type=MESH)

    vt[...] = qs[:, 384:512].T
    kt[...] = qs[:, 256:384].T

    def masked(q, cols):
        st = mm_nt(qs[:, 256:384], q)
        return jnp.where(posk[:, 0:1] <= posr[0:1, cols], st, -1e30)

    def att_place():
        return attp.at[part(64 * (c // 2), 64), part(256 * lax.rem(c, 2), 256)]

    def att_to(to):
        return over_c(C_ATT, to, osend.at[part(64 * to, 64)], att_place())

    def attend(n, carry):
        rows = part(256 * n, 256)

        for g in range(2):
            st = masked(qs[rows, 128 * g : 128 * g + 128], rows)
            top = jnp.max(st, axis=0, keepdims=True)
            e = jnp.exp2((st - top) * SCALE2)
            sums = jnp.sum(e, axis=0, keepdims=True)
            lse[g : g + 1, rows] = top * SCALE2 + jnp.log2(sums)
            result = mm(vt[...], e.astype(BF)) * (1.0 / sums)
            osend[rows, 128 * g : 128 * g + 128] = result.T.astype(BF)
        for i in range(4):
            to = 4 * n + i

            @pl.when(to != c)
            def _(to=to):
                att_to(to).start()

            @pl.when(to == c)
            def _(to=to):
                attp[part(64 * (c // 2), 64), part(256 * lax.rem(c, 2), 256)] = osend[
                    part(64 * to, 64), :
                ]

        return carry

    lax.fori_loop(0, 4, attend, 0)

    @pl.when(first)
    def _():
        weight_pass(wide)


    def await_att(b):
        for i in range(4):
            to = 4 * b + i

            @pl.when(to != c)
            def _(to=to, i=i):
                k = lax.rem(c - to + 16, 16)
                place = attp.at[part(64 * (2 * b + i // 2), 64), pl.ds(256 * (i % 2), 256)]
                remote(place, place, cs.at[C_ATT, k], cr.at[C_ATT, k], {"ctx": lax.rem(c + k, 16)}).wait_recv()

    def give(e, n, b, value):
        place = psend.at[(X_SUM1, X_SUM2, X_SUM3, X_SUM4).index(e) % 2, b]

        @pl.when(n < 3)
        def _():
            place[...] = value.astype(BF)

        @pl.when(n == 0)
        def _():
            total(e, 0).start()
            total(e, 1).start()

        @pl.when(n == 1)
        def _():
            total(e, 2).start()

        @pl.when(n == 2)
        def _():
            total(e, 3).start()
            total_pass(e)

        @pl.when(n == 3)
        def _():
            own[...] = value

    def far_first(n):
        return lax.rem(x + jnp.where(n == 0, 2, jnp.where(n == 1, 1, jnp.where(n == 2, 3, 0))), 4)

    def combine(n, carry):
        b = far_first(n)
        await_att(b)
        give(X_SUM1, n, b, mm(attp[part(128 * b, 128), :], wop[...]))
        return carry

    for copy in local_copies():
        copy.wait()
    lax.fori_loop(0, 4, combine, 0)
    middle = xall[my_rows, :].astype(F32) + total_take(X_SUM1)
    mid[...] = middle
    n2[my_rows, :] = (
        middle * lax.rsqrt(jnp.mean(middle * middle, axis=-1, keepdims=True) + EPSILON) * gain_mlp
    ).astype(BF)
    n2_own = n2.at[my_rows]
    gather_start(X_N2, n2_own, n2)

    @pl.when(first)
    def _():
        weight_wait(wide)

    def pair(blocks, ref):
        return jnp.concatenate([ref[part(128 * b, 128), :] for b in blocks], axis=0)

    def far_copy(d, b):
        return piece(X_SUM2, d, d, psend.at[1, b], prec3.at[d - 1])

    def feed(ds):
        blocks = [lax.rem(x + d, 4) for d in ds]
        a = pair(blocks, n2)
        ga, u = mm(a, wgf[...]), mm(a, wuf[...])
        h = (ga * (1.0 / (1.0 + jnp.exp(-ga))) * u).astype(BF)
        result = mm(h, wd[...])
        for n, (d, b) in enumerate(zip(ds, blocks)):
            rows, cut = part(128 * b, 128), slice(128 * n, 128 * n + 128)
            gate[rows, :] = ga[cut].astype(BF)
            up[rows, :] = u[cut].astype(BF)
            hidden[rows, :] = h[cut]
            if d == 0:
                own[...] = result[cut]
            else:
                psend[1, b] = result[cut].astype(BF)
                far_copy(d, b).start()

    gather_pass(X_N2, n2_own, n2)
    feed((1, 3))
    gather_far(X_N2, n2_own, n2)
    feed((2, 0))
    result = mid[...] + own[...]
    for d in (1, 3, 2):
        far_copy(d, lax.rem(x + d, 4)).wait_recv()
        result = result + prec3[d - 1].astype(F32)
    out[...] = result.astype(BF)

    @pl.when(first)
    def _():
        gather_sent(X_IN, xin, xall, forwarded=False)
        gather(X_IN, 6, out, xall).start()
        gather_start(X_IN, out, xall, True)

    held = dict(zip(ARRAYS, (h_gate, h_up, h_down, h_out, h_heads_a, h_heads_b)))

    def ring(name):
        axis, d = FLOWS[name][:2]
        other = "z" if axis == "y" else "y"
        group = where[axis] if name in STAY else lax.rem(x + where[axis], 4)
        return NAMES.index(name), axis, other, d, group, where[other]

    def hand(name):
        axis, d = FLOWS[name][:2]
        if name in STAY:
            return where[axis], d
        return lax.rem(x - where[axis] + 4, 4), -d

    def at(i, d, s):
        return lax.rem(i - d * s + 8, 4)

    def columns(name):
        return pl.ds(FLOWS[name][3], FLOWS[name][5])

    def place_of(name, g, p):
        return held[FLOWS[name][2]].at[g, p, :, columns(name)]

    def partial(name, g, p):
        array, cols = FLOWS[name][2], columns(name)
        if array == "down":
            return wd.at[part(256 * g + 64 * p, 64), cols]
        if array == "out":
            return wop.at[part(96 * g, 96), part(384 * p, 384)]
        rows = pl.ds(pl.multiple_of(384 * g + 96 * p, 96), 96)
        if name in LATE:
            return wqkv.at[rows, pl.ds(384 * LATE.index(name), 384)]
        return (wgf if array == "gate" else wuf).at[rows, cols]

    def arrival(name, s, q):
        n = 4 * (s - 1) + q
        array, cols = FLOWS[name][2], columns(name)
        if array == "gate":
            return wsend.at[s, part(96 * q, 96), cols]
        if array == "up":
            slot = wsend.at[3, part(96 * q, 96), cols]
            return slot if s == 0 else dgu.at[part(96 * n, 96), cols]
        if array == "down":
            return arrive_down.at[q, :, cols] if s == 0 else n2.at[part(64 * n, 64), cols]
        return arrive_out.at[s, q]

    def arrival2(name, s):
        array, cols = FLOWS[name][2], columns(name)
        if array in ("gate", "up"):
            return (gate if array == "gate" else up).at[part(96 * s, 96), cols]
        if array == "down":
            return prec3.at[s, pl.ds(0, 64), cols]
        return {"out": second_out, "heads_a": second_a, "heads_b": second_b}[array].at[s]

    def flow(name, n, src, dst, device):
        f = NAMES.index(name)
        return remote(src, dst, fs.at[f, n], fr.at[f, n], device)

    def copy_first(name, s, q):
        f, axis, other, d, i, j = ring(name)
        src = partial(name, at(i, d, 1 + s), at(j, d, 1 + q))
        return flow(name, 4 * s + q, src, arrival(name, s, q), near(axis, d))

    def copy_second(name, s):
        f, axis, other, d, i, j = ring(name)
        src = partial(name, i, at(j, d, 1 + s))
        return flow(name, 12 + s, src, arrival2(name, s), near(other, d))

    def copy_mirror(name):
        f, axis, other, d, i, j = ring(name)
        n = 6 if name in LATE else 15
        device = {"fsdp": lax.rem(x + where[axis], 4)}
        return flow(name, n, partial(name, i, j), place_of(name, x, j), device)

    def copy_own(name):
        f, axis, other, d, i, j = ring(name)
        group = i if name in STAY else x
        return pltpu.make_async_copy(partial(name, i, j), place_of(name, group, j), os.at[f])

    def copy_small(name, s):
        f, axis, other, d, i, j = ring(name)
        place = place_of(name, hand(name)[0], at(j, d, s))
        return flow(name, 16 + s, place, place, near(other, d))

    def copy_big(name, s, q):
        f, axis, other, d, i, j = ring(name)
        place = place_of(name, at(*hand(name), s), at(j, d, q))
        return flow(name, 20 + 4 * s + q, place, place, near(axis, d))

    def first_start(names):
        def body(q, carry):
            for name in names:
                copy_first(name, 0, q).start()
            return carry

        lax.fori_loop(0, 4, body, 0)

    def first_step(names, s):
        def body(q, carry):
            for name in names:
                f, axis, other, d, i, j = ring(name)
                copy_first(name, s, q).wait_recv()
                place = partial(name, at(i, d, 2 + s), at(j, d, 1 + q))
                place[...] = place[...] + arrival(name, s, q)[...]
                if s < 2:
                    copy_first(name, s + 1, q).start()
                else:

                    @pl.when(q == 0)
                    def _(name=name):
                        copy_second(name, 0).start()

            return carry

        lax.fori_loop(0, 4, body, 0)

    def second_step(names, s):
        for name in names:
            f, axis, other, d, i, j = ring(name)
            copy_second(name, s).wait_recv()
            place = partial(name, i, at(j, d, 2 + s))
            place[...] = place[...] + arrival2(name, s)[...]
            if s < 2:
                copy_second(name, s + 1).start()

    def mirror_step(names, act):
        for name in names:
            if name in STAY:
                act(copy_own(name))
                continue
            axis = FLOWS[name][0]

            @pl.when(where[axis] != 0)
            def _(name=name):
                act(copy_mirror(name))

            @pl.when(where[axis] == 0)
            def _(name=name):
                act(copy_own(name))

    def finish_copy(copy):
        copy.wait()

    def small_step(names, q):
        for name in names:
            if q > 0:
                copy_small(name, q - 1).wait_recv()
            if q < 3:
                copy_small(name, q).start()
        for name in names:
            copy_big(name, 0, q).start()

    def big_step(names, s, low, high):
        def body(q, carry):
            for name in names:
                copy_big(name, s, q).wait_recv()
                if s < 2:
                    copy_big(name, s + 1, q).start()
            return carry

        lax.fori_loop(low, high, body, 0)

    def gain_sum_copy(n, k):
        axis = "xyz"[n]
        if n == 0:
            src = ggain.at[:, part(lax.rem(x + k, 4) * 384, 384)]
        else:
            src = gain_in.at[n, 0]
        return remote(src, gain_in.at[n, k], gs.at[n, k], gr.at[n, k], near(axis, k))

    def gain_start(n):
        for k in (1, 2, 3):
            gain_sum_copy(n, k).start()

    def gain_sum(n):
        mine = ggain[:, part(x * 384, 384)] if n == 0 else gain_in[n, 0]
        for k in (1, 2, 3):
            gain_sum_copy(n, k).wait()
        return mine + gain_in[n, 1] + gain_in[n, 2] + gain_in[n, 3]

    def late(name, n):
        f, axis, other, d, i, j = ring(name)
        cols = pl.ds(384 * LATE.index(name), 384)
        k = (n if n < 6 else n - 1) % 3 + 1
        if n < 3:
            src = wqkv.at[part(384 * lax.rem(i + k, 4), 384), cols]
            return flow(name, n, src, (arrive_a, arrive_b)[LATE.index(name)].at[k - 1], near(axis, k))
        if n < 6:
            src = partial(name, i, lax.rem(j + k, 4))
            return flow(name, n, src, arrival2(name, k - 1), near(other, k))
        if n < 10:
            place = held[name].at[hand(name)[0], j]
            return flow(name, n, place, place, near(other, k))
        place = held[name].at[hand(name)[0]]
        return flow(name, n, place, place, near(axis, k))

    def late_each(items, act):
        for n in items:
            for name in LATE:
                act(late(name, n))

    def late_first():
        late_each(range(3), arrive)
        for name in LATE:
            f, axis, other, d, i, j = ring(name)
            rows, cols = part(384 * i, 384), pl.ds(384 * LATE.index(name), 384)
            got = (arrive_a, arrive_b)[LATE.index(name)]
            sums = wqkv[rows, cols].astype(F32)
            for k in range(3):
                sums = sums + got[k].astype(F32)
            wqkv[rows, cols] = sums.astype(BF)
        late_each(range(3, 6), begin)

    def late_second():
        late_each(range(3, 6), arrive)
        for name in LATE:
            f, axis, other, d, i, j = ring(name)
            place = partial(name, i, j)
            sums = place[...].astype(F32)
            for k in range(3):
                sums = sums + arrival2(name, k)[...].astype(F32)
            place[...] = sums.astype(BF)
        mirror_step(LATE, begin)

    def late_small():
        mirror_step(LATE, finish_copy)
        late_each(range(7, 10), begin)

    def late_big():
        late_each(range(7, 10), arrive)
        late_each(range(10, 13), begin)

    def feed_grads(s, carry):
        rows = part(384 * at(ring("gate")[4], 1, 1 + s), 384)
        wgf[rows, :] = mm_tn(n2[:, rows], dgu[0:512, :]).astype(BF)
        rows = part(384 * at(ring("up")[4], -1, 1 + s), 384)
        wuf[rows, :] = mm_tn(n2[:, rows], dgu[512:1024, :]).astype(BF)
        rows = part(256 * at(z, 1, 1 + s), 256)
        wd[rows, :] = mm_tn(hidden[:, rows], dyf[...]).astype(BF)

        return carry

    @pl.when(first)
    def _():
        gather_pass(X_DY, dx, dyf)
        gather(X_DY, 6, dx, dyf).wait_recv()

    gather_far(X_DY, dx, dyf)

    def feed_back(ds):
        blocks = [lax.rem(x + d, 4) for d in ds]
        dh = mm_nt(pair(blocks, dyf), wd[...])
        ga, u = pair(blocks, gate).astype(F32), pair(blocks, up).astype(F32)
        s = 1.0 / (1.0 + jnp.exp(-ga))
        dga = (dh * u * (s * (1.0 + ga * (1.0 - s)))).astype(BF)
        du = (dh * (ga * s)).astype(BF)
        result = mm_nt(dga, wgf[...]) + mm_nt(du, wuf[...])
        for n, (d, b) in enumerate(zip(ds, blocks)):
            rows, cut = part(128 * b, 128), slice(128 * n, 128 * n + 128)
            dgu[rows, :] = dga[cut]
            dgu[part(512 + 128 * b, 128), :] = du[cut]
            if d == 0:
                own[...] = result[cut]
            else:
                psend[0, b] = result[cut].astype(BF)
                for i in {2: (0, 1), 1: (2,), 3: (3,)}[d]:
                    total(X_SUM3, i).start()

    total_sent(X_SUM1)
    feed_back((2, 1))
    feed_back((3, 0))
    weight_each(heads, range(3, 15), leave)
    weight_each(wide, range(15), leave)
    gather_sent(X_N2, n2_own, n2)
    gather_sent(X_DY, dyin, dyf, started=False)
    for d in (1, 2, 3):
        far_copy(d, lax.rem(x + d, 4)).wait_send()
    lax.fori_loop(0, 1, feed_grads, 0)
    first_start(("gate", "up", "down"))
    total_pass(X_SUM3)
    lax.fori_loop(1, 4, feed_grads, 0)
    first_start(("gate_rest", "up_rest", "down_rest"))
    def norm_back(value, grad, gain_row):
        r = lax.rsqrt(jnp.mean(value * value, axis=-1, keepdims=True) + EPSILON)
        unit = value * r
        t = grad * gain_row
        back = r * (t - unit * jnp.mean(t * unit, axis=-1, keepdims=True))
        return back, jnp.sum(grad * unit, axis=0, keepdims=True)

    back, g_mlp = norm_back(mid[...], total_take(X_SUM3), gain_mlp)
    dmid = dyf[my_rows, :].astype(F32) + back
    mid[...] = dmid
    ggain[...] = jnp.zeros_like(ggain)
    ggain[1:2, :] = g_mlp
    dbr[my_rows, :] = dmid.astype(BF)
    dbr_own = dbr.at[my_rows]
    gather_start(X_DBR, dbr_own, dbr)

    def branch(n, carry):
        b = in_order(n)
        rows = part(128 * b, 128)

        @pl.when(n == 1)
        def _():
            gather_pass(X_DBR, dbr_own, dbr)

        @pl.when(n == 3)
        def _():
            gather_far(X_DBR, dbr_own, dbr)

        dsend[rows, :] = mm_nt(dbr[rows, :], wop[...]).astype(BF)
        for i in range(4):

            @pl.when(4 * b + i != c)
            def _(i=i):
                to_pair(dsend, C_DATT, b, i, 256, das).start()

            @pl.when(4 * b + i == c)
            def _(i=i):
                das[part(64 * c, 64), :] = dsend[
                    part(128 * b + 64 * (i // 2), 64), 256 * (i % 2) : 256 * (i % 2) + 256
                ]

        return carry

    lax.fori_loop(0, 4, branch, 0)
    for n in range(2):
        rows = slice(256 * n, 256 * n + 256)
        att[rows, :] = jnp.concatenate(
            [attp[rows, 128 * h : 128 * h + 96] for h in range(4)], axis=1
        )
    wop[0:384, :] = mm_tn(att[...], dbr[...]).astype(BF)
    first_start(("out",))

    def await_das(k, carry):
        place = das.at[part(64 * lax.rem(c - k + 16, 16), 64)]
        over_c(C_DATT, lax.rem(c + k, 16), place, place).wait_recv()
        return carry

    lax.fori_loop(1, 16, await_das, 0)
    first_step(EARLY, 0)
    dk[...] = jnp.zeros_like(dk)
    dv[...] = jnp.zeros_like(dv)

    def grad_place(h):
        return dqp.at[part(64 * (c // 2), 64), part(512 * lax.rem(c, 2) + 256 * h, 256)]

    def grad_to(e, to):
        h = e - C_DQ
        return over_c(e, to, dqs.at[part(64 * to, 64), pl.ds(256 * h, 256)], grad_place(h))

    def attend_back(n, carry):
        rows = part(256 * n, 256)
        for g in range(2):
            cols = slice(128 * g, 128 * g + 128)
            q, da = qs[rows, cols], das[rows, cols]
            p = jnp.exp2(masked(q, rows) * SCALE2 - lse[g : g + 1, rows])
            dp = mm_nt(qs[:, 384:512], da)
            dv[...] += mm(p.astype(BF), da)
            ds = (p * (dp - jnp.sum(p * dp, axis=0, keepdims=True))).astype(BF)
            dk[...] += mm(ds, q)
            dq = mm(kt[...], ds).T * SCALE
            dqs[rows, cols] = turn(dq, cos_s[rows, :], -sin_s[rows, :]).astype(BF)
        for i in range(4):
            to = 4 * n + i

            @pl.when(to != c)
            def _(to=to):
                grad_to(C_DQ, to).start()

            @pl.when(to == c)
            def _(to=to):
                grad_place(0)[...] = dqs[part(64 * to, 64), 0:256]

        return carry

    lax.fori_loop(0, 4, attend_back, 0)
    dqs[:, 256:384] = turn(dk[...] * SCALE, cos_s[...], -sin_s[...]).astype(BF)
    dqs[:, 384:512] = dv[...].astype(BF)

    def send_dkv(k, carry):
        grad_to(C_DKV, lax.rem(c + k, 16)).start()
        return carry

    lax.fori_loop(1, 16, send_dkv, 0)
    grad_place(1)[...] = dqs[part(64 * c, 64), 256:512]
    first_step(EARLY, 1)

    def await_dqkv(b):
        for i in range(4):
            to = 4 * b + i

            @pl.when(to != c)
            def _(to=to, i=i):
                k = lax.rem(c - to + 16, 16)
                for h in range(2):
                    place = dqp.at[
                        part(64 * (2 * b + i // 2), 64), pl.ds(512 * (i % 2) + 256 * h, 256)
                    ]
                    e = C_DQ + h
                    remote(
                        place, place, cs.at[e, k], cr.at[e, k], {"ctx": lax.rem(c + k, 16)}
                    ).wait_recv()

    def input_grad(n, carry):
        b = far_first(n)
        await_dqkv(b)
        give(X_SUM4, n, b, mm_nt(dqp[part(128 * b, 128), :], wqkv[...]))
        return carry

    lax.fori_loop(0, 4, input_grad, 0)
    @pl.when(first)
    def _():
        first_step(EARLY, 2)

    for n in range(2):
        rows = slice(256 * n, 256 * n + 256)
        pieces = []
        for h in range(8):
            if h % 4 == 3:
                pieces.append(dqp[rows, 128 * h : 128 * h + 96])
            else:
                pieces.append(dqp[rows, 128 * h : 128 * h + 48])
                pieces.append(dqp[rows, 128 * h + 64 : 128 * h + 112])
        dqkv[rows, :] = jnp.concatenate(pieces, axis=1)

    def head_grads(g, carry):
        rows = part(384 * g, 384)
        wqkv[rows, 0:768] = mm_tn(nf[:, rows], dqkv[...]).astype(BF)
        return carry

    lax.fori_loop(0, 4, head_grads, 0)
    late_each(range(3), begin)
    back, g_attn = norm_back(xall[my_rows, :].astype(F32), total_take(X_SUM4), gain_attn)
    dx[...] = (mid[...] + back).astype(BF)
    ggain[0:1, :] = g_attn

    @pl.when(second)
    def _():
        gather_sent(X_DY, dyin, dyf, forwarded=False)
        gather(X_DY, 6, dx, dyf).start()
        gather_start(X_DY, dx, dyf, True)

    gain_start(0)

    @pl.when(second)
    def _():
        first_step(EARLY, 2)

    second_step(EARLY, 0)
    gain_in[1, 0] = gain_sum(0)
    gain_start(1)
    second_step(EARLY, 1)
    second_step(EARLY, 2)
    mirror_step(EARLY, begin)
    gain_in[2, 0] = gain_sum(1)
    gain_start(2)
    late_first()
    late_second()
    mirror_step(EARLY, finish_copy)
    small_step(EARLY, 0)
    late_small()
    small_step(EARLY, 1)
    late_big()
    small_step(EARLY, 2)
    small_step(EARLY, 3)
    for n in range(3):
        big_step(EARLY, n, 0, 4)
    late_each(range(10, 13), arrive)
    o_gain[...] = gain_sum(2)

    def sent_c(k, carry):
        to = lax.rem(c + k, 16)
        place = qs.at[part(64 * to, 64)]
        over_c(C_QKV, to, place, place).wait_send()
        att_to(to).wait_send()
        place = das.at[part(64 * to, 64)]
        over_c(C_DATT, to, place, place).wait_send()
        grad_to(C_DQ, to).wait_send()
        grad_to(C_DKV, to).wait_send()
        return carry

    lax.fori_loop(1, 16, sent_c, 0)
    total_sent(X_SUM3)
    total_sent(X_SUM4)
    gather_sent(X_DBR, dbr_own, dbr)
    gather_sent(X_IN, xin, xall, started=False)

    def sent_first(q, carry):
        for name in EARLY:
            for n in range(3):
                copy_first(name, n, q).wait_send()
                copy_big(name, n, q).wait_send()
        return carry

    lax.fori_loop(0, 4, sent_first, 0)
    late_each((0, 1, 2, 3, 4, 5, 7, 8, 9, 10, 11, 12), leave)
    for name in EARLY:
        for n in range(3):
            copy_second(name, n).wait_send()
            copy_small(name, n).wait_send()

    @pl.when(first)
    def _():
        gather_sent(X_IN, xin, xall, forwarded=False)
        gather(X_IN, 6, out, xall).wait_send()

    @pl.when(second)
    def _():
        gather_sent(X_DY, dyin, dyf, forwarded=False)
        gather(X_DY, 6, dx, dyf).wait_send()


def run_layer(xin, dyin, positions, norm_attn, norm_mlp, wq, wk, wv, wo, wd, wg, wu, cid):
    vm = pl.BlockSpec(memory_space=pltpu.VMEM)
    hbm = pl.BlockSpec(memory_space=pl.ANY)
    dma = pltpu.SemaphoreType.DMA
    shapes = [
        ((128, WIDTH), BF),
        ((128, WIDTH), BF),
        *(((4, 4) + shape, BF) for shape in ARRAYS.values()),
        ((8, 384), F32),
    ]
    scratch = [
        ((512, WIDTH), BF),
        ((2, 512, WIDTH), BF),
        ((1024, 1024), BF),
        ((512, 768), BF),
        ((512, 384), BF),
        ((512, WIDTH), BF),
        ((512, 1024), BF),
        ((8, WIDTH), F32),
        ((4, 64, WIDTH), BF),
        ((3, 4, 96, 384), BF),
        *(((3, 384, 384), BF),) * 2,
        *(((3, 96, 384), BF),) * 3,
        ((3, 4, 8, 384), F32),
        ((4, 384, 1024), BF),
        ((WIDTH, 1024), BF),
        ((WIDTH, 1024), BF),
        ((WIDTH, 1024), BF),
        ((512, WIDTH), BF),
        ((1024, WIDTH), BF),
        ((2, 2, 64, WIDTH), BF),
        ((512, WIDTH), BF),
        ((8, 384), F32),
        ((8, 128), F32),
        ((8, WIDTH), F32),
        ((4, 8, 128), F32),
        ((4, 2, 8, 128), F32),
        ((16, 8, 128), F32),
        ((8, 1024), F32),
        ((1024, 128), F32),
        ((512, 128), F32),
        ((512, 128), F32),
        ((1024, 128), F32),
        ((1024, 128), F32),
        ((512, 1024), BF),
        ((1024, 512), BF),
        ((128, 1024), BF),
        ((128, 1024), BF),
        ((8, 1024), F32),
        ((1024, 256), BF),
        ((512, 512), BF),
        ((128, WIDTH), F32),
        ((512, 1024), BF),
        ((512, 1024), BF),
        ((128, WIDTH), F32),
        ((2, 4, 128, WIDTH), BF),
        ((2, 2, 128, WIDTH), BF),
        ((3, 128, WIDTH), BF),
        ((512, 512), BF),
        ((1024, 256), BF),
        ((1024, 128), F32),
        ((1024, 128), F32),
        ((1024, 512), BF),
        ((512, 1024), BF),
    ]
    return pl.pallas_call(
        layer_kernel,
        out_shape=[jax.ShapeDtypeStruct(s, d) for s, d in shapes],
        in_specs=[vm] * 8 + [hbm] * 4,
        out_specs=[vm] * 2 + [hbm] * len(ARRAYS) + [vm],
        scratch_shapes=[pltpu.VMEM(s, d) for s, d in scratch]
        + [dma((13, 7)), dma((13, 7)), dma((6, 16)), dma((6, 16)), dma((4, 15)), dma((4, 15)), dma((7,)), pltpu.SemaphoreType.REGULAR]
        + [dma((9, 32)), dma((9, 32)), dma((3, 4)), dma((3, 4)), dma((9,))],
        name="layer",
        compiler_params=pltpu.CompilerParams(
            collective_id=cid, has_side_effects=True, vmem_limit_bytes=63 << 20
        ),
    )(xin, dyin, positions, norm_attn, norm_mlp, wq, wk, wv, wo, wd, wg, wu)


def local(
    inputs,
    positions,
    out_grad,
    norm_attn,
    w_query,
    key_weight,
    value_weight,
    output_weight,
    norm_mlp,
    w_gate,
    w_up,
    w_down,
):
    out, dx, *summed, g_gain = run_layer(
        inputs.reshape(128, WIDTH),
        out_grad.reshape(128, WIDTH),
        positions,
        norm_attn,
        norm_mlp,
        w_query[0],
        key_weight[0],
        value_weight[0],
        output_weight[0],
        w_down[0],
        w_gate[0],
        w_up[0],
        0,
    )
    g_gate, g_up, g_query, g_key, g_value, g_out, g_down, g_attn, g_mlp = widen(*summed, g_gain)
    return (
        out.reshape(1, 2, 64, WIDTH),
        dx.reshape(1, 2, 64, WIDTH),
        g_attn,
        g_query[None],
        g_key[None],
        g_value[None],
        g_out[None],
        g_mlp,
        g_gate[None],
        g_up[None],
        g_down[None],
    )


def solution(mesh):
    rows = P("section", "fsdp", None)
    return jax.shard_map(
        local,
        mesh=mesh,
        in_specs=(
            P("fsdp", "ctx", None),
            P("fsdp", "ctx"),
            P("fsdp", "ctx", None),
            P("section", "fsdp"),
            rows,
            rows,
            rows,
            rows,
            P("section", "fsdp"),
            rows,
            rows,
            rows,
        ),
        out_specs=(
            P("section", "fsdp", "ctx", None),
            P("section", "fsdp", "ctx", None),
            P("section", "fsdp"),
            rows,
            rows,
            rows,
            rows,
            P("section", "fsdp"),
            rows,
            rows,
            rows,
        ),
        check_vma=False,
    )
```

```python
import jax
import jax.numpy as jnp
from jax import lax
from jax.experimental import pallas as pl
from jax.experimental.pallas import tpu as pltpu
from jax.sharding import PartitionSpec as P

QUERY_HEADS = 16
KEY_VALUE_HEADS = 8
HEAD_SIZE = 96
WIDTH = 1536
FF = 4096
THETA = 100000.0
EPSILON = 1e-05
MESH = pl.DeviceIdType.MESH
N_X = 4
N_C = 16
BF = jnp.bfloat16
F32 = jnp.float32


def mm(a, b):
    return jnp.dot(a, b, preferred_element_type=F32)


def mm_tn(a, b):
    return lax.dot_general(a, b, (((0,), (0,)), ((), ())), preferred_element_type=F32)


def mm_nt(a, b):
    return lax.dot_general(a, b, (((1,), (1,)), ((), ())), preferred_element_type=F32)


def remote(src, dst, send, recv, device):
    return pltpu.make_async_remote_copy(
        src_ref=src, dst_ref=dst, send_sem=send, recv_sem=recv, device_id=device, device_id_type=MESH
    )


def part(start, size):
    return pl.ds(pl.multiple_of(start, size), size)


def widen_kernel(w_gate, w_up, w_down, w_out, w_a, w_b, gains, gate, up, query, key, value, g_out, g_down, g_attn, g_mlp):
    g_attn[...] = gains[0:1, :]
    g_mlp[...] = gains[1:2, :]
    g_down[...] = w_down[...].astype(F32)
    keys, values = [], []
    for x in range(N_X):
        gate[:, 1024 * x : 1024 * x + 1024] = w_gate[x, 0].astype(F32)
        up[:, 1024 * x : 1024 * x + 1024] = w_up[x, 0].astype(F32)
        g_out[:, 384 * x : 384 * x + 384] = w_out[0, x].astype(F32)
        a, b = w_a[x, 0].astype(F32), w_b[x, 0].astype(F32)
        query[:, 384 * x : 384 * x + 384] = jnp.concatenate([a[:, :192], b[:, :192]], axis=1)
        keys += [a[:, 192:288], b[:, 192:288]]
        values += [a[:, 288:], b[:, 288:]]
    key[...] = jnp.concatenate(keys, axis=1)
    value[...] = jnp.concatenate(values, axis=1)


def widen(gate, up, down, out, heads_a, heads_b, gains):
    steps = 4

    def spec(r, cols):
        return pl.BlockSpec((r, cols), lambda i: (i, 0))

    def shape(r, cols):
        return jax.ShapeDtypeStruct((r, cols), F32)

    def blocks(cols):
        return pl.BlockSpec((4, 1, 96, cols), lambda i: (0, i, 0, 0))

    return pl.pallas_call(
        widen_kernel,
        grid=(steps,),
        out_shape=[
            shape(384, FF),
            shape(384, FF),
            shape(384, 1536),
            shape(384, 768),
            shape(384, 768),
            shape(384, 1536),
            shape(1024, 1536),
            shape(1, 384),
            shape(1, 384),
        ],
        in_specs=[
            blocks(1024),
            blocks(1024),
            spec(256, 1536),
            pl.BlockSpec((1, 4, 96, 384), lambda i: (i, 0, 0, 0)),
            blocks(384),
            blocks(384),
            pl.BlockSpec((8, 384), lambda i: (0, 0)),
        ],
        out_specs=[
            spec(96, FF),
            spec(96, FF),
            spec(96, 1536),
            spec(96, 768),
            spec(96, 768),
            spec(96, 1536),
            spec(256, 1536),
            pl.BlockSpec((1, 384), lambda i: (0, 0)),
            pl.BlockSpec((1, 384), lambda i: (0, 0)),
        ],
        name="widen",
        compiler_params=pltpu.CompilerParams(vmem_limit_bytes=60 << 20),
    )(gate, up, down.reshape(1024, 1536), out, heads_a, heads_b, gains)


X_GAIN, X_POS, X_IN, X_DY, X_QKV, X_GATE, X_UP, X_SUM1, X_N2, X_SUM2, X_SUM3, X_DBR, X_SUM4 = range(13)
C_POS, C_QKV, C_ATT, C_DATT, C_DQ, C_DKV = range(6)
SCALE = HEAD_SIZE ** (-0.5)
SCALE2 = SCALE * 1.4426950408889634
STEP2 = -2.0 / HEAD_SIZE * 16.609640474436812
FLOWS = {
    "gate": ("y", 1, "gate", 0, 96, 896),
    "up": ("y", -1, "up", 0, 96, 896),
    "down": ("z", 1, "down", 0, 64, 1280),
    "out": ("z", -1, "out", 0, 96, 384),
    "gate_rest": ("z", -1, "gate", 896, 96, 128),
    "up_rest": ("z", -1, "up", 896, 96, 128),
    "down_rest": ("z", -1, "down", 1280, 64, 256),
    "heads_a": ("y", 1, "heads_a", 0, 96, 384),
    "heads_b": ("z", -1, "heads_b", 0, 96, 384),
}
ARRAYS = {
    "gate": (96, 1024),
    "up": (96, 1024),
    "down": (64, 1536),
    "out": (96, 384),
    "heads_a": (96, 384),
    "heads_b": (96, 384),
}
NAMES = list(FLOWS)
EARLY, LATE = NAMES[:7], NAMES[7:]
MAIN = [name for name in EARLY if name != "out"]
STAY = ("down", "out", "down_rest")


def spread(w, heads):
    blank = jnp.zeros((w.shape[0], 16), w.dtype)
    pieces = []
    for h in heads:
        pieces += [w[:, 96 * h : 96 * h + 48], blank, w[:, 96 * h + 48 : 96 * h + 96], blank]
    return pieces


def as_column(row):
    eye = lax.broadcasted_iota(jnp.int32, (128, 128), 0) == lax.broadcasted_iota(
        jnp.int32, (128, 128), 1
    )
    return jnp.sum(jnp.where(eye, jnp.broadcast_to(row, (128, 128)), 0.0), axis=1, keepdims=True)


def turn(u, cosine, sine):
    return u * cosine + pltpu.roll(u, 64, 1) * sine


def layer_kernel(
    xin,
    dyin,
    positions,
    norm_attn,
    norm_mlp,
    wq,
    wk,
    wv,
    wo_in,
    wd_in,
    wg,
    wu,
    out,
    dx,
    h_gate,
    h_up,
    h_down,
    h_out,
    h_heads_a,
    h_heads_b,
    o_gain,
    nf,
    rows2,
    dgu,
    dqkv,
    att,
    dbr,
    hidden,
    ggain,
    arrive_down,
    arrive_out,
    arrive_a,
    arrive_b,
    second_out,
    second_a,
    second_b,
    gain_in,
    wsend,
    wqkv,
    wgf,
    wuf,
    wop,
    wd,
    relay_s,
    xall,
    gains,
    pos,
    gain,
    posx,
    posv,
    posc,
    posr,
    posk,
    cos_c,
    sin_c,
    cos_s,
    sin_s,
    qsend,
    qs,
    vt,
    kt,
    lse,
    osend,
    attp,
    mid,
    gate,
    up,
    own,
    psend,
    prec,
    prec3,
    dsend,
    das,
    dk,
    dv,
    dqs,
    dqp,
    xs,
    xr,
    cs,
    cr,
    ws,
    wr,
    ls,
    go,
    fs,
    fr,
    gs,
    gr,
    os,
):
    section = lax.axis_index("section")
    x = lax.axis_index("fsdp")
    c = lax.axis_index("ctx")
    y, z = lax.rem(c, 4), c // 4
    first, second = section == 0, section == 1
    my_rows = part(128 * x, 128)
    n2, dyf = rows2.at[0], rows2.at[1]
    where = {"x": x, "y": y, "z": z}

    def near(axis, step):
        if axis == "x":
            return {"fsdp": lax.rem(x + step + 4, 4)}
        if axis == "y":
            return {"ctx": 4 * z + lax.rem(y + step + 4, 4)}
        return {"ctx": 4 * lax.rem(z + step + 4, 4) + y}


    barrier = pltpu.get_barrier_semaphore()
    for k in range(1, 4):
        pl.semaphore_signal(
            barrier, inc=1, device_id={"fsdp": lax.rem(x + k, 4)}, device_id_type=MESH
        )
    for k in range(4):
        pl.semaphore_signal(
            barrier,
            inc=1,
            device_id={"section": 1 - section, "fsdp": lax.rem(x + k, 4)},
            device_id_type=MESH,
        )

    def greet(k, carry):
        pl.semaphore_signal(
            barrier, inc=1, device_id={"ctx": lax.rem(c + k, 16)}, device_id_type=MESH
        )
        return carry

    lax.fori_loop(1, 16, greet, 0)
    pl.semaphore_wait(barrier, 22)

    def ahead(k):
        return lax.rem(x + k, 4)

    def behind(k):
        return lax.rem(x - k + 4, 4)

    def over_x(e, k, src, dst):
        return remote(src, dst, xs.at[e, k], xr.at[e, k], {"fsdp": ahead(k)})

    def over_c(e, to, src, dst):
        k = lax.rem(to - c + 16, 16)
        return remote(src, dst, cs.at[e, k], cr.at[e, k], {"ctx": to})

    def piece(e, i, d, src, dst, flip=False):
        device = {"fsdp": lax.rem(x + d + 4, 4)}
        if flip:
            device["section"] = 1 - section
        return remote(src, dst, xs.at[e, i], xr.at[e, i], device)

    def half(ref, b, n):
        return ref.at[part(128 * b + 64 * n, 64)]

    def gather(e, i, src, ref, flip=False):
        if i == 6:
            return piece(e, 6, 0, src, ref.at[my_rows], True)
        if i >= 4:
            place = half(ref, lax.rem(x + (3 if i == 4 else 1), 4), i - 4)
            return piece(e, i, 1 if i == 4 else -1, place, place)
        n = i % 2
        return piece(e, i, 1 if i < 2 else -1, half(src, 0, n), half(ref, x, n), flip)

    def gather_start(e, src, ref, flip=False):
        for i in (0, 3, 1, 2):
            gather(e, i, src, ref, flip).start()

    def gather_pass(e, src, ref):
        for i, n in ((0, 4), (3, 5)):
            gather(e, i, src, ref).wait_recv()
            gather(e, n, src, ref).start()
        for i in (1, 2):
            gather(e, i, src, ref).wait_recv()

    def gather_far(e, src, ref):
        for i in (4, 5):
            gather(e, i, src, ref).wait_recv()

    def gather_sent(e, src, ref, forwarded=True, started=True, flip=False):
        for i in (0, 1, 2, 3) if started else ():
            gather(e, i, src, ref, flip).wait_send()
        for i in (4, 5) if forwarded else ():
            gather(e, i, src, ref).wait_send()

    def total(e, i):
        n = (X_SUM1, X_SUM2, X_SUM3, X_SUM4).index(e) % 2
        to = (2, 2, 1, 3, 1, 3)[i]
        h = (0, 1, 1, 0, 0, 1)[i]
        src = psend.at[n, lax.rem(x + to, 4), pl.ds(64 * h, 64)]
        if i < 2:
            dst = relay_s.at[n, i]
        else:
            dst = prec.at[n, 0 if to == 1 else 1, pl.ds(64 * h, 64)]
        return piece(e, i, (1, -1, 1, -1, 1, -1)[i], src, dst)

    def total_pass(e):
        n = (X_SUM1, X_SUM2, X_SUM3, X_SUM4).index(e) % 2
        for i in (0, 1):
            total(e, i).wait_recv()
            b, rows = lax.rem(x + (1, 3)[i], 4), slice(64 * i, 64 * i + 64)
            psend[n, b, rows] = psend[n, b, rows] + relay_s[n, i]
            total(e, 4 + i).start()

    def total_take(e):
        n = (X_SUM1, X_SUM2, X_SUM3, X_SUM4).index(e) % 2
        for i in (2, 3, 4, 5):
            total(e, i).wait_recv()
        return own[...] + prec[n, 0].astype(F32) + prec[n, 1].astype(F32)

    def total_sent(e):
        for i in range(6):
            total(e, i).wait_send()

    def quarter(n):
        return (z, y)[n % 2]

    def weight(n, i):
        dst = (wqkv, wqkv, wgf, wuf)[n]
        cols = (pl.ds(0, 512), pl.ds(512, 512), pl.ds(0, 1024), pl.ds(0, 1024))[n]
        q = quarter(n)
        if i < 3:
            to = lax.rem(x + i + 1, 4)
            rows = part(96 * q, 96)
            if n < 2:
                src = wsend.at[to, rows, cols]
            else:
                src = (wg, wu)[n - 2].at[rows, part(1024 * to, 1024)]
            place = dst.at[pl.ds(pl.multiple_of(384 * x + 96 * q, 96), 96), cols]
            device = {"fsdp": to}
        else:
            b = lax.rem(x + 1 + i % 3, 4)
            step = (1, -1, 1, -1)[i // 3 - 1]
            if i < 9:
                rows = pl.ds(pl.multiple_of(384 * b + 96 * q, 96), 96)
            else:
                far, h = lax.rem(q - step + 4, 4), i // 3 - 3
                rows = pl.ds(pl.multiple_of(384 * b + 96 * far + 48 * h, 48), 48)
            src = place = dst.at[rows, cols]
            r = lax.rem(q + step + 4, 4)
            device = {"ctx": 4 * r + y if n % 2 == 0 else 4 * z + r}
        return remote(src, place, ws.at[n, i], wr.at[n, i], device)

    def fetch_to(n, b):
        i, q = lax.rem(b - x + 3, 4), quarter(n)
        cols = pl.ds(512 * n, 512)
        rows = pl.ds(pl.multiple_of(384 * x + 96 * q, 96), 96)
        src = wsend.at[b, part(96 * q, 96), cols]
        return remote(src, wqkv.at[rows, cols], ws.at[n, i], wr.at[n, i], {"fsdp": b})

    def weight_each(which, items, act):
        for i in items:
            for n in which:
                act(weight(n, i))

    def begin(copy):
        copy.start()

    def arrive(copy):
        copy.wait_recv()

    def leave(copy):
        copy.wait_send()

    def weight_fetch(which):
        weight_each(which, (1, 0, 2), begin)

    def weight_share(which):
        weight_each(which, range(3), arrive)
        weight_each(which, range(3, 9), begin)

    def weight_pass(which):
        for k in range(3):
            weight_each(which, (3 + k,), arrive)
            weight_each(which, (9 + k,), begin)
        for k in range(3):
            weight_each(which, (6 + k,), arrive)
            weight_each(which, (12 + k,), begin)

    def weight_wait(which):
        weight_each(which, range(9, 15), arrive)

    heads, wide = (0, 1), (2, 3)

    def gain_copy(k):
        return over_x(X_GAIN, k, gains, gain.at[:, part(384 * x, 384)])

    def pos_copy(k):
        return over_x(X_POS, k, pos, posx.at[x])

    pos[...] = jnp.broadcast_to(
        jnp.concatenate([positions[0:1, :], positions[1:2, :]], axis=1).astype(F32), (8, 128)
    )
    gains[...] = jnp.broadcast_to(norm_attn[...].astype(F32), (8, 384))
    gains[1:2, :] = norm_mlp[...].astype(F32)
    for k in (2, 1, 3):
        pos_copy(k).start()
        gain_copy(k).start()
    gain[:, part(384 * x, 384)] = gains[...]
    posx[x] = pos[...]

    def local_copies():
        yield pltpu.make_async_copy(
            wg.at[:, part(1024 * x, 1024)], wgf.at[part(384 * x, 384)], ls.at[0]
        )
        yield pltpu.make_async_copy(
            wu.at[:, part(1024 * x, 1024)], wuf.at[part(384 * x, 384)], ls.at[1]
        )
        yield pltpu.make_async_copy(wd_in, wd, ls.at[2])
        for h in range(4):
            yield pltpu.make_async_copy(
                wo_in.at[pl.ds(96 * h, 96)], wop.at[pl.ds(128 * h, 96)], ls.at[3 + h]
            )

    def head_columns(b, j, rows):
        w_q = wq[rows, 384 * b + 192 * j : 384 * b + 192 * j + 192]
        w_k = wk[rows, 96 * (2 * b + j) : 96 * (2 * b + j) + 96]
        w_v = wv[rows, 96 * (2 * b + j) : 96 * (2 * b + j) + 96]
        blank = jnp.zeros((w_v.shape[0], 32), BF)
        return jnp.concatenate(spread(w_q, (0, 1)) + spread(w_k, (0,)) + [w_v, blank], axis=1)

    for b in range(4):

        @pl.when(b != x)
        def _(b=b):
            for j in heads:
                rows = part(96 * quarter(j), 96)
                wsend[b, rows, 512 * j : 512 * j + 512] = head_columns(b, j, rows)

                @pl.when(first)
                def _(j=j):
                    fetch_to(j, b).start()

    @pl.when(first)
    def _():
        gather_start(X_IN, xin, xall)
        xall[my_rows, :] = xin[...]

    for b in range(4):

        @pl.when(b == x)
        def _(b=b):
            for j in heads:
                wqkv[384 * b : 384 * b + 384, 512 * j : 512 * j + 512] = head_columns(
                    b, j, slice(0, 384)
                )

    for copy in local_copies():
        copy.start()
    for h in range(4):
        wop[128 * h + 96 : 128 * h + 128, :] = jnp.zeros((32, WIDTH), BF)

    lane = lax.broadcasted_iota(jnp.int32, (1, 128), 1)
    sign = jnp.where(lane < 64, -1.0, 1.0)
    index = jnp.where(lane < 64, lane, lane - 64)
    freq = jnp.where(index < 48, jnp.exp2(index.astype(F32) * STEP2), 0.0)
    for k in (1, 3, 2):
        pos_copy(k).wait()
    for b in range(4):
        block = posx[b]
        posv[b, 0] = block
        posv[b, 1] = pltpu.roll(block, 64, 1)

    def pos_to(to):
        return over_c(C_POS, to, posv.at[to // 4, lax.rem(to, 4) // 2], posc.at[c])

    def send_pos(k, carry):
        pos_to(lax.rem(c + k, 16)).start()
        return carry

    lax.fori_loop(1, 16, send_pos, 0)
    posc[c] = posv[c // 4, lax.rem(c, 4) // 2]

    @pl.when(first)
    def _():
        weight_share(heads)

    for b in range(4):
        angle = as_column(posx[b][0:1, :]) * freq
        cos_c[128 * b : 128 * b + 128, :] = jnp.cos(angle)
        sin_c[128 * b : 128 * b + 128, :] = jnp.sin(angle) * sign

    def tables():
        def await_pos(k, carry):
            pos_to(lax.rem(c + k, 16)).wait()
            return carry

        def table(i, carry):
            row = jnp.where(
                lane < 64, posc[2 * i][0:1, :], pltpu.roll(posc[2 * i + 1], 64, 1)[0:1, :]
            )
            block = part(128 * i, 128)
            posr[0:1, block] = row
            column = as_column(row)
            posk[block, :] = jnp.broadcast_to(column, (128, 128))
            angle = column * freq
            cos_s[block, :] = jnp.cos(angle)
            sin_s[block, :] = jnp.sin(angle) * sign
            return carry

        lax.fori_loop(1, 16, await_pos, 0)
        lax.fori_loop(0, 8, table, 0)

    for k in (1, 3, 2):
        gain_copy(k).wait()

    @pl.when(first)
    def _():
        weight_pass(heads)
        gather_pass(X_IN, xin, xall)
        weight_fetch(wide)
        weight_wait(heads)

    @pl.when(second)
    def _():
        tables()
        gather_start(X_DY, dyin, dyf)
        dyf[my_rows, :] = dyin[...]
        gather_pass(X_DY, dyin, dyf)
        pl.semaphore_wait(go, 1)
        weight_fetch(heads + wide)
        weight_share(heads + wide)
        weight_pass(heads + wide)
        weight_wait(heads + wide)

    gain_attn, gain_mlp = gain[0:1, :], gain[1:2, :]

    def to_pair(ref, e, b, i, width, dst):
        src = ref.at[part(128 * b + 64 * (i // 2), 64), pl.ds(width * (i % 2), width)]
        return over_c(e, 4 * b + i, src, dst.at[part(64 * c, 64)])

    def in_order(n):
        return behind(jnp.where(n == 2, 3, jnp.where(n == 3, 2, n)))

    def project(n, carry):
        b = in_order(n)
        rows = part(128 * b, 128)

        @pl.when(jnp.logical_and(second, n == 0))
        def _():
            gather(X_IN, 6, out, xall).wait_recv()

        @pl.when(jnp.logical_and(second, n == 1))
        def _():
            gather_pass(X_IN, xin, xall)

        @pl.when(n == 3)
        def _():
            gather_far(X_IN, xin, xall)

        value = xall[rows, :].astype(F32)
        normed = (
            value
            * lax.rsqrt(jnp.mean(value * value, axis=-1, keepdims=True) + EPSILON)
            * gain_attn
        ).astype(BF)
        nf[rows, :] = normed
        u = mm(normed, wqkv[...])
        cosine, sine = cos_c[rows, :], sin_c[rows, :]
        for h in range(8):
            head = u[:, 128 * h : 128 * h + 128]
            if h % 4 != 3:
                head = turn(head, cosine, sine)
            qsend[rows, 128 * h : 128 * h + 128] = head.astype(BF)
        for i in range(4):

            @pl.when(4 * b + i != c)
            def _(i=i):
                to_pair(qsend, C_QKV, b, i, 512, qs).start()

            @pl.when(4 * b + i == c)
            def _(i=i):
                qs[part(64 * c, 64), :] = qsend[
                    part(128 * b + 64 * (i // 2), 64), 512 * (i % 2) : 512 * (i % 2) + 512
                ]

        return carry

    lax.fori_loop(0, 4, project, 0)

    @pl.when(first)
    def _():
        tables()

    weight_each(heads, range(3), leave)


    def await_qkv(k, carry):
        place = qs.at[part(64 * lax.rem(c - k + 16, 16), 64)]
        over_c(C_QKV, lax.rem(c + k, 16), place, place).wait_recv()
        return carry

    lax.fori_loop(1, 16, await_qkv, 0)

    @pl.when(first)
    def _():
        weight_share(wide)
        pl.semaphore_signal(go, inc=1, device_id={"section": 1}, device_id_type=MESH)

    vt[...] = qs[:, 384:512].T
    kt[...] = qs[:, 256:384].T

    def masked(q, cols):
        st = mm_nt(qs[:, 256:384], q)
        return jnp.where(posk[:, 0:1] <= posr[0:1, cols], st, -1e30)

    def att_place():
        return attp.at[part(64 * (c // 2), 64), part(256 * lax.rem(c, 2), 256)]

    def att_to(to):
        return over_c(C_ATT, to, osend.at[part(64 * to, 64)], att_place())

    def attend(n, carry):
        rows = part(256 * n, 256)

        for g in range(2):
            st = masked(qs[rows, 128 * g : 128 * g + 128], rows)
            top = jnp.max(st, axis=0, keepdims=True)
            e = jnp.exp2((st - top) * SCALE2)
            sums = jnp.sum(e, axis=0, keepdims=True)
            lse[g : g + 1, rows] = top * SCALE2 + jnp.log2(sums)
            result = mm(vt[...], e.astype(BF)) * (1.0 / sums)
            osend[rows, 128 * g : 128 * g + 128] = result.T.astype(BF)
        for i in range(4):
            to = 4 * n + i

            @pl.when(to != c)
            def _(to=to):
                att_to(to).start()

            @pl.when(to == c)
            def _(to=to):
                attp[part(64 * (c // 2), 64), part(256 * lax.rem(c, 2), 256)] = osend[
                    part(64 * to, 64), :
                ]

        return carry

    lax.fori_loop(0, 4, attend, 0)

    @pl.when(first)
    def _():
        weight_pass(wide)


    def await_att(b):
        for i in range(4):
            to = 4 * b + i

            @pl.when(to != c)
            def _(to=to, i=i):
                k = lax.rem(c - to + 16, 16)
                place = attp.at[part(64 * (2 * b + i // 2), 64), pl.ds(256 * (i % 2), 256)]
                remote(place, place, cs.at[C_ATT, k], cr.at[C_ATT, k], {"ctx": lax.rem(c + k, 16)}).wait_recv()

    def give(e, n, b, value):
        place = psend.at[(X_SUM1, X_SUM2, X_SUM3, X_SUM4).index(e) % 2, b]

        @pl.when(n < 3)
        def _():
            place[...] = value.astype(BF)

        @pl.when(n == 0)
        def _():
            total(e, 0).start()
            total(e, 1).start()

        @pl.when(n == 1)
        def _():
            total(e, 2).start()

        @pl.when(n == 2)
        def _():
            total(e, 3).start()
            total_pass(e)

        @pl.when(n == 3)
        def _():
            own[...] = value

    def far_first(n):
        return lax.rem(x + jnp.where(n == 0, 2, jnp.where(n == 1, 1, jnp.where(n == 2, 3, 0))), 4)

    def combine(n, carry):
        b = far_first(n)
        await_att(b)
        give(X_SUM1, n, b, mm(attp[part(128 * b, 128), :], wop[...]))
        return carry

    for copy in local_copies():
        copy.wait()
    lax.fori_loop(0, 4, combine, 0)
    middle = xall[my_rows, :].astype(F32) + total_take(X_SUM1)
    mid[...] = middle
    n2[my_rows, :] = (
        middle * lax.rsqrt(jnp.mean(middle * middle, axis=-1, keepdims=True) + EPSILON) * gain_mlp
    ).astype(BF)
    n2_own = n2.at[my_rows]
    gather_start(X_N2, n2_own, n2)

    @pl.when(first)
    def _():
        weight_wait(wide)

    def pair(blocks, ref):
        return jnp.concatenate([ref[part(128 * b, 128), :] for b in blocks], axis=0)

    def far_copy(d, b):
        return piece(X_SUM2, d, d, psend.at[1, b], prec3.at[d - 1])

    def feed(ds):
        blocks = [lax.rem(x + d, 4) for d in ds]
        a = pair(blocks, n2)
        ga, u = mm(a, wgf[...]), mm(a, wuf[...])
        h = (ga * (1.0 / (1.0 + jnp.exp(-ga))) * u).astype(BF)
        result = mm(h, wd[...])
        for n, (d, b) in enumerate(zip(ds, blocks)):
            rows, cut = part(128 * b, 128), slice(128 * n, 128 * n + 128)
            gate[rows, :] = ga[cut].astype(BF)
            up[rows, :] = u[cut].astype(BF)
            hidden[rows, :] = h[cut]
            if d == 0:
                own[...] = result[cut]
            else:
                psend[1, b] = result[cut].astype(BF)
                far_copy(d, b).start()

    gather_pass(X_N2, n2_own, n2)
    feed((1, 3))
    gather_far(X_N2, n2_own, n2)
    feed((2, 0))
    result = mid[...] + own[...]
    for d in (1, 3, 2):
        far_copy(d, lax.rem(x + d, 4)).wait_recv()
        result = result + prec3[d - 1].astype(F32)
    out[...] = result.astype(BF)

    @pl.when(first)
    def _():
        gather_sent(X_IN, xin, xall, forwarded=False)
        gather(X_IN, 6, out, xall).start()
        gather_start(X_IN, out, xall, True)

    held = dict(zip(ARRAYS, (h_gate, h_up, h_down, h_out, h_heads_a, h_heads_b)))

    def ring(name):
        axis, d = FLOWS[name][:2]
        other = "z" if axis == "y" else "y"
        group = where[axis] if name in STAY else lax.rem(x + where[axis], 4)
        return NAMES.index(name), axis, other, d, group, where[other]

    def hand(name):
        axis, d = FLOWS[name][:2]
        if name in STAY:
            return where[axis], d
        return lax.rem(x - where[axis] + 4, 4), -d

    def at(i, d, s):
        return lax.rem(i - d * s + 8, 4)

    def columns(name):
        return pl.ds(FLOWS[name][3], FLOWS[name][5])

    def place_of(name, g, p):
        return held[FLOWS[name][2]].at[g, p, :, columns(name)]

    def partial(name, g, p):
        array, cols = FLOWS[name][2], columns(name)
        if array == "down":
            return wd.at[part(256 * g + 64 * p, 64), cols]
        if array == "out":
            return wop.at[part(96 * g, 96), part(384 * p, 384)]
        rows = pl.ds(pl.multiple_of(384 * g + 96 * p, 96), 96)
        if name in LATE:
            return wqkv.at[rows, pl.ds(384 * LATE.index(name), 384)]
        return (wgf if array == "gate" else wuf).at[rows, cols]

    def arrival(name, s, q):
        n = 4 * (s - 1) + q
        array, cols = FLOWS[name][2], columns(name)
        if array == "gate":
            return wsend.at[s, part(96 * q, 96), cols]
        if array == "up":
            slot = wsend.at[3, part(96 * q, 96), cols]
            return slot if s == 0 else dgu.at[part(96 * n, 96), cols]
        if array == "down":
            return arrive_down.at[q, :, cols] if s == 0 else n2.at[part(64 * n, 64), cols]
        return arrive_out.at[s, q]

    def arrival2(name, s):
        array, cols = FLOWS[name][2], columns(name)
        if array in ("gate", "up"):
            return (gate if array == "gate" else up).at[part(96 * s, 96), cols]
        if array == "down":
            return prec3.at[s, pl.ds(0, 64), cols]
        return {"out": second_out, "heads_a": second_a, "heads_b": second_b}[array].at[s]

    def flow(name, n, src, dst, device):
        f = NAMES.index(name)
        return remote(src, dst, fs.at[f, n], fr.at[f, n], device)

    def copy_first(name, s, q):
        f, axis, other, d, i, j = ring(name)
        src = partial(name, at(i, d, 1 + s), at(j, d, 1 + q))
        return flow(name, 4 * s + q, src, arrival(name, s, q), near(axis, d))

    def copy_second(name, s):
        f, axis, other, d, i, j = ring(name)
        src = partial(name, i, at(j, d, 1 + s))
        return flow(name, 12 + s, src, arrival2(name, s), near(other, d))

    def copy_mirror(name):
        f, axis, other, d, i, j = ring(name)
        n = 6 if name in LATE else 15
        device = {"fsdp": lax.rem(x + where[axis], 4)}
        return flow(name, n, partial(name, i, j), place_of(name, x, j), device)

    def copy_own(name):
        f, axis, other, d, i, j = ring(name)
        group = i if name in STAY else x
        return pltpu.make_async_copy(partial(name, i, j), place_of(name, group, j), os.at[f])

    def copy_small(name, s):
        f, axis, other, d, i, j = ring(name)
        place = place_of(name, hand(name)[0], at(j, d, s))
        return flow(name, 16 + s, place, place, near(other, d))

    def copy_big(name, s, q):
        f, axis, other, d, i, j = ring(name)
        place = place_of(name, at(*hand(name), s), at(j, d, q))
        return flow(name, 20 + 4 * s + q, place, place, near(axis, d))

    def first_start(names):
        def body(q, carry):
            for name in names:
                copy_first(name, 0, q).start()
            return carry

        lax.fori_loop(0, 4, body, 0)

    def first_step(names, s):
        def body(q, carry):
            for name in names:
                f, axis, other, d, i, j = ring(name)
                copy_first(name, s, q).wait_recv()
                place = partial(name, at(i, d, 2 + s), at(j, d, 1 + q))
                place[...] = place[...] + arrival(name, s, q)[...]
                if s < 2:
                    copy_first(name, s + 1, q).start()
                else:

                    @pl.when(q == 0)
                    def _(name=name):
                        copy_second(name, 0).start()

            return carry

        lax.fori_loop(0, 4, body, 0)

    def second_step(names, s):
        for name in names:
            f, axis, other, d, i, j = ring(name)
            copy_second(name, s).wait_recv()
            place = partial(name, i, at(j, d, 2 + s))
            place[...] = place[...] + arrival2(name, s)[...]
            if s < 2:
                copy_second(name, s + 1).start()

    def mirror_step(names, act):
        for name in names:
            if name in STAY:
                act(copy_own(name))
                continue
            axis = FLOWS[name][0]

            @pl.when(where[axis] != 0)
            def _(name=name):
                act(copy_mirror(name))

            @pl.when(where[axis] == 0)
            def _(name=name):
                act(copy_own(name))

    def finish_copy(copy):
        copy.wait()

    def small_step(names, q):
        for name in names:
            if q > 0:
                copy_small(name, q - 1).wait_recv()
            if q < 3:
                copy_small(name, q).start()
        for name in names:
            copy_big(name, 0, q).start()

    def big_step(names, s, low, high):
        def body(q, carry):
            for name in names:
                copy_big(name, s, q).wait_recv()
                if s < 2:
                    copy_big(name, s + 1, q).start()
            return carry

        lax.fori_loop(low, high, body, 0)

    def gain_sum_copy(n, k):
        axis = "xyz"[n]
        if n == 0:
            src = ggain.at[:, part(lax.rem(x + k, 4) * 384, 384)]
        else:
            src = gain_in.at[n, 0]
        return remote(src, gain_in.at[n, k], gs.at[n, k], gr.at[n, k], near(axis, k))

    def gain_start(n):
        for k in (1, 2, 3):
            gain_sum_copy(n, k).start()

    def gain_sum(n):
        mine = ggain[:, part(x * 384, 384)] if n == 0 else gain_in[n, 0]
        for k in (1, 2, 3):
            gain_sum_copy(n, k).wait()
        return mine + gain_in[n, 1] + gain_in[n, 2] + gain_in[n, 3]

    def late(name, n):
        f, axis, other, d, i, j = ring(name)
        cols = pl.ds(384 * LATE.index(name), 384)
        k = (n if n < 6 else n - 1) % 3 + 1
        if n < 3:
            src = wqkv.at[part(384 * lax.rem(i + k, 4), 384), cols]
            return flow(name, n, src, (arrive_a, arrive_b)[LATE.index(name)].at[k - 1], near(axis, k))
        if n < 6:
            src = partial(name, i, lax.rem(j + k, 4))
            return flow(name, n, src, arrival2(name, k - 1), near(other, k))
        if n < 10:
            place = held[name].at[hand(name)[0], j]
            return flow(name, n, place, place, near(other, k))
        place = held[name].at[hand(name)[0]]
        return flow(name, n, place, place, near(axis, k))

    def late_each(items, act):
        for n in items:
            for name in LATE:
                act(late(name, n))

    def late_first():
        late_each(range(3), arrive)
        for name in LATE:
            f, axis, other, d, i, j = ring(name)
            rows, cols = part(384 * i, 384), pl.ds(384 * LATE.index(name), 384)
            got = (arrive_a, arrive_b)[LATE.index(name)]
            sums = wqkv[rows, cols].astype(F32)
            for k in range(3):
                sums = sums + got[k].astype(F32)
            wqkv[rows, cols] = sums.astype(BF)
        late_each(range(3, 6), begin)

    def late_second():
        late_each(range(3, 6), arrive)
        for name in LATE:
            f, axis, other, d, i, j = ring(name)
            place = partial(name, i, j)
            sums = place[...].astype(F32)
            for k in range(3):
                sums = sums + arrival2(name, k)[...].astype(F32)
            place[...] = sums.astype(BF)
        mirror_step(LATE, begin)

    def late_small():
        mirror_step(LATE, finish_copy)
        late_each(range(7, 10), begin)

    def late_big():
        late_each(range(7, 10), arrive)
        late_each(range(10, 13), begin)

    def feed_grads(s, carry):
        rows = part(384 * at(ring("gate")[4], 1, 1 + s), 384)
        wgf[rows, :] = mm_tn(n2[:, rows], dgu[0:512, :]).astype(BF)
        rows = part(384 * at(ring("up")[4], -1, 1 + s), 384)
        wuf[rows, :] = mm_tn(n2[:, rows], dgu[512:1024, :]).astype(BF)
        rows = part(256 * at(z, 1, 1 + s), 256)
        wd[rows, :] = mm_tn(hidden[:, rows], dyf[...]).astype(BF)

        return carry

    @pl.when(first)
    def _():
        gather_pass(X_DY, dx, dyf)
        gather(X_DY, 6, dx, dyf).wait_recv()

    gather_far(X_DY, dx, dyf)

    def feed_back(ds):
        blocks = [lax.rem(x + d, 4) for d in ds]
        dh = mm_nt(pair(blocks, dyf), wd[...])
        ga, u = pair(blocks, gate).astype(F32), pair(blocks, up).astype(F32)
        s = 1.0 / (1.0 + jnp.exp(-ga))
        dga = (dh * u * (s * (1.0 + ga * (1.0 - s)))).astype(BF)
        du = (dh * (ga * s)).astype(BF)
        result = mm_nt(dga, wgf[...]) + mm_nt(du, wuf[...])
        for n, (d, b) in enumerate(zip(ds, blocks)):
            rows, cut = part(128 * b, 128), slice(128 * n, 128 * n + 128)
            dgu[rows, :] = dga[cut]
            dgu[part(512 + 128 * b, 128), :] = du[cut]
            if d == 0:
                own[...] = result[cut]
            else:
                psend[0, b] = result[cut].astype(BF)
                for i in {2: (0, 1), 1: (2,), 3: (3,)}[d]:
                    total(X_SUM3, i).start()

    total_sent(X_SUM1)
    feed_back((2, 1))
    feed_back((3, 0))
    weight_each(heads, range(3, 15), leave)
    weight_each(wide, range(15), leave)
    gather_sent(X_N2, n2_own, n2)
    gather_sent(X_DY, dyin, dyf, started=False)
    for d in (1, 2, 3):
        far_copy(d, lax.rem(x + d, 4)).wait_send()
    lax.fori_loop(0, 1, feed_grads, 0)
    first_start(("gate", "up", "down"))
    total_pass(X_SUM3)
    lax.fori_loop(1, 4, feed_grads, 0)
    first_start(("gate_rest", "up_rest", "down_rest"))
    def norm_back(value, grad, gain_row):
        r = lax.rsqrt(jnp.mean(value * value, axis=-1, keepdims=True) + EPSILON)
        unit = value * r
        t = grad * gain_row
        back = r * (t - unit * jnp.mean(t * unit, axis=-1, keepdims=True))
        return back, jnp.sum(grad * unit, axis=0, keepdims=True)

    back, g_mlp = norm_back(mid[...], total_take(X_SUM3), gain_mlp)
    dmid = dyf[my_rows, :].astype(F32) + back
    mid[...] = dmid
    ggain[...] = jnp.zeros_like(ggain)
    ggain[1:2, :] = g_mlp
    dbr[my_rows, :] = dmid.astype(BF)
    dbr_own = dbr.at[my_rows]
    gather_start(X_DBR, dbr_own, dbr)

    def branch(n, carry):
        b = in_order(n)
        rows = part(128 * b, 128)

        @pl.when(n == 1)
        def _():
            gather_pass(X_DBR, dbr_own, dbr)

        @pl.when(n == 3)
        def _():
            gather_far(X_DBR, dbr_own, dbr)

        dsend[rows, :] = mm_nt(dbr[rows, :], wop[...]).astype(BF)
        for i in range(4):

            @pl.when(4 * b + i != c)
            def _(i=i):
                to_pair(dsend, C_DATT, b, i, 256, das).start()

            @pl.when(4 * b + i == c)
            def _(i=i):
                das[part(64 * c, 64), :] = dsend[
                    part(128 * b + 64 * (i // 2), 64), 256 * (i % 2) : 256 * (i % 2) + 256
                ]

        return carry

    lax.fori_loop(0, 4, branch, 0)
    for n in range(2):
        rows = slice(256 * n, 256 * n + 256)
        att[rows, :] = jnp.concatenate(
            [attp[rows, 128 * h : 128 * h + 96] for h in range(4)], axis=1
        )
    wop[0:384, :] = mm_tn(att[...], dbr[...]).astype(BF)
    first_start(("out",))

    def await_das(k, carry):
        place = das.at[part(64 * lax.rem(c - k + 16, 16), 64)]
        over_c(C_DATT, lax.rem(c + k, 16), place, place).wait_recv()
        return carry

    lax.fori_loop(1, 16, await_das, 0)
    first_step(MAIN, 0)
    dk[...] = jnp.zeros_like(dk)
    dv[...] = jnp.zeros_like(dv)

    def grad_place(h):
        return dqp.at[part(64 * (c // 2), 64), part(512 * lax.rem(c, 2) + 256 * h, 256)]

    def grad_to(e, to):
        h = e - C_DQ
        return over_c(e, to, dqs.at[part(64 * to, 64), pl.ds(256 * h, 256)], grad_place(h))

    def attend_back(n, carry):
        rows = part(256 * n, 256)
        for g in range(2):
            cols = slice(128 * g, 128 * g + 128)
            q, da = qs[rows, cols], das[rows, cols]
            p = jnp.exp2(masked(q, rows) * SCALE2 - lse[g : g + 1, rows])
            dp = mm_nt(qs[:, 384:512], da)
            dv[...] += mm(p.astype(BF), da)
            ds = (p * (dp - jnp.sum(p * dp, axis=0, keepdims=True))).astype(BF)
            dk[...] += mm(ds, q)
            dq = mm(kt[...], ds).T * SCALE
            dqs[rows, cols] = turn(dq, cos_s[rows, :], -sin_s[rows, :]).astype(BF)
        for i in range(4):
            to = 4 * n + i

            @pl.when(to != c)
            def _(to=to):
                grad_to(C_DQ, to).start()

            @pl.when(to == c)
            def _(to=to):
                grad_place(0)[...] = dqs[part(64 * to, 64), 0:256]

        return carry

    lax.fori_loop(0, 4, attend_back, 0)
    dqs[:, 256:384] = turn(dk[...] * SCALE, cos_s[...], -sin_s[...]).astype(BF)
    dqs[:, 384:512] = dv[...].astype(BF)

    def send_dkv(k, carry):
        grad_to(C_DKV, lax.rem(c + k, 16)).start()
        return carry

    lax.fori_loop(1, 16, send_dkv, 0)
    grad_place(1)[...] = dqs[part(64 * c, 64), 256:512]
    first_step(MAIN, 1)
    first_step(("out",), 0)

    def await_dqkv(b):
        for i in range(4):
            to = 4 * b + i

            @pl.when(to != c)
            def _(to=to, i=i):
                k = lax.rem(c - to + 16, 16)
                for h in range(2):
                    place = dqp.at[
                        part(64 * (2 * b + i // 2), 64), pl.ds(512 * (i % 2) + 256 * h, 256)
                    ]
                    e = C_DQ + h
                    remote(
                        place, place, cs.at[e, k], cr.at[e, k], {"ctx": lax.rem(c + k, 16)}
                    ).wait_recv()

    def input_grad(n, carry):
        b = far_first(n)
        await_dqkv(b)
        give(X_SUM4, n, b, mm_nt(dqp[part(128 * b, 128), :], wqkv[...]))
        return carry

    lax.fori_loop(0, 4, input_grad, 0)
    @pl.when(first)
    def _():
        first_step(MAIN, 2)

    first_step(("out",), 1)
    for n in range(2):
        rows = slice(256 * n, 256 * n + 256)
        pieces = []
        for h in range(8):
            if h % 4 == 3:
                pieces.append(dqp[rows, 128 * h : 128 * h + 96])
            else:
                pieces.append(dqp[rows, 128 * h : 128 * h + 48])
                pieces.append(dqp[rows, 128 * h + 64 : 128 * h + 112])
        dqkv[rows, :] = jnp.concatenate(pieces, axis=1)

    def head_grads(g, carry):
        rows = part(384 * g, 384)
        wqkv[rows, 0:768] = mm_tn(nf[:, rows], dqkv[...]).astype(BF)
        return carry

    lax.fori_loop(0, 4, head_grads, 0)
    late_each(range(3), begin)
    back, g_attn = norm_back(xall[my_rows, :].astype(F32), total_take(X_SUM4), gain_attn)
    dx[...] = (mid[...] + back).astype(BF)
    ggain[0:1, :] = g_attn

    @pl.when(second)
    def _():
        gather_sent(X_DY, dyin, dyf, forwarded=False)
        gather(X_DY, 6, dx, dyf).start()
        gather_start(X_DY, dx, dyf, True)

    gain_start(0)

    @pl.when(second)
    def _():
        first_step(MAIN, 2)

    first_step(("out",), 2)
    second_step(EARLY, 0)
    gain_in[1, 0] = gain_sum(0)
    gain_start(1)
    second_step(EARLY, 1)
    second_step(EARLY, 2)
    mirror_step(EARLY, begin)
    gain_in[2, 0] = gain_sum(1)
    gain_start(2)
    late_first()
    late_second()
    mirror_step(EARLY, finish_copy)
    small_step(EARLY, 0)
    late_small()
    small_step(EARLY, 1)
    late_big()
    small_step(EARLY, 2)
    small_step(EARLY, 3)
    for n in range(3):
        big_step(EARLY, n, 0, 4)
    late_each(range(10, 13), arrive)
    o_gain[...] = gain_sum(2)

    def sent_c(k, carry):
        to = lax.rem(c + k, 16)
        place = qs.at[part(64 * to, 64)]
        over_c(C_QKV, to, place, place).wait_send()
        att_to(to).wait_send()
        place = das.at[part(64 * to, 64)]
        over_c(C_DATT, to, place, place).wait_send()
        grad_to(C_DQ, to).wait_send()
        grad_to(C_DKV, to).wait_send()
        return carry

    lax.fori_loop(1, 16, sent_c, 0)
    total_sent(X_SUM3)
    total_sent(X_SUM4)
    gather_sent(X_DBR, dbr_own, dbr)
    gather_sent(X_IN, xin, xall, started=False)

    def sent_first(q, carry):
        for name in EARLY:
            for n in range(3):
                copy_first(name, n, q).wait_send()
                copy_big(name, n, q).wait_send()
        return carry

    lax.fori_loop(0, 4, sent_first, 0)
    late_each((0, 1, 2, 3, 4, 5, 7, 8, 9, 10, 11, 12), leave)
    for name in EARLY:
        for n in range(3):
            copy_second(name, n).wait_send()
            copy_small(name, n).wait_send()

    @pl.when(first)
    def _():
        gather_sent(X_IN, xin, xall, forwarded=False)
        gather(X_IN, 6, out, xall).wait_send()

    @pl.when(second)
    def _():
        gather_sent(X_DY, dyin, dyf, forwarded=False)
        gather(X_DY, 6, dx, dyf).wait_send()


def run_layer(xin, dyin, positions, norm_attn, norm_mlp, wq, wk, wv, wo, wd, wg, wu, cid):
    vm = pl.BlockSpec(memory_space=pltpu.VMEM)
    hbm = pl.BlockSpec(memory_space=pl.ANY)
    dma = pltpu.SemaphoreType.DMA
    shapes = [
        ((128, WIDTH), BF),
        ((128, WIDTH), BF),
        *(((4, 4) + shape, BF) for shape in ARRAYS.values()),
        ((8, 384), F32),
    ]
    scratch = [
        ((512, WIDTH), BF),
        ((2, 512, WIDTH), BF),
        ((1024, 1024), BF),
        ((512, 768), BF),
        ((512, 384), BF),
        ((512, WIDTH), BF),
        ((512, 1024), BF),
        ((8, WIDTH), F32),
        ((4, 64, WIDTH), BF),
        ((3, 4, 96, 384), BF),
        *(((3, 384, 384), BF),) * 2,
        *(((3, 96, 384), BF),) * 3,
        ((3, 4, 8, 384), F32),
        ((4, 384, 1024), BF),
        ((WIDTH, 1024), BF),
        ((WIDTH, 1024), BF),
        ((WIDTH, 1024), BF),
        ((512, WIDTH), BF),
        ((1024, WIDTH), BF),
        ((2, 2, 64, WIDTH), BF),
        ((512, WIDTH), BF),
        ((8, 384), F32),
        ((8, 128), F32),
        ((8, WIDTH), F32),
        ((4, 8, 128), F32),
        ((4, 2, 8, 128), F32),
        ((16, 8, 128), F32),
        ((8, 1024), F32),
        ((1024, 128), F32),
        ((512, 128), F32),
        ((512, 128), F32),
        ((1024, 128), F32),
        ((1024, 128), F32),
        ((512, 1024), BF),
        ((1024, 512), BF),
        ((128, 1024), BF),
        ((128, 1024), BF),
        ((8, 1024), F32),
        ((1024, 256), BF),
        ((512, 512), BF),
        ((128, WIDTH), F32),
        ((512, 1024), BF),
        ((512, 1024), BF),
        ((128, WIDTH), F32),
        ((2, 4, 128, WIDTH), BF),
        ((2, 2, 128, WIDTH), BF),
        ((3, 128, WIDTH), BF),
        ((512, 512), BF),
        ((1024, 256), BF),
        ((1024, 128), F32),
        ((1024, 128), F32),
        ((1024, 512), BF),
        ((512, 1024), BF),
    ]
    return pl.pallas_call(
        layer_kernel,
        out_shape=[jax.ShapeDtypeStruct(s, d) for s, d in shapes],
        in_specs=[vm] * 8 + [hbm] * 4,
        out_specs=[vm] * 2 + [hbm] * len(ARRAYS) + [vm],
        scratch_shapes=[pltpu.VMEM(s, d) for s, d in scratch]
        + [dma((13, 7)), dma((13, 7)), dma((6, 16)), dma((6, 16)), dma((4, 15)), dma((4, 15)), dma((7,)), pltpu.SemaphoreType.REGULAR]
        + [dma((9, 32)), dma((9, 32)), dma((3, 4)), dma((3, 4)), dma((9,))],
        name="layer",
        compiler_params=pltpu.CompilerParams(
            collective_id=cid, has_side_effects=True, vmem_limit_bytes=63 << 20
        ),
    )(xin, dyin, positions, norm_attn, norm_mlp, wq, wk, wv, wo, wd, wg, wu)


def local(
    inputs,
    positions,
    out_grad,
    norm_attn,
    w_query,
    key_weight,
    value_weight,
    output_weight,
    norm_mlp,
    w_gate,
    w_up,
    w_down,
):
    out, dx, *summed, g_gain = run_layer(
        inputs.reshape(128, WIDTH),
        out_grad.reshape(128, WIDTH),
        positions,
        norm_attn,
        norm_mlp,
        w_query[0],
        key_weight[0],
        value_weight[0],
        output_weight[0],
        w_down[0],
        w_gate[0],
        w_up[0],
        0,
    )
    g_gate, g_up, g_query, g_key, g_value, g_out, g_down, g_attn, g_mlp = widen(*summed, g_gain)
    return (
        out.reshape(1, 2, 64, WIDTH),
        dx.reshape(1, 2, 64, WIDTH),
        g_attn,
        g_query[None],
        g_key[None],
        g_value[None],
        g_out[None],
        g_mlp,
        g_gate[None],
        g_up[None],
        g_down[None],
    )


def solution(mesh):
    rows = P("section", "fsdp", None)
    return jax.shard_map(
        local,
        mesh=mesh,
        in_specs=(
            P("fsdp", "ctx", None),
            P("fsdp", "ctx"),
            P("fsdp", "ctx", None),
            P("section", "fsdp"),
            rows,
            rows,
            rows,
            rows,
            P("section", "fsdp"),
            rows,
            rows,
            rows,
        ),
        out_specs=(
            P("section", "fsdp", "ctx", None),
            P("section", "fsdp", "ctx", None),
            P("section", "fsdp"),
            rows,
            rows,
            rows,
            rows,
            P("section", "fsdp"),
            rows,
            rows,
            rows,
        ),
        check_vma=False,
    )
```
